32 devices in a mesh: batch: 8 (over z, x), module: 4 (over y, core).
Axes of the slice: x: 2, y: 2, z: 4, core: 2. Of those that a mesh axis runs over, the one named last changes fastest.
Arguments:
- tokens: bfloat16 [16384, 256], P(('batch', 'module')), may hold values from -6 to 6
- seg_lengths: int32 [8, 8], P('batch'), may hold values from 1 to 1024, 2048 in all within a row
- valid: int32 [16384], P('batch'), may hold values 0 or 1
- cotangent: bfloat16 [16384, 256], P(('batch', 'module')), may hold values from -6 to 6
- gain_one: float32 [256], replicated, may hold values from 0.5 to 1.5
- w_query: bfloat16 [256, 256], replicated, may hold values from -0.375 to 0.375
- w_key: bfloat16 [256, 256], replicated, may hold values from -0.375 to 0.375
- w_value: bfloat16 [256, 256], replicated, may hold values from -0.375 to 0.375
- w_attn_out: bfloat16 [256, 256], replicated, may hold values from -2 to 2
- w_cross: bfloat16 [256, 256], replicated, may hold values from -0.375 to 0.375
- b_cross: float32 [256], replicated, may hold values from -3 to 3
- w_mix: bfloat16 [256, 256], replicated, may hold values from -3 to 3
- w_ens1: bfloat16 [1024, 256], replicated, may hold values from -0.1875 to 0.1875
- gain_two: float32 [256], replicated, may hold values from 0.5 to 1.5
- w_up: bfloat16 [256, 1024], replicated, may hold values from -0.375 to 0.375
- b_up: float32 [1024], replicated, may hold values from -3 to 3
- w_ens2: bfloat16 [1280, 256], replicated, may hold values from -0.15625 to 0.15625
Outputs:
- out_rows: float32 [16384, 256], P(('batch', 'module'))
- grad_tokens: float32 [16384, 256], P(('batch', 'module'))
- grad_gain_one: float32 [256], replicated
- grad_query: float32 [256, 256], replicated
- grad_key: float32 [256, 256], replicated
- grad_value: float32 [256, 256], replicated
- grad_attn_out: float32 [256, 256], replicated
- grad_cross: float32 [256, 256], replicated
- grad_b_cross: float32 [256], replicated
- grad_mix: float32 [256, 256], replicated
- grad_ens1: float32 [1024, 256], replicated
- grad_gain_two: float32 [256], replicated
- grad_up: float32 [256, 1024], replicated
- grad_b_up: float32 [1024], replicated
- grad_ens2: float32 [1280, 256], replicated
The draws below stay inside these ranges and needn't reach their ends.
Inputs may be any that keep to these rules, and one draw needn't show every extreme that they name: `seg_lengths`: each row's 8 lengths sum to 2048 and the longest is exactly 1024.
All inputs are finite; a program needn't handle non-finite values. No bound on the sum of `valid` on one device may be relied on, other than what follows from the above.
Results may differ from the reference program's by a relative error of at most 0.014.
Values may be sent and summed in bfloat16 or wider, within the bound.
No kernel may reach another device: no remote copies, remote signals or barrier semaphores. Data moves between devices by JAX's collectives and lax.ppermute only.
A program may use at most 64 MiB of HBM per device.

```python
import math
import jax
import jax.numpy as jnp
import numpy as np
from jax import lax

D = 256
HEADS = 4
HEAD_DIM = 64
FF = 1024
SEGS = 8
SHARD_TOK = 2048
SEG_MAX = 1024
TOKENS = 16384
N_BATCH = 8


def set_ends(entries, stream_key, smallest, largest):
    shape = entries.shape
    spot = [jax.random.randint(jax.random.fold_in(stream_key, axis), (), 0, shape[axis]) for axis in range(len(shape))]
    entries = entries.at[tuple(spot)].set(smallest)
    longest = shape.index(max(shape))
    spot[longest] = (spot[longest] + 1) % shape[longest]
    return entries.at[tuple(spot)].set(largest)


def block_scale(own_key, dims, shards, smallest, top_value):
    level, own = 1.0, jax.random.fold_in(own_key, 6)
    for position, shards_of in shards:
        heights = jnp.exp(jax.random.uniform(jax.random.fold_in(own, position), (shards_of,), jnp.float32, smallest / len(shards), top_value / len(shards)))
        level = level * jnp.repeat(heights, dims[position] // shards_of).reshape([-1 if axis == position else 1 for axis in range(len(dims))])
    return level


def length_profile(count, total, most, lean):
    portions = [(1 << 20) // math.isqrt(standing ** lean) + 1 for standing in range(2, count + 1)]
    spare, given = total - most - (count - 1), [1] * (count - 1)
    while spare > 0:
        movable = [i for i in range(count - 1) if given[i] < most]
        mass, remaining = sum([portions[i] for i in movable]), spare
        for i in movable:
            addition = min(most - given[i], max(1, remaining * portions[i] // mass), spare)
            given[i] = given[i] + addition
            spare = spare - addition
    return np.array([most] + given)


def uneven(stream_key, number_of, total, most, skew):
    if number_of == 2:
        one = jax.random.randint(stream_key, (), max(1, total - most), min(most, total - 1) + 1)
        return jnp.stack([one, total - one])
    sizes = jnp.asarray(length_profile(number_of, total, most, skew), jnp.int32)
    couples = (number_of - 1) // 2
    donor, taker = sizes[1:1 + 2 * couples:2], sizes[2:2 + 2 * couples:2]
    margin = jnp.minimum(donor - 1, most - taker)
    shifted = jax.random.randint(jax.random.fold_in(stream_key, 1), (couples,), 0, 1 << 20) % (margin + 1)
    sizes = sizes.at[1:1 + 2 * couples:2].set(donor - shifted).at[2:2 + 2 * couples:2].set(taker + shifted)
    return sizes[jax.random.permutation(jax.random.fold_in(stream_key, 2), number_of)]


def normal_values(stream_key, dims, scale, reach, cuts=(), kind=jnp.bfloat16):
    values = scale * jax.random.normal(stream_key, dims, jnp.float32)
    if cuts:
        values = values * block_scale(stream_key, dims, cuts, -0.22, 0.18)
    return jnp.clip(values, -reach, reach).astype(kind)


def setup_inputs(seed: int = 0) -> dict:
    splits = jax.random.split(jax.random.key(seed), 18)
    tokens = normal_values(splits[0], (TOKENS, D), 1.0, 6.0, ((0, 32),))
    seg_lengths = jax.vmap(lambda own: uneven(own, SEGS, SHARD_TOK, SEG_MAX, 2))(jax.random.split(splits[1], N_BATCH)).reshape((N_BATCH, SEGS)).astype(jnp.int32)
    valid = set_ends((jax.random.randint(splits[2], (TOKENS,), 0, 8) < 7).astype(jnp.int32), jax.random.fold_in(splits[2], 1), 0, 1)
    cotangent = normal_values(splits[3], (TOKENS, D), 1.0, 6.0, ((0, 32),))
    gain_one = jnp.clip(1.0 + 0.1 * jax.random.normal(splits[4], (D,), jnp.float32), 0.5, 1.5)
    w_query = normal_values(splits[5], (D, D), D ** -0.5, 0.375)
    w_key = normal_values(splits[6], (D, D), D ** -0.5, 0.375)
    w_value = normal_values(splits[7], (D, D), D ** -0.5, 0.375)
    w_attn_out = normal_values(splits[8], (D, D), (D // 32) ** -0.5, 2.0)
    w_cross = normal_values(splits[9], (D, D), D ** -0.5, 0.375)
    b_cross = normal_values(splits[10], (D,), 0.5, 3.0, (), jnp.float32)
    w_mix = normal_values(splits[11], (D, D), 0.5, 3.0)
    w_ens1 = normal_values(splits[12], (4 * D, D), (4 * D) ** -0.5, 0.1875)
    gain_two = jnp.clip(1.0 + 0.1 * jax.random.normal(splits[13], (D,), jnp.float32), 0.5, 1.5)
    w_up = normal_values(splits[14], (D, FF), D ** -0.5, 0.375)
    b_up = normal_values(splits[15], (FF,), 0.5, 3.0, (), jnp.float32)
    w_ens2 = normal_values(splits[16], (FF + D, D), (FF + D) ** -0.5, 0.15625)
    return dict(tokens=tokens, seg_lengths=seg_lengths, valid=valid, cotangent=cotangent, gain_one=gain_one, w_query=w_query, w_key=w_key, w_value=w_value, w_attn_out=w_attn_out, w_cross=w_cross, b_cross=b_cross, w_mix=w_mix, w_ens1=w_ens1, gain_two=gain_two, w_up=w_up, b_up=b_up, w_ens2=w_ens2)


@jax.custom_vjp
def low(v):
    return lax.optimization_barrier(v.astype(jnp.bfloat16)).astype(jnp.float32)

@jax.custom_vjp
def low_back(v):
    return v

def low_keep(v):
    return (low(v), None)

def low_pass(kept, grad):
    return (grad,)

def back_keep(v):
    return (v, None)

def back_low(kept, grad):
    return (low(grad),)
low.defvjp(low_keep, low_pass)
low_back.defvjp(back_keep, back_low)

def matmul_high(left, right):
    return jnp.dot(left, right, precision=lax.Precision.HIGHEST)

def layer_norm(values, gain):
    center = values - lax.optimization_barrier(jnp.mean(values, axis=-1, keepdims=True))
    return center * lax.rsqrt(lax.optimization_barrier(jnp.mean(center * center, axis=-1, keepdims=True)) + 1e-05) * gain

def shard_forward(params, block_rows, lengths, padding):
    gain_one, w_query, w_key, w_value, w_attn_out, w_cross, b_cross, w_mix, w_ens1, gain_two, w_up, b_up, w_ens2 = params
    row_count = block_rows.shape[0]
    places = jnp.arange(row_count, dtype=jnp.int32)
    bounds = jnp.cumsum(lengths).astype(jnp.int32)
    member = lax.optimization_barrier(jnp.sum((places[:, None] >= bounds[None, :]).astype(jnp.int32), axis=1)).astype(jnp.int32)
    valid_weight = padding.astype(jnp.float32)
    normed = low(layer_norm(block_rows, gain_one))
    queries = low(low_back(matmul_high(normed, w_query))).reshape(row_count, HEADS, HEAD_DIM)
    key_rows = low(low_back(matmul_high(normed, w_key))).reshape(row_count, HEADS, HEAD_DIM)
    value_rows = low(low_back(matmul_high(normed, w_value))).reshape(row_count, HEADS, HEAD_DIM)
    allowed = (member[:, None] == member[None, :]) & ((padding[None, :] > 0) | (places[:, None] == places[None, :]))
    scores = low_back(jnp.einsum('qhd,khd->hqk', queries, key_rows, precision=lax.Precision.HIGHEST) * 0.125)
    scores = jnp.where(allowed[None], scores, -1e+30)
    probs = jax.nn.softmax(scores, axis=-1)
    attended = jnp.einsum('hqk,khd->qhd', low(probs), value_rows, precision=lax.Precision.HIGHEST).reshape(row_count, D)
    attended = low(low_back(attended))
    width = 2 * HEAD_DIM
    modules = []
    for group in range(2):
        piece = matmul_high(attended[:, group * width:(group + 1) * width], w_attn_out[group * width:(group + 1) * width])
        modules.append(low(low_back(piece)))
    crossed = low_back(matmul_high(normed, w_cross) + b_cross)
    modules.append(low(low_back(normed * crossed)))
    onehot = (member[:, None] == jnp.arange(SEGS, dtype=jnp.int32)[None, :]).astype(jnp.float32)
    counts = lax.optimization_barrier(jnp.sum(onehot * valid_weight[:, None], axis=0))
    seg_sums = matmul_high(onehot.T, normed * valid_weight[:, None])
    seg_means = seg_sums / jnp.maximum(counts, 1.0)[:, None]
    mixed = low(matmul_high(onehot, seg_means))
    modules.append(low(low_back(matmul_high(mixed, w_mix))))
    joined = jnp.concatenate(modules, axis=1)
    first = block_rows + low_back(matmul_high(joined, w_ens1))
    normed_two = low(layer_norm(first, gain_two))
    inner = low_back(matmul_high(normed_two, w_up) + b_up)
    active = low(jax.nn.gelu(inner, approximate=False))
    return first + low_back(matmul_high(jnp.concatenate([active, normed_two], axis=1), w_ens2))

def reference(tokens, seg_lengths, valid, cotangent, gain_one, w_query, w_key, w_value, w_attn_out, w_cross, b_cross, w_mix, w_ens1, gain_two, w_up, b_up, w_ens2):
    params = tuple((entry.astype(jnp.float32) for entry in (gain_one, w_query, w_key, w_value, w_attn_out, w_cross, b_cross, w_mix, w_ens1, gain_two, w_up, b_up, w_ens2)))
    start = tokens.astype(jnp.float32)

    def forward(weights, inputs):

        def one_shard(carry, pieces):
            block_rows, lengths, padding = pieces
            return (carry, shard_forward(weights, block_rows, lengths, padding))
        blocks = inputs.reshape(N_BATCH, SHARD_TOK, D)
        paddings = valid.reshape(N_BATCH, SHARD_TOK)
        carry, result = lax.scan(jax.checkpoint(one_shard), jnp.zeros((), jnp.float32), (blocks, seg_lengths, paddings))
        return result.reshape(TOKENS, D)
    result, pull = jax.vjp(forward, params, start)
    grads, grad_start = pull(cotangent.astype(jnp.float32))
    return (result, grad_start, grads[0], grads[1], grads[2], grads[3], grads[4], grads[5], grads[6], grads[7], grads[8], grads[9], grads[10], grads[11], grads[12])
```

```python
import functools

import jax
import jax.numpy as jnp
from jax import lax
from jax.experimental import pallas as pl
from jax.experimental.pallas import tpu as pltpu
from jax.sharding import PartitionSpec as P

D = 256
HEADS = 4
HEAD_DIM = 64
FF = 1024
SEGS = 8
LANES = 128
WIDE = HEADS * LANES
HUGE = -1e30
BF = jnp.bfloat16
F32 = jnp.float32
MIB = 1024 * 1024


def low(v):
    return v.astype(BF)


def high(v):
    return v.astype(F32)


def dot(a, b):
    return jnp.dot(a, b, preferred_element_type=F32)


def dot_nt(a, b):
    return lax.dot_general(a, b, (((1,), (1,)), ((), ())), preferred_element_type=F32)


def dot_tn(a, b):
    return lax.dot_general(a, b, (((0,), (0,)), ((), ())), preferred_element_type=F32)


def head_sums(selector, product):
    upper = low(product)
    lower = low(product - high(upper))
    return dot_nt(selector, upper) + dot_nt(selector, lower)


def unit_rows(values):
    center = values - jnp.mean(values, axis=1, keepdims=True)
    scale = lax.rsqrt(jnp.mean(center * center, axis=1, keepdims=True) + 1e-05)
    return center * scale, scale


def norm_back(grad, unit, scale, gain):
    scaled = grad * gain
    first_mean = jnp.mean(scaled, axis=1, keepdims=True)
    second_mean = jnp.mean(scaled * unit, axis=1, keepdims=True)
    return scale * (scaled - first_mean - unit * second_mean)


def in_vmem():
    return pl.BlockSpec(memory_space=pltpu.VMEM)


def in_smem():
    return pl.BlockSpec(memory_space=pltpu.SMEM)


def call(body, outs, n_smem, n_vmem, scratch=(), limit=48, flops=0):
    return pl.pallas_call(
        body,
        out_shape=[jax.ShapeDtypeStruct(shape, kind) for shape, kind in outs],
        in_specs=[in_smem()] * n_smem + [in_vmem()] * n_vmem,
        out_specs=[in_vmem()] * len(outs),
        scratch_shapes=list(scratch),
        compiler_params=pltpu.CompilerParams(vmem_limit_bytes=limit * MIB),
        cost_estimate=pl.CostEstimate(flops=flops, bytes_accessed=1 * MIB, transcendentals=0),
    )


def widen(weight):
    rows = weight.shape[0]
    gap = jnp.zeros((rows, LANES - HEAD_DIM), weight.dtype)
    pieces = []
    for head in range(HEADS):
        pieces += [weight[:, head * HEAD_DIM : (head + 1) * HEAD_DIM], gap]
    return jnp.concatenate(pieces, axis=1)


def widen_rows(weight):
    gap = jnp.zeros((LANES - HEAD_DIM, weight.shape[1]), weight.dtype)
    pieces = []
    for head in range(HEADS):
        pieces += [weight[head * HEAD_DIM : (head + 1) * HEAD_DIM], gap]
    return jnp.concatenate(pieces, axis=0)


def narrow(wide):
    return jnp.concatenate(
        [wide[:, h * LANES : h * LANES + HEAD_DIM] for h in range(HEADS)], axis=1
    )


def narrow_rows(wide):
    return jnp.concatenate([wide[h * LANES : h * LANES + HEAD_DIM] for h in range(HEADS)], axis=0)


def segment_rows(seg_ref, first_place, count):
    spread = lax.broadcasted_iota(jnp.int32, (16, count), 0)
    places = lax.broadcasted_iota(jnp.int32, (16, count), 1) + first_place
    begin = jnp.zeros((16, count), jnp.int32)
    end = jnp.zeros((16, count), jnp.int32)
    edge = jnp.int32(0)
    for j in range(SEGS):
        begin = jnp.where(spread == j, edge, begin)
        edge = edge + seg_ref[0, j]
        end = jnp.where(spread == j, edge, end)
    return spread, (places >= begin) & (places < end)


def lane_selector(top):
    rows = lax.broadcasted_iota(jnp.int32, (16, WIDE), 0)
    lanes = lax.broadcasted_iota(jnp.int32, (16, WIDE), 1)
    return ((lanes & (LANES - 1)) == rows + HEAD_DIM) & (rows < top)


def head_selector():
    rows = lax.broadcasted_iota(jnp.int32, (16, WIDE), 0)
    lanes = lax.broadcasted_iota(jnp.int32, (16, WIDE), 1)
    return low(jnp.where((lanes >> 7) == rows, 1.0, 0.0))


def prep_kernel(wq, wk, wv, wo, wq_pad, wk_pad, wv_pad, wo_pad, wk_t, wv_t):
    wq_pad[...] = low(widen(high(wq[...])))
    wk_pad[...] = low(widen(high(wk[...])))
    wv_pad[...] = low(widen(high(wv[...])))
    wo_pad[...] = low(widen_rows(high(wo[...])))
    wk_t[...] = low(high(wk[...]).T)
    wv_t[...] = low(high(wv[...]).T)


def forward_kernel(
    own_rows, rows, chunk,
    me_ref, seg_ref,
    t0, t1, t2, t3, valid, cot,
    gain_one, wq_pad, wk_pad, wv_pad, wo_pad, wk_t, wv_t,
    w_cross, b_cross, w_mix, w_ens1, gain_two, w_up, b_up, w_ens2,
    out_rows, d_first_out, dn_own, payload, vectors,
    normed, q_aug, k_aug, v_pad, kt, grad_att, lse_out, delta_out, pself_out, dself_out, seg_grad_out,
    vt, scores, o_t,
):
    me = me_ref[0]
    base = pl.multiple_of(me * own_rows, own_rows)
    gain = gain_one[...]
    for delta, piece in enumerate((t0, t1, t2, t3)):
        unit, _ = unit_rows(high(piece[...]))
        at = pl.multiple_of((me ^ delta) * own_rows, own_rows)
        normed[pl.ds(at, own_rows), :] = low(unit * gain)
    normed_own = normed[pl.ds(base, own_rows), :]

    valid_row = valid[...]
    spread, inside = segment_rows(seg_ref, 0, rows)
    real = valid_row > 0
    inside_valid = jnp.where(inside & real, 1.0, 0.0)
    counts = jnp.maximum(jnp.sum(inside_valid, axis=1, keepdims=True), 1.0)
    code = jnp.where(inside, HUGE, 0.0)
    code = jnp.where(spread == SEGS, jnp.where(real, 0.0, HUGE), code)
    lanes9 = low(jnp.where(lane_selector(SEGS + 1), 1.0, 0.0))
    k_wide = dot(normed[...], wk_pad[...])
    k_aug[...] = low(k_wide + dot_tn(low(code), lanes9))
    _, inside_own = segment_rows(seg_ref, base, own_rows)
    own_code = jnp.where(inside_own, 0.0, 1.0)
    q_wide = dot(normed_own, wq_pad[...])
    q_aug[...] = low(q_wide * 0.125 + dot_tn(low(own_code), lanes9))
    v_pad[...] = low(dot(normed[...], wv_pad[...]))
    kt[...] = low(dot_nt(wk_t[...], normed[...]))
    vt[...] = low(dot_nt(wv_t[...], normed[...]))

    heads16 = head_selector()
    lanes_own = lax.broadcasted_iota(jnp.int32, (own_rows, WIDE), 1) & (LANES - 1)
    k_own = k_aug[pl.ds(base, own_rows), :]
    v_own = v_pad[pl.ds(base, own_rows), :]
    self_product = jnp.where(lanes_own < HEAD_DIM, high(q_aug[...]) * high(k_own), 0.0)
    self_scores = head_sums(heads16, self_product)
    own_real = valid[:, pl.ds(base, own_rows)] > 0
    vt_own = vt[:, pl.ds(base, own_rows)]
    o_t[...] = jnp.zeros_like(o_t)
    lse_out[...] = jnp.zeros_like(lse_out)
    for h in range(HEADS):
        lanes = slice(h * LANES, (h + 1) * LANES)
        q_h = q_aug[:, lanes]
        top = jnp.where(own_real, HUGE, self_scores[h : h + 1])
        self_h = top
        for c in range(rows // chunk):
            part = dot_nt(k_aug[c * chunk : (c + 1) * chunk, lanes], q_h)
            scores[c * chunk : (c + 1) * chunk, :] = part
            top = jnp.maximum(top, jnp.max(part, axis=0, keepdims=True))
        p_self = jnp.exp(self_h - top)
        total = p_self
        acc = high(low(p_self)) * high(vt_own[h * HEAD_DIM : (h + 1) * HEAD_DIM])
        for c in range(rows // chunk):
            p = jnp.exp(scores[c * chunk : (c + 1) * chunk, :] - top)
            total = total + jnp.sum(p, axis=0, keepdims=True)
            acc = acc + dot(
                vt[h * HEAD_DIM : (h + 1) * HEAD_DIM, c * chunk : (c + 1) * chunk], low(p)
            )
        o_t[h * LANES : h * LANES + HEAD_DIM, :] = acc / total
        lse_out[h : h + 1, :] = top + jnp.log(total)
    att = o_t[...].T
    att_low = low(att)

    modules = []
    for g in range(2):
        lanes = slice(g * 256, (g + 1) * 256)
        modules.append(low(dot(att_low[:, lanes], wo_pad[lanes, :])))
    crossed = dot(normed_own, w_cross[...]) + b_cross[...]
    modules.append(low(high(normed_own) * crossed))
    seg_mean = low(dot(low(inside_valid), normed[...]) / counts)
    own_member = low(jnp.where(inside_own, 1.0, 0.0))
    mixed = low(dot_tn(own_member, seg_mean))
    modules.append(low(dot(mixed, w_mix[...])))
    first = high(t0[...])
    for i in range(4):
        first = first + dot(modules[i], w_ens1[i * D : (i + 1) * D, :])
    unit_two, scale_two = unit_rows(first)
    normed_two = low(unit_two * gain_two[...])
    inner = dot(normed_two, w_up[...]) + b_up[...]
    cdf = 0.5 * (1.0 + lax.erf(inner * 0.7071067811865476))
    active = low(inner * cdf)
    slope = cdf + inner * jnp.exp(-0.5 * inner * inner) * 0.3989422804014327
    out_rows[...] = first + (dot(active, w_ens2[:FF, :]) + dot(normed_two, w_ens2[FF:, :]))

    half = payload.shape[0] // 2

    def put(at, grad):
        middle = grad.shape[0] // 2
        payload[at : at + middle, :] = low(grad[:middle])
        payload[half + at : half + at + middle, :] = low(grad[middle:])
        return at + middle

    e2 = cot[...]
    at = put(0, dot_tn(active, e2))
    at = put(at, dot_tn(normed_two, e2))
    d_inner = low(dot_nt(e2, w_ens2[:FF, :]) * slope)
    b_up_grad = jnp.sum(high(d_inner), axis=0, keepdims=True)
    grad_up = dot_tn(normed_two, d_inner)
    for i in range(FF // D):
        at = put(at, grad_up[:, i * D : (i + 1) * D])
    d_norm2 = dot_nt(e2, w_ens2[FF:, :]) + dot_nt(d_inner, w_up[...])
    d_first = high(e2) + norm_back(d_norm2, unit_two, scale_two, gain_two[...])
    d_first_out[...] = d_first
    e1 = low(d_first)
    d_modules = []
    for i in range(4):
        at = put(at, dot_tn(modules[i], e1))
        d_modules.append(low(dot_nt(e1, w_ens1[i * D : (i + 1) * D, :])))
    out_grads = []
    for g in range(2):
        lanes = slice(g * 256, (g + 1) * 256)
        out_grads.append(dot_tn(att_low[:, lanes], d_modules[g]))
        grad_att[:, lanes] = low(dot_nt(d_modules[g], wo_pad[lanes, :]))
    at = put(at, narrow_rows(jnp.concatenate(out_grads, axis=0)))
    d_cross = low(high(d_modules[2]) * high(normed_own))
    at = put(at, dot_tn(normed_own, d_cross))
    at = put(at, dot_tn(mixed, d_modules[3]))
    dn_own[...] = high(d_modules[2]) * crossed + dot_nt(d_cross, w_cross[...])
    d_mixed = dot_nt(d_modules[3], w_mix[...])
    mixed_up = low(d_mixed)
    mixed_down = low(d_mixed - high(mixed_up))
    seg_grad_out[...] = (dot(own_member, mixed_up) + dot(own_member, mixed_down)) / counts
    vectors[...] = jnp.zeros_like(vectors)
    for i in range(FF // D):
        vectors[i : i + 1, :] = b_up_grad[:, i * D : (i + 1) * D]
    vectors[4:5, :] = jnp.sum(high(d_cross), axis=0, keepdims=True)
    vectors[5:6, :] = jnp.sum(d_norm2 * unit_two, axis=0, keepdims=True)

    d_att = high(grad_att[...])
    delta = head_sums(heads16, d_att * att)
    delta_out[...] = delta
    p_self = jnp.where(own_real, 0.0, jnp.exp(self_scores - lse_out[...]))
    dp_self = head_sums(heads16, d_att * high(v_own))
    pself_out[...] = low(p_self)
    dself_out[...] = low(p_self * (dp_self - delta))


def backward_kernel(
    own_rows, rows, chunk,
    me_ref, seg_ref,
    normed, q_aug, k_aug, v_pad, kt, grad_att, lse, delta, pself, dself, seg_grad, dn_own, valid,
    gain_one, wq_pad, wk_pad, wv_pad, vectors,
    keep, send,
    dk, dv, dq_t, dn, both,
):
    me = me_ref[0]
    base = pl.multiple_of(me * own_rows, own_rows)
    heads16 = head_selector()
    dq_t[...] = jnp.zeros_like(dq_t)
    kt_own = kt[:, pl.ds(base, own_rows)]
    for h in range(HEADS):
        lanes = slice(h * LANES, (h + 1) * LANES)
        q_h = q_aug[:, lanes]
        g_h = grad_att[:, lanes]
        lse_h = lse[h : h + 1, :]
        delta_h = delta[h : h + 1, :]
        acc = high(dself[h : h + 1, :]) * high(kt_own[h * HEAD_DIM : (h + 1) * HEAD_DIM])
        for c in range(rows // chunk):
            at = slice(c * chunk, (c + 1) * chunk)
            p = jnp.exp(dot_nt(k_aug[at, lanes], q_h) - lse_h)
            ds = low(p * (dot_nt(v_pad[at, lanes], g_h) - delta_h))
            dv[at, lanes] = dot(low(p), g_h)
            dk[at, lanes] = dot(ds, q_h)
            acc = acc + dot(kt[h * HEAD_DIM : (h + 1) * HEAD_DIM, at], ds)
        dq_t[h * LANES : h * LANES + HEAD_DIM, :] = acc
    own = pl.ds(base, own_rows)
    dk[own, :] = dk[own, :] + dot_tn(dself[...], heads16) * high(q_aug[...])
    dv[own, :] = dv[own, :] + dot_tn(pself[...], heads16) * high(grad_att[...])
    dq = low(dq_t[...].T * 0.125)
    dk_low = low(dk[...])
    dv_low = low(dv[...])
    _, inside = segment_rows(seg_ref, 0, rows)
    member = low(jnp.where(inside & (valid[...] > 0), 1.0, 0.0))
    up = low(seg_grad[...])
    down = low(seg_grad[...] - high(up))
    mixing = dot_tn(member, up) + dot_tn(member, down)
    dn[...] = dot_nt(dk_low, wk_pad[...]) + dot_nt(dv_low, wv_pad[...]) + mixing
    dn[own, :] = dn[own, :] + dot_nt(dq, wq_pad[...]) + dn_own[...]
    gain_grad = jnp.sum(dn[...] * high(normed[...]), axis=0, keepdims=True) / gain_one[...]

    def rows_of(step):
        return dn[pl.ds(pl.multiple_of((me ^ step) * own_rows, own_rows), own_rows), :]

    keep[:own_rows, :] = low(rows_of(0))
    send[:own_rows, :] = low(rows_of(1))
    keep[own_rows : 2 * own_rows, :] = low(rows_of(2))
    send[own_rows : 2 * own_rows, :] = low(rows_of(3))
    normed_own = normed[own, :]
    third = D // 2
    for i, grad in enumerate(
        (
            narrow(dot_tn(normed_own, dq)),
            narrow(dot_tn(normed[...], dk_low)),
            narrow(dot_tn(normed[...], dv_low)),
        )
    ):
        both[i * third : (i + 1) * third, :] = low(grad[:third])
        both[(3 + i) * third : (4 + i) * third, :] = low(grad[third:])
    core = me & 1
    mine = pl.ds(pl.multiple_of(core * 3 * third, third), 3 * third)
    other = pl.ds(pl.multiple_of((1 - core) * 3 * third, third), 3 * third)
    keep[2 * own_rows : 2 * own_rows + 3 * third, :] = both[mine, :]
    send[2 * own_rows : 2 * own_rows + 3 * third, :] = both[other, :]
    tail = lax.broadcasted_iota(jnp.int32, (16, D), 0)
    row = jnp.where(tail == 6, gain_grad, vectors[...])
    keep[2 * own_rows + 3 * third :, :] = low(row)
    send[2 * own_rows + 3 * third :, :] = low(row)


def finish_kernel(mine, other, tokens, d_first, gain_one, grad_tokens):
    unit, scale = unit_rows(high(tokens[...]))
    total = high(mine[...]) + high(other[...])
    grad_tokens[...] = d_first[...] + norm_back(total, unit, scale, gain_one[...])


def swap(value, axis, count, step):
    return lax.ppermute(value, axis, [(i, i ^ step) for i in range(count)])


def split(value, bit):
    half = value.shape[0] // 2
    return (
        lax.dynamic_slice_in_dim(value, bit * half, half, 0),
        lax.dynamic_slice_in_dim(value, (1 - bit) * half, half, 0),
    )


def join(mine, other, bit):
    return jnp.where(
        bit == 0, jnp.concatenate([mine, other], 0), jnp.concatenate([other, mine], 0)
    )


def added(one, two):
    return low(high(one) + high(two))


def shards(
    n_batch,
    n_module,
    tokens,
    seg_lengths,
    valid,
    cotangent,
    gain_one,
    w_query,
    w_key,
    w_value,
    w_attn_out,
    w_cross,
    b_cross,
    w_mix,
    w_ens1,
    gain_two,
    w_up,
    b_up,
    w_ens2,
):
    module = lax.axis_index("module")
    batch = lax.axis_index("batch")
    core = module & 1
    y_bit = (module >> 1) & 1
    x_bit = batch & 1
    own_rows = tokens.shape[0]
    rows = valid.shape[0]
    chunk = 512
    me = jnp.reshape(module, (1,)).astype(jnp.int32)

    def by_core(value):
        return swap(value, "module", n_module, 1)

    def by_y(value):
        return swap(value, "module", n_module, 2)

    def by_batch(value, step):
        return swap(value, "batch", n_batch, step)

    from_y = by_y(tokens)
    from_core = by_core(tokens)
    from_far = by_core(from_y)
    bf_square = ((D, D), BF)
    wq_pad, wk_pad, wv_pad, wo_pad, wk_t, wv_t = call(
        prep_kernel, [((D, WIDE), BF)] * 3 + [((WIDE, D), BF)] + [bf_square] * 2, 0, 4
    )(w_query, w_key, w_value, w_attn_out)
    valid_row = valid.reshape(1, rows)
    gain_row = gain_one.reshape(1, D)
    (
        out_rows, d_first, dn_own, payload, vectors,
        normed, q_aug, k_aug, v_pad, kt, grad_att, lse, delta, pself, dself, seg_grad,
    ) = call(
        functools.partial(forward_kernel, own_rows, rows, chunk),
        [
            ((own_rows, D), F32), ((own_rows, D), F32), ((own_rows, D), F32), ((16 * D, D), BF), ((16, D), F32),
            ((rows, D), BF), ((own_rows, WIDE), BF), ((rows, WIDE), BF), ((rows, WIDE), BF), ((D, rows), BF),
            ((own_rows, WIDE), BF), ((16, own_rows), F32), ((16, own_rows), F32), ((16, own_rows), BF),
            ((16, own_rows), BF), ((16, D), F32),
        ],
        2, 21,
        [pltpu.VMEM((D, rows), BF), pltpu.VMEM((rows, own_rows), F32), pltpu.VMEM((WIDE, own_rows), F32)],
    )(
        me, seg_lengths, tokens, from_core, from_y, from_far, valid_row, cotangent,
        gain_row, wq_pad, wk_pad, wv_pad, wo_pad, wk_t, wv_t,
        w_cross, b_cross.reshape(1, D), w_mix, w_ens1, gain_two.reshape(1, D), w_up, b_up.reshape(1, FF), w_ens2,
    )

    keep, send = split(payload, core)
    big = added(keep, by_core(send))
    middle = big.shape[0] // 2
    a_keep, a_send = split(big[:middle], y_bit)
    b_keep, b_send = split(big[middle:], x_bit)
    a = added(a_keep, by_y(a_send))
    b = added(b_keep, by_batch(b_send, 1))
    a_keep, a_send = split(a, x_bit)
    b_keep, b_send = split(b, y_bit)
    a = added(a_keep, by_batch(a_send, 1))
    b = added(b_keep, by_y(b_send))

    def through_batch(value):
        steps = []
        step = 2
        while step < n_batch:
            steps.append(step)
            step *= 2
        if not steps:
            return value
        low_bit = (batch >> 1) & 1
        kept, sent = split(value, low_bit)
        value = added(kept, by_batch(sent, steps[0]))
        for step in steps[1:]:
            value = added(value, by_batch(value, step))
        return join(value, by_batch(value, steps[0]), low_bit)

    ab = through_batch(jnp.concatenate([a, b], axis=0))
    a, b = ab[: middle // 4], ab[middle // 4 :]
    a = join(a, by_batch(a, 1), x_bit)
    b = join(b, by_y(b), y_bit)
    a = join(a, by_y(a), y_bit)
    b = join(b, by_batch(b, 1), x_bit)
    big = jnp.concatenate([a, b], axis=0)
    big = join(big, by_core(big), core)

    third = D // 2
    small = 2 * own_rows + 3 * third + 16
    keep, send = call(
        functools.partial(backward_kernel, own_rows, rows, chunk),
        [((small, D), BF)] * 2,
        2, 18,
        [
            pltpu.VMEM((rows, WIDE), F32), pltpu.VMEM((rows, WIDE), F32), pltpu.VMEM((WIDE, own_rows), F32),
            pltpu.VMEM((rows, D), F32), pltpu.VMEM((6 * third, D), BF),
        ],
    )(
        me, seg_lengths, normed, q_aug, k_aug, v_pad, kt, grad_att, lse, delta, pself, dself, seg_grad,
        dn_own, valid_row, gain_row, wq_pad, wk_pad, wv_pad, vectors,
    )
    total = added(keep, by_core(send))
    dn_mine, dn_other = total[:own_rows], total[own_rows : 2 * own_rows]
    qkv_keep, qkv_send = split(total[2 * own_rows : 2 * own_rows + 3 * third], y_bit)
    vec = total[2 * own_rows + 3 * third :]
    got = by_y(jnp.concatenate([dn_other, qkv_send, vec], axis=0))
    (grad_tokens,) = call(finish_kernel, [((own_rows, D), F32)], 0, 5)(
        dn_mine, got[:own_rows], tokens, d_first, gain_row
    )
    qkv = added(qkv_keep, got[own_rows:-16])
    vec = added(vec, got[-16:])
    qkv_keep, qkv_send = split(qkv, x_bit)
    got = by_batch(jnp.concatenate([qkv_send, vec], axis=0), 1)
    qkv = added(qkv_keep, got[:-16])
    vec = added(vec, got[-16:])
    step = 2
    while step < n_batch:
        both = jnp.concatenate([qkv, vec], axis=0)
        both = added(both, by_batch(both, step))
        qkv, vec = both[:-16], both[-16:]
        step *= 2
    qkv = join(qkv, by_batch(qkv, 1), x_bit)
    qkv = join(qkv, by_y(qkv), y_bit)
    qkv = join(qkv, by_core(qkv), core)

    half = big.shape[0] // 2
    place = [0]

    def take(source, count, split_at):
        at = place[0]
        place[0] = at + count // 2
        return high(
            jnp.concatenate(
                [source[at : at + count // 2], source[split_at + at : split_at + at + count // 2]],
                axis=0,
            )
        )

    ens2 = jnp.concatenate([take(big, FF, half), take(big, D, half)], axis=0)
    up = jnp.concatenate([take(big, D, half) for _ in range(FF // D)], axis=1)
    ens1 = jnp.concatenate([take(big, D, half) for _ in range(4)], axis=0)
    attn_out = take(big, D, half)
    cross = take(big, D, half)
    mix = take(big, D, half)
    place[0] = 0
    query, key, value = [take(qkv, D, 3 * third) for _ in range(3)]
    vec = high(vec)
    return (
        out_rows, grad_tokens, vec[6], query, key, value, attn_out, cross, vec[4], mix, ens1, vec[5],
        up, vec[:4].reshape(FF), ens2,
    )


def solution(mesh):
    rows = P(("batch", "module"), None)
    in_specs = (rows, P("batch", None), P("batch"), rows) + (P(),) * 13
    out_specs = (rows, rows) + (P(),) * 13
    body = functools.partial(shards, mesh.shape["batch"], mesh.shape["module"])
    return jax.shard_map(body, mesh=mesh, in_specs=in_specs, out_specs=out_specs, check_vma=False)
```

```python
import functools

import jax
import jax.numpy as jnp
from jax import lax
from jax.experimental import pallas as pl
from jax.experimental.pallas import tpu as pltpu
from jax.sharding import PartitionSpec as P

D = 256
HEADS = 4
HEAD_DIM = 64
FF = 1024
SEGS = 8
LANES = 128
WIDE = HEADS * LANES
HUGE = -1e30
BF = jnp.bfloat16
F32 = jnp.float32
MIB = 1024 * 1024


def low(v):
    return v.astype(BF)


def high(v):
    return v.astype(F32)


def dot(a, b):
    return jnp.dot(a, b, preferred_element_type=F32)


def dot_nt(a, b):
    return lax.dot_general(a, b, (((1,), (1,)), ((), ())), preferred_element_type=F32)


def dot_tn(a, b):
    return lax.dot_general(a, b, (((0,), (0,)), ((), ())), preferred_element_type=F32)


def head_sums(selector, product):
    upper = low(product)
    lower = low(product - high(upper))
    return dot_nt(selector, upper) + dot_nt(selector, lower)


def unit_rows(values):
    center = values - jnp.mean(values, axis=1, keepdims=True)
    scale = lax.rsqrt(jnp.mean(center * center, axis=1, keepdims=True) + 1e-05)
    return center * scale, scale


def norm_back(grad, unit, scale, gain):
    scaled = grad * gain
    first_mean = jnp.mean(scaled, axis=1, keepdims=True)
    second_mean = jnp.mean(scaled * unit, axis=1, keepdims=True)
    return scale * (scaled - first_mean - unit * second_mean)


def call(body, outs, scratch, places, limit, microseconds):
    spaces = {"s": pltpu.SMEM, "v": pltpu.VMEM, "h": pltpu.HBM}
    return pl.pallas_call(
        body,
        out_shape=[jax.ShapeDtypeStruct(shape, kind) for shape, kind in outs],
        in_specs=[pl.BlockSpec(memory_space=spaces[place]) for place in places],
        out_specs=[pl.BlockSpec(memory_space=pltpu.VMEM)] * len(outs),
        scratch_shapes=list(scratch),
        compiler_params=pltpu.CompilerParams(vmem_limit_bytes=limit * MIB),
        cost_estimate=pl.CostEstimate(
            flops=microseconds * 10**9, bytes_accessed=1 * MIB, transcendentals=0
        ),
    )


def widen(weight):
    rows = weight.shape[0]
    gap = jnp.zeros((rows, LANES - HEAD_DIM), weight.dtype)
    pieces = []
    for head in range(HEADS):
        pieces += [weight[:, head * HEAD_DIM : (head + 1) * HEAD_DIM], gap]
    return jnp.concatenate(pieces, axis=1)


def widen_rows(weight):
    gap = jnp.zeros((LANES - HEAD_DIM, weight.shape[1]), weight.dtype)
    pieces = []
    for head in range(HEADS):
        pieces += [weight[head * HEAD_DIM : (head + 1) * HEAD_DIM], gap]
    return jnp.concatenate(pieces, axis=0)


def narrow(wide):
    return jnp.concatenate(
        [wide[:, h * LANES : h * LANES + HEAD_DIM] for h in range(HEADS)], axis=1
    )


def narrow_rows(wide):
    return jnp.concatenate([wide[h * LANES : h * LANES + HEAD_DIM] for h in range(HEADS)], axis=0)


def segment_rows(seg_ref, first_place, count):
    spread = lax.broadcasted_iota(jnp.int32, (16, count), 0)
    places = lax.broadcasted_iota(jnp.int32, (16, count), 1) + first_place
    begin = jnp.zeros((16, count), jnp.int32)
    end = jnp.zeros((16, count), jnp.int32)
    edge = jnp.int32(0)
    for j in range(SEGS):
        begin = jnp.where(spread == j, edge, begin)
        edge = edge + seg_ref[0, j]
        end = jnp.where(spread == j, edge, end)
    return spread, (places >= begin) & (places < end)


def head_selector():
    rows = lax.broadcasted_iota(jnp.int32, (16, WIDE), 0)
    lanes = lax.broadcasted_iota(jnp.int32, (16, WIDE), 1)
    return low(jnp.where((lanes >> 7) == rows, 1.0, 0.0))


def start_kernel(me_ref, token):
    token[...] = jnp.zeros_like(token)


def project(rows_in, gain, code, wk_pad, wv_pad, wk_t, wv_t, at, normed, normed_t, k_aug, v_pad, kt, vt):
    count = rows_in.shape[0]
    unit, _ = unit_rows(high(rows_in))
    value = low(unit * gain)
    flipped = value.T
    normed[at : at + count, :] = value
    normed_t[:, at : at + count] = flipped
    wide = low(dot(value, wk_pad))
    k_aug[at : at + count, :] = wide + jnp.concatenate([code] * HEADS, axis=1)
    v_pad[at : at + count, :] = low(dot(value, wv_pad))
    kt[:, at : at + count] = low(dot(wk_t, flipped))
    vt[:, at : at + count] = low(dot(wv_t, flipped))


def lane_codes(rows_code):
    picked = lax.broadcasted_iota(jnp.int32, (16, LANES), 1) - HEAD_DIM
    picked = (picked == lax.broadcasted_iota(jnp.int32, (16, LANES), 0)) & (picked <= SEGS)
    return low(dot_tn(low(rows_code), low(jnp.where(picked, 1.0, 0.0))))


def first_kernel(
    own_rows,
    me_ref, seg, token, core_rows, tokens, valid, gain_one, wq, wk, wv, wo,
    wq_pad, wk_pad, wv_pad, wo_pad, wk_t, wv_t, codes, real, counted,
    normed, normed_t, q_aug, k_aug, v_pad, kt, vt,
):
    me = me_ref[0]
    for step in range(4):
        at = pl.multiple_of((me ^ step) * own_rows, own_rows)
        spread, inside = segment_rows(seg, at, own_rows)
        ok = valid[:, pl.ds(at, own_rows)] > 0
        code = jnp.where(inside, HUGE, 0.0)
        code = jnp.where(spread == SEGS, jnp.where(ok, 0.0, HUGE), code)
        codes[step * own_rows : (step + 1) * own_rows, :] = lane_codes(code)
        real[:, step * own_rows : (step + 1) * own_rows] = jnp.where(ok, 1.0, 0.0)
        counted[:, step * own_rows : (step + 1) * own_rows] = low(jnp.where(inside & ok, 1.0, 0.0))
    wq_pad[...] = low(widen(high(wq[...])))
    wk_pad[...] = low(widen(high(wk[...])))
    wv_pad[...] = low(widen(high(wv[...])))
    wo_pad[...] = low(widen_rows(high(wo[...])))
    wk_t[...] = wk[...].T
    wv_t[...] = wv[...].T
    gain = gain_one[...]
    for step, rows_in in enumerate((tokens, core_rows)):
        at = step * own_rows
        project(
            rows_in[...], gain, codes[at : at + own_rows, :], wk_pad[...], wv_pad[...], wk_t[...], wv_t[...], at,
            normed, normed_t, k_aug, v_pad, kt, vt,
        )
    spread, inside = segment_rows(seg, pl.multiple_of(me * own_rows, own_rows), own_rows)
    own_code = lane_codes(jnp.where(inside, 0.0, 1.0))
    scaled = low(dot(normed[:own_rows, :], wq_pad[...]) * 0.125)
    q_aug[...] = scaled + jnp.concatenate([own_code] * HEADS, axis=1)


def forward_kernel(
    own_rows,
    me_ref, y_rows, far_rows, codes, real, counted, tokens, cot,
    gain_one, wk_pad, wv_pad, wo_pad, wk_t, wv_t,
    w_cross, b_cross, w_mix, w_ens1, gain_two, w_up, b_up, w_ens2,
    normed_a, normed_ta, q_aug, k_a, v_a, kt_a, vt_a,
    out_rows, d_first_out, dn_own, payload, vectors,
    normed_b, normed_tb, k_b, v_b, kt_b,
    grad_att, lse_out, delta_out, pself_out, dself_out, seg_grad_out,
    vt_b, scores, o_t,
):
    gain = gain_one[...]
    for step, rows_in in enumerate((y_rows[...], far_rows[:own_rows, :])):
        at = step * own_rows
        project(
            rows_in, gain, codes[at + 2 * own_rows : at + 3 * own_rows, :],
            wk_pad[...], wv_pad[...], wk_t[...], wv_t[...], at,
            normed_b, normed_tb, k_b, v_b, kt_b, vt_b,
        )
    normed_own = normed_a[:own_rows, :]
    heads16 = head_selector()
    lanes_own = lax.broadcasted_iota(jnp.int32, (own_rows, WIDE), 1) & (LANES - 1)
    v_own = v_a[:own_rows, :]
    self_product = jnp.where(
        lanes_own < HEAD_DIM, high(q_aug[...]) * high(k_a[:own_rows, :]), 0.0
    )
    self_scores = head_sums(heads16, self_product)
    own_real = real[:, :own_rows] > 0
    o_t[...] = jnp.zeros_like(o_t)
    lse_out[...] = jnp.zeros_like(lse_out)
    half_keys = 2 * own_rows
    for h in range(HEADS):
        lanes = slice(h * LANES, (h + 1) * LANES)
        rows_h = slice(h * HEAD_DIM, (h + 1) * HEAD_DIM)
        q_h = q_aug[:, lanes]
        top = jnp.where(own_real, HUGE, self_scores[h : h + 1])
        self_h = top
        for c, k_half in enumerate((k_a, k_b)):
            part = dot_nt(k_half[:, lanes], q_h)
            scores[c * half_keys : (c + 1) * half_keys, :] = part
            top = jnp.maximum(top, jnp.max(part, axis=0, keepdims=True))
        p_self = jnp.exp(self_h - top)
        total = p_self
        acc = high(low(p_self)) * high(vt_a[rows_h, :own_rows])
        for c, vt_half in enumerate((vt_a, vt_b)):
            p = jnp.exp(scores[c * half_keys : (c + 1) * half_keys, :] - top)
            total = total + jnp.sum(p, axis=0, keepdims=True)
            acc = acc + dot(vt_half[rows_h, :], low(p))
        o_t[h * LANES : h * LANES + HEAD_DIM, :] = acc / total
        lse_out[h : h + 1, :] = top + jnp.log(total)
    att = o_t[...].T
    att_low = low(att)

    modules = []
    for g in range(2):
        lanes = slice(g * 256, (g + 1) * 256)
        modules.append(low(dot(att_low[:, lanes], wo_pad[lanes, :])))
    crossed = dot(normed_own, w_cross[...]) + b_cross[...]
    modules.append(low(high(normed_own) * crossed))
    counts = jnp.sum(high(counted[...]), axis=1, keepdims=True)
    counts = jnp.maximum(counts, 1.0)
    seg_sums = dot(counted[:, :half_keys], normed_a[...]) + dot(counted[:, half_keys:], normed_b[...])
    seg_mean = low(seg_sums / counts)
    picked = lax.broadcasted_iota(jnp.int32, (LANES, 16), 0) - HEAD_DIM
    picked = (picked == lax.broadcasted_iota(jnp.int32, (LANES, 16), 1)) & (picked < SEGS)
    own_member = 1.0 - dot(q_aug[:, :LANES], low(jnp.where(picked, 1.0, 0.0)))
    own_lane = lax.broadcasted_iota(jnp.int32, (own_rows, 16), 1)
    own_member = low(jnp.where(own_lane < SEGS, own_member, 0.0))
    mixed = low(dot(own_member, seg_mean))
    modules.append(low(dot(mixed, w_mix[...])))
    first = high(tokens[...])
    for i in range(4):
        first = first + dot(modules[i], w_ens1[i * D : (i + 1) * D, :])
    unit_two, scale_two = unit_rows(first)
    normed_two = low(unit_two * gain_two[...])
    inner = dot(normed_two, w_up[...]) + b_up[...]
    cdf = 0.5 * (1.0 + lax.erf(inner * 0.7071067811865476))
    active = low(inner * cdf)
    slope = cdf + inner * jnp.exp(-0.5 * inner * inner) * 0.3989422804014327
    out_rows[...] = first + (dot(active, w_ens2[:FF, :]) + dot(normed_two, w_ens2[FF:, :]))

    core, y_bit, x_bit, z_bit = bits_of(me_ref)
    orders = (y_bit * 4 + x_bit * 2 + z_bit, x_bit * 4 + y_bit * 2 + z_bit)
    block = payload.shape[0] // 32
    place = [0]

    def put(grad):
        middle = grad.shape[0] // 2
        for i in range(middle // block):
            n = place[0]
            place[0] = n + 1
            spot = (n // 8) * 8 + ((n % 8) ^ orders[n // 8])
            for side in range(2):
                start = pl.multiple_of(((side ^ core) * 16 + spot) * block, block)
                first = side * middle + i * block
                payload[pl.ds(start, block), :] = low(grad[first : first + block])

    e2 = cot[...]
    put(dot_tn(active, e2))
    put(dot_tn(normed_two, e2))
    d_inner = low(dot_nt(e2, w_ens2[:FF, :]) * slope)
    b_up_grad = jnp.sum(high(d_inner), axis=0, keepdims=True)
    grad_up = dot_tn(normed_two, d_inner)
    for i in range(FF // D):
        put(grad_up[:, i * D : (i + 1) * D])
    d_norm2 = dot_nt(e2, w_ens2[FF:, :]) + dot_nt(d_inner, w_up[...])
    d_first = high(e2) + norm_back(d_norm2, unit_two, scale_two, gain_two[...])
    d_first_out[...] = d_first
    e1 = low(d_first)
    d_modules = []
    for i in range(4):
        put(dot_tn(modules[i], e1))
        d_modules.append(low(dot_nt(e1, w_ens1[i * D : (i + 1) * D, :])))
    out_grads = []
    for g in range(2):
        lanes = slice(g * 256, (g + 1) * 256)
        out_grads.append(dot_tn(att_low[:, lanes], d_modules[g]))
        grad_att[:, lanes] = low(dot_nt(d_modules[g], wo_pad[lanes, :]))
    put(narrow_rows(jnp.concatenate(out_grads, axis=0)))
    d_cross = low(high(d_modules[2]) * high(normed_own))
    put(dot_tn(normed_own, d_cross))
    put(dot_tn(mixed, d_modules[3]))
    dn_own[...] = high(d_modules[2]) * crossed + dot_nt(d_cross, w_cross[...])
    d_mixed = dot_nt(d_modules[3], w_mix[...])
    mixed_up = low(d_mixed)
    mixed_down = low(d_mixed - high(mixed_up))
    seg_grad_out[...] = (dot_tn(own_member, mixed_up) + dot_tn(own_member, mixed_down)) / counts
    vectors[...] = jnp.zeros_like(vectors)
    for i in range(FF // D):
        vectors[i : i + 1, :] = b_up_grad[:, i * D : (i + 1) * D]
    vectors[4:5, :] = jnp.sum(high(d_cross), axis=0, keepdims=True)
    vectors[5:6, :] = jnp.sum(d_norm2 * unit_two, axis=0, keepdims=True)

    d_att = high(grad_att[...])
    delta = head_sums(heads16, d_att * att)
    delta_out[...] = delta
    p_self = jnp.where(own_real, 0.0, jnp.exp(self_scores - lse_out[...]))
    dp_self = head_sums(heads16, d_att * high(v_own))
    pself_out[...] = low(p_self)
    dself_out[...] = low(p_self * (dp_self - delta))


def head_kernel(
    own_rows, h,
    q_aug, k_a, k_b, v_a, v_b, kt_a, kt_b, grad_att, lse, delta, pself, dself, after_one, after_two,
    dk_out, dv_out, dq_out,
):
    half_keys = 2 * own_rows
    row16 = lax.broadcasted_iota(jnp.int32, (16, LANES), 0)
    spread = low(jnp.where(row16 == h, 1.0, 0.0))
    lanes = slice(h * LANES, (h + 1) * LANES)
    rows_h = slice(h * HEAD_DIM, (h + 1) * HEAD_DIM)
    q_h = q_aug[:, lanes]
    g_h = grad_att[:, lanes]
    lse_h = lse[h : h + 1, :]
    delta_h = delta[h : h + 1, :]
    acc = high(dself[h : h + 1, :]) * high(kt_a[rows_h, :own_rows])
    for c, (k_half, v_half, kt_half) in enumerate(((k_a, v_a, kt_a), (k_b, v_b, kt_b))):
        at = slice(c * half_keys, (c + 1) * half_keys)
        p = jnp.exp(dot_nt(k_half[:, lanes], q_h) - lse_h)
        ds = low(p * (dot_nt(v_half[:, lanes], g_h) - delta_h))
        dv = dot(low(p), g_h)
        dk = dot(ds, q_h)
        if c == 0:
            dk_self = dot_tn(dself[...], spread) * high(q_h)
            dv_self = dot_tn(pself[...], spread) * high(g_h)
            dk_out[:own_rows, :] = low(dk[:own_rows] + dk_self)
            dv_out[:own_rows, :] = low(dv[:own_rows] + dv_self)
            dk_out[own_rows:half_keys, :] = low(dk[own_rows:])
            dv_out[own_rows:half_keys, :] = low(dv[own_rows:])
        else:
            dk_out[at, :] = low(dk)
            dv_out[at, :] = low(dv)
        acc = acc + dot(kt_half[rows_h, :], ds)
    dq_out[...] = low(acc * 0.125)


def rows_kernel(
    own_rows,
    dk0, dk1, dk2, dk3, dv0, dv1, dv2, dv3, dq0, dq1, dq2, dq3, after, normed_a, normed_b, counted, seg_grad, dn_own,
    gain_one, wq, wk_pad, wv_pad, vectors,
    out, dq_out,
    dn,
):
    half_keys = 2 * own_rows
    dq = jnp.concatenate([high(part[...]) for part in (dq0, dq1, dq2, dq3)], axis=0)
    dq_rows = low(dq.T)
    dq_out[...] = dq_rows
    dk_pairs = [jnp.concatenate([dk0[...], dk1[...]], axis=1), jnp.concatenate([dk2[...], dk3[...]], axis=1)]
    dv_pairs = [jnp.concatenate([dv0[...], dv1[...]], axis=1), jnp.concatenate([dv2[...], dv3[...]], axis=1)]
    up = low(seg_grad[...])
    down = low(seg_grad[...] - high(up))
    for c in range(2):
        at = slice(c * half_keys, (c + 1) * half_keys)
        mixing = dot_tn(counted[:, at], up) + dot_tn(counted[:, at], down)
        dn[at, :] = mixing + (
            dot_nt(dk_pairs[0][at, :], wk_pad[:, :256])
            + dot_nt(dk_pairs[1][at, :], wk_pad[:, 256:])
            + dot_nt(dv_pairs[0][at, :], wv_pad[:, :256])
            + dot_nt(dv_pairs[1][at, :], wv_pad[:, 256:])
        )
    dn[:own_rows, :] = dn[:own_rows, :] + (dot_nt(dq_rows, wq[...]) + dn_own[...])
    gain_grad = jnp.sum(dn[:half_keys, :] * high(normed_a[...]), axis=0, keepdims=True)
    gain_grad += jnp.sum(dn[half_keys:, :] * high(normed_b[...]), axis=0, keepdims=True)
    gain_grad = gain_grad / gain_one[...]
    count = out.shape[0] // 2
    for step in range(4):
        at = (step % 2) * count + (step // 2) * own_rows
        out[at : at + own_rows, :] = low(dn[step * own_rows : (step + 1) * own_rows, :])
    tail = lax.broadcasted_iota(jnp.int32, (16, D), 0)
    row = jnp.where(tail == 6, gain_grad, vectors[...])
    out[count - 16 : count, :] = low(row)
    out[2 * count - 16 :, :] = low(row)


def weights_kernel(
    own_rows,
    me_ref,
    dk0, dk1, dk2, dk3, dv0, dv1, dv2, dv3, dq_rows, normed_ta, normed_tb, after,
    out,
):
    half_keys = 2 * own_rows

    def key_grad(parts):
        pairs = [jnp.concatenate([parts[i][...], parts[i + 1][...]], axis=1) for i in (0, 2)]
        return narrow(
            jnp.concatenate(
                [
                    dot(normed_ta[...], pair[:half_keys]) + dot(normed_tb[...], pair[half_keys:])
                    for pair in pairs
                ],
                axis=1,
            )
        )

    core, y_bit, x_bit, _ = bits_of(me_ref)
    order = core * 4 + y_bit * 2 + x_bit
    part = D // 8
    for i, grad in enumerate(
        (
            dot(normed_ta[:, :own_rows], dq_rows[...]),
            key_grad((dk0, dk1, dk2, dk3)),
            key_grad((dv0, dv1, dv2, dv3)),
        )
    ):
        for n in range(8):
            at = ((n ^ order) * 3 + i) * part
            out[pl.ds(pl.multiple_of(at, part), part), :] = low(grad[n * part : (n + 1) * part])


def finish_kernel(mine, other, tokens, d_first, gain_one, after, grad_tokens, done):
    unit, scale = unit_rows(high(tokens[...]))
    total = high(mine[...]) + high(other[...])
    grad_tokens[...] = d_first[...] + norm_back(total, unit, scale, gain_one[...])
    done[...] = after[:16, :]


def unpack_kernel(me_ref, mine, other, after, attn_out, cross, mix, ens1, up, ens2):
    core, y_bit, x_bit, z_bit = bits_of(me_ref)
    orders = (y_bit * 4 + x_bit * 2 + z_bit, x_bit * 4 + y_bit * 2 + z_bit)
    block = mine.shape[0] // 16
    every = slice(None)
    jobs = [(ens2, 0, FF, every), (ens2, FF, D, every)]
    jobs += [(up, 0, D, slice(i * D, (i + 1) * D)) for i in range(FF // D)]
    jobs += [(ens1, i * D, D, every) for i in range(4)]
    jobs += [(attn_out, 0, D, every), (cross, 0, D, every), (mix, 0, D, every)]
    n = 0
    for to, first, count, columns in jobs:
        for i in range(count // 2 // block):
            spot = (n // 8) * 8 + ((n % 8) ^ orders[n // 8])
            n += 1
            for side, source in ((core, mine), (1 - core, other)):
                at = pl.multiple_of(first + side * (count // 2) + i * block, block)
                value = source[pl.ds(pl.multiple_of(spot * block, block), block), :]
                to[pl.ds(at, block), columns] = high(value)


def unpack_small_kernel(
    me_ref, mine, other, vec, gain_one, query, key, value, b_cross, gain_two, b_up
):
    core, y_bit, x_bit, _ = bits_of(me_ref)
    order = y_bit * 2 + x_bit
    part = D // 8
    for side, source in ((core, mine), (1 - core, other)):
        for n in range(4):
            for i, to in enumerate((query, key, value)):
                at = pl.multiple_of((n ^ order) * 3 * part + i * part, part)
                here = pl.ds(pl.multiple_of((side * 4 + n) * part, part), part)
                to[here, :] = high(source[pl.ds(at, part), :])
    wide = high(vec[...])
    for i in range(FF // D):
        b_up[:, i * D : (i + 1) * D] = wide[i : i + 1]
    b_cross[...] = wide[4:5]
    gain_two[...] = wide[5:6]
    gain_one[...] = wide[6:7]


def swap(value, axis, count, step):
    return lax.ppermute(value, axis, [(i, i ^ step) for i in range(count)])


def bits_of(me_ref):
    module, batch = me_ref[0], me_ref[1]
    return module & 1, (module >> 1) & 1, batch & 1, (batch >> 1) & 1


def sum_kernel(jobs, afters, *refs):
    inputs, outs = refs[: 2 * len(jobs)], refs[2 * len(jobs) + afters :]
    o = 0
    for j, cuts in enumerate(jobs):
        mine, got = inputs[2 * j], inputs[2 * j + 1]
        for spans in cuts:
            to = 0
            for first, count in spans:
                here = slice(first, first + count)
                outs[o][to : to + count, :] = added(mine[here, :], got[here, :])
                to += count
            o += 1


def join_kernel(jobs, afters, *refs):
    out = refs[-1]
    at = 0
    for ref in refs[:jobs]:
        count = ref.shape[0]
        out[at : at + count, :] = ref[...]
        at += count


def added(one, two):
    return low(high(one) + high(two))


def shards(
    n_batch,
    n_module,
    tokens,
    seg_lengths,
    valid,
    cotangent,
    gain_one,
    w_query,
    w_key,
    w_value,
    w_attn_out,
    w_cross,
    b_cross,
    w_mix,
    w_ens1,
    gain_two,
    w_up,
    b_up,
    w_ens2,
):
    module = lax.axis_index("module")
    batch = lax.axis_index("batch")
    own = tokens.shape[0]
    rows = valid.shape[0]
    me = jnp.stack([module, batch]).astype(jnp.int32)

    def by_core(value):
        return swap(value, "module", n_module, 1)

    def by_y(value):
        return swap(value, "module", n_module, 2)

    def by_batch(value, step):
        return swap(value, "batch", n_batch, step)

    from_core = by_core(tokens)
    from_y = by_y(tokens)
    square = ((D, D), BF)
    keys = 2 * own
    row = ((1, D), F32)
    gain_row, valid_row = gain_one.reshape(1, D), valid.reshape(1, rows)
    (token,) = call(start_kernel, [((8, LANES), F32)], [], "s", 4, 20)(me)
    (
        wq_pad, wk_pad, wv_pad, wo_pad, wk_t, wv_t, codes, real, counted,
        normed_a, normed_ta, q_aug, k_a, v_a, kt_a, vt_a,
    ) = call(
        functools.partial(first_kernel, own),
        [
            ((D, WIDE), BF), ((D, WIDE), BF), ((D, WIDE), BF), ((WIDE, D), BF), square, square,
            ((rows, LANES), BF), ((1, rows), F32), ((16, rows), BF),
            ((keys, D), BF), ((D, keys), BF), ((own, WIDE), BF), ((keys, WIDE), BF), ((keys, WIDE), BF),
            ((D, keys), BF), ((D, keys), BF),
        ],
        [], "ss" + "v" * 9, 16, 5,
    )(
        me, seg_lengths, token, from_core, tokens, valid_row, gain_row, w_query, w_key, w_value, w_attn_out
    )
    from_far = by_core(jnp.concatenate([from_y, normed_a[:16]], axis=0))
    (
        out_rows, d_first, dn_own, payload, vectors, normed_b, normed_tb, k_b, v_b, kt_b,
        grad_att, lse, delta, pself, dself, seg_grad,
    ) = call(
        functools.partial(forward_kernel, own),
        [
            ((own, D), F32), ((own, D), F32), ((own, D), F32), ((16 * D, D), BF), ((16, D), F32),
            ((keys, D), BF), ((D, keys), BF), ((keys, WIDE), BF), ((keys, WIDE), BF), ((D, keys), BF),
            ((own, WIDE), BF), ((16, own), F32), ((16, own), F32), ((16, own), BF), ((16, own), BF), ((16, D), F32),
        ],
        [pltpu.VMEM((D, keys), BF), pltpu.VMEM((rows, own), F32), pltpu.VMEM((WIDE, own), F32)],
        "s" + "v" * 28, 32, 18,
    )(
        me, from_y, from_far, codes, real, counted, tokens, cotangent, gain_row, wk_pad, wv_pad, wo_pad, wk_t, wv_t,
        w_cross, b_cross.reshape(1, D), w_mix, w_ens1, gain_two.reshape(1, D), w_up, b_up.reshape(1, FF), w_ens2,
        normed_a, normed_ta, q_aug, k_a, v_a, kt_a, vt_a,
    )

    def head(index, after_one, after_two):
        return call(
            functools.partial(head_kernel, own, index),
            [((rows, LANES), BF), ((rows, LANES), BF), ((HEAD_DIM, own), BF)],
            [], "v" * 14, 16, 3,
        )(
            q_aug, k_a, k_b, v_a, v_b, kt_a, kt_b, grad_att, lse, delta, pself, dself, after_one[:16], after_two[:16]
        )

    def sums(jobs, pairs, *after):
        outs = [((sum(count for _, count in spans), D), BF) for cuts in jobs for spans in cuts]
        args = [value for pair in pairs for value in pair] + list(after)
        body = functools.partial(sum_kernel, jobs, len(after))
        return call(body, outs, [], "v" * len(args), 8, 1)(*args)

    def joined(parts, *after):
        count = sum(part.shape[0] for part in parts)
        body = functools.partial(join_kernel, len(parts), len(after))
        args = list(parts) + list(after)
        return call(body, [((count, D), BF)], [], "v" * len(args), 8, 1)(*args)[0]

    size = payload.shape[0] // 8
    got = by_core(payload[4 * size :])
    dk0, dv0, dq0 = head(0, lse, lse)
    quarters = [[(i * size, size)] for i in range(4)]
    a, a_send, b, b_send = sums([quarters], [(payload, got)])
    dk1, dv1, dq1 = head(1, a, dq0)
    dk2, dv2, dq2 = head(2, b, dq1)
    a_got, b_got = by_y(a_send), by_batch(b_send, 1)
    halves = [[(0, size // 2)], [(size // 2, size // 2)]]
    a, a_send, b, b_send = sums([halves] * 2, [(a, a_got), (b, b_got)])
    dk3, dv3, dq3 = head(3, a, dq2)
    a_got, b_got = by_batch(a_send, 1), by_y(b_send)
    eighth = size // 4
    eighths = [[(0, eighth)], [(eighth, eighth)]]
    a, a_send, b, b_send = sums([eighths] * 2, [(a, a_got), (b, b_got)])
    ab, ab_send = joined([a, b]), joined([a_send, b_send])
    ab_got = by_batch(ab_send, 2)

    steps = [1 << place for place in range(1, n_batch.bit_length() - 1)]
    part = D // 8
    count = 2 * own + 16
    shared, dq_rows = call(
        functools.partial(rows_kernel, own),
        [((2 * count, D), BF), ((own, D), BF)],
        [pltpu.VMEM((rows, D), F32)],
        "v" * 23, 16, 3,
    )(
        dk0, dk1, dk2, dk3, dv0, dv1, dv2, dv3, dq0, dq1, dq2, dq3, ab, normed_a, normed_b, counted, seg_grad, dn_own,
        gain_row, w_query, wk_pad, wv_pad, vectors,
    )
    shared_got = by_core(shared[count:])
    every = [[[(0, 2 * eighth)]]]
    (ab,) = sums(every, [(ab, ab_got)], shared)
    ab_got = by_batch(ab, steps[1]) if len(steps) > 1 else ab
    (q,) = call(functools.partial(weights_kernel, own), [((24 * part, D), BF)], [], "s" + "v" * 12, 16, 3)(
        me, dk0, dk1, dk2, dk3, dv0, dv1, dv2, dv3, dq_rows, normed_ta, normed_tb, ab
    )
    q_got = by_core(q[12 * part :])
    dn, dn_send, vec = sums([[[(0, own)], [(own, own)], [(2 * own, 16)]]], [(shared, shared_got)], q)
    q, q_send = sums([[[(0, 6 * part)], [(6 * part, 6 * part)]]], [(q, q_got)], vec)
    q_got = by_y(joined([q_send, vec]))
    dn_got = by_y(dn_send)
    six = 6 * part
    q, q_send = sums(
        [[[(0, 3 * part), (six, 16)], [(3 * part, 3 * part + 16)]]], [(joined([q, vec]), q_got)]
    )
    q_got = by_batch(q_send, 1)
    for i in range(1, len(steps)):
        (ab,) = sums(every, [(ab, ab_got)], q)
        if i + 1 < len(steps):
            ab_got = by_batch(ab, steps[i + 1])
    ab_got = by_batch(ab, steps[0])
    whole = [[[(0, 3 * part + 16)]]]
    (q,) = sums(whole, [(q, q_got)], ab)
    q_got = by_batch(q, steps[0])
    a = joined([ab[:eighth], ab_got[:eighth]], q)
    b = joined([ab[eighth:], ab_got[eighth:]], q)
    a_got, b_got = by_batch(a, 1), by_y(b)
    for step in steps[1:]:
        (q,) = sums(whole, [(q, q_got)], a, b)
        q_got = by_batch(q, step)
    grad_tokens, done = call(
        finish_kernel, [((own, D), F32), ((16, D), BF)], [], "v" * 6, 16, 2
    )(dn, dn_got, tokens, d_first, gain_row, q)
    a = joined([a, a_got], done)
    b = joined([b, b_got], done)
    a_got, b_got = by_y(a), by_batch(b, 1)
    (q,) = sums(whole, [(q, q_got)], a, b)
    q, vec = q[: 3 * part], q[3 * part :]
    q_got = by_batch(q, 1)
    q = joined([q, q_got])
    q_got = by_y(q)
    big = joined([a, a_got, b, b_got], q)
    big_got = by_core(big)
    q = joined([q, q_got], big)
    q_got = by_core(q)
    wide = ((D, D), F32)
    attn_out, cross, mix, ens1, up, ens2 = call(
        unpack_kernel,
        [wide, wide, wide, ((4 * D, D), F32), ((D, FF), F32), ((FF + D, D), F32)],
        [], "svvv", 16, 3,
    )(me, big, big_got, q)
    gain_one_g, query, key, value, b_cross_g, gain_two_g, b_up_g = call(
        unpack_small_kernel, [row, wide, wide, wide, row, row, ((1, FF), F32)], [], "svvv", 16, 1
    )(me, q, q_got, vec)
    return (
        out_rows, grad_tokens, gain_one_g.reshape(D), query, key, value, attn_out, cross, b_cross_g.reshape(D), mix,
        ens1, gain_two_g.reshape(D), up, b_up_g.reshape(FF), ens2,
    )


def solution(mesh):
    rows = P(("batch", "module"), None)
    in_specs = (rows, P("batch", None), P("batch"), rows) + (P(),) * 13
    out_specs = (rows, rows) + (P(),) * 13
    body = functools.partial(shards, mesh.shape["batch"], mesh.shape["module"])
    return jax.shard_map(body, mesh=mesh, in_specs=in_specs, out_specs=out_specs, check_vma=False)
```

```python
import functools

import jax
import jax.numpy as jnp
from jax import lax
from jax.experimental import pallas as pl
from jax.experimental.pallas import tpu as pltpu
from jax.sharding import PartitionSpec as P

D = 256
HEADS = 4
HEAD_DIM = 64
FF = 1024
SEGS = 8
LANES = 128
WIDE = HEADS * LANES
HUGE = -1e30
TALL = HEAD_DIM + 16
BF = jnp.bfloat16
F32 = jnp.float32
MIB = 1024 * 1024


def low(v):
    return v.astype(BF)


def high(v):
    return v.astype(F32)


def dot(a, b):
    return jnp.dot(a, b, preferred_element_type=F32)


def dot_nt(a, b):
    return lax.dot_general(a, b, (((1,), (1,)), ((), ())), preferred_element_type=F32)


def dot_tn(a, b):
    return lax.dot_general(a, b, (((0,), (0,)), ((), ())), preferred_element_type=F32)


def head_sums(selector, product):
    upper = low(product)
    lower = low(product - high(upper))
    return dot_nt(selector, upper) + dot_nt(selector, lower)


def unit_rows(values):
    center = values - jnp.mean(values, axis=1, keepdims=True)
    scale = lax.rsqrt(jnp.mean(center * center, axis=1, keepdims=True) + 1e-05)
    return center * scale, scale


def norm_back(grad, unit, scale, gain):
    scaled = grad * gain
    first_mean = jnp.mean(scaled, axis=1, keepdims=True)
    second_mean = jnp.mean(scaled * unit, axis=1, keepdims=True)
    return scale * (scaled - first_mean - unit * second_mean)


def call(body, outs, scratch, places, limit, microseconds):
    spaces = {"s": pltpu.SMEM, "v": pltpu.VMEM, "h": pltpu.HBM}
    return pl.pallas_call(
        body,
        out_shape=[jax.ShapeDtypeStruct(shape, kind) for shape, kind in outs],
        in_specs=[pl.BlockSpec(memory_space=spaces[place]) for place in places],
        out_specs=[pl.BlockSpec(memory_space=pltpu.VMEM)] * len(outs),
        scratch_shapes=list(scratch),
        compiler_params=pltpu.CompilerParams(vmem_limit_bytes=limit * MIB),
        cost_estimate=pl.CostEstimate(
            flops=microseconds * 10**9, bytes_accessed=0, transcendentals=0
        ),
    )


def widen(weight):
    rows = weight.shape[0]
    gap = jnp.zeros((rows, LANES - HEAD_DIM), weight.dtype)
    pieces = []
    for head in range(HEADS):
        pieces += [weight[:, head * HEAD_DIM : (head + 1) * HEAD_DIM], gap]
    return jnp.concatenate(pieces, axis=1)


def widen_rows(weight):
    gap = jnp.zeros((LANES - HEAD_DIM, weight.shape[1]), weight.dtype)
    pieces = []
    for head in range(HEADS):
        pieces += [weight[head * HEAD_DIM : (head + 1) * HEAD_DIM], gap]
    return jnp.concatenate(pieces, axis=0)


def narrow(wide):
    return jnp.concatenate(
        [wide[:, h * LANES : h * LANES + HEAD_DIM] for h in range(HEADS)], axis=1
    )


def narrow_rows(wide):
    return jnp.concatenate([wide[h * LANES : h * LANES + HEAD_DIM] for h in range(HEADS)], axis=0)


def segment_rows(seg_ref, first_place, count):
    spread = lax.broadcasted_iota(jnp.int32, (16, count), 0)
    places = lax.broadcasted_iota(jnp.int32, (16, count), 1) + first_place
    begin = jnp.zeros((16, count), jnp.int32)
    end = jnp.zeros((16, count), jnp.int32)
    edge = jnp.int32(0)
    for j in range(SEGS):
        begin = jnp.where(spread == j, edge, begin)
        edge = edge + seg_ref[0, j]
        end = jnp.where(spread == j, edge, end)
    return spread, (places >= begin) & (places < end)


def head_selector():
    rows = lax.broadcasted_iota(jnp.int32, (16, WIDE), 0)
    lanes = lax.broadcasted_iota(jnp.int32, (16, WIDE), 1)
    return low(jnp.where((lanes >> 7) == rows, 1.0, 0.0))


def start_kernel(me_ref, spot):
    rows = lax.broadcasted_iota(jnp.int32, spot.shape, 0)
    spot[...] = jnp.where(rows == 0, me_ref[0], me_ref[1])


def project(rows_in, gain, code, wk_pad, wv_pad, wk_t, wv_t, at, normed, normed_t, k_aug, v_pad, kt, vt):
    count = rows_in.shape[0]
    unit, _ = unit_rows(high(rows_in))
    value = low(unit * gain)
    flipped = value.T
    normed[at : at + count, :] = value
    normed_t[:, at : at + count] = flipped
    wide = low(dot(value, wk_pad))
    k_aug[at : at + count, :] = wide + jnp.concatenate([code] * HEADS, axis=1)
    v_lane = lax.broadcasted_iota(jnp.int32, (1, WIDE), 1) & (LANES - 1)
    v_ones = jnp.where((v_lane >= HEAD_DIM) & (v_lane < HEAD_DIM + 3), 1.0, 0.0)
    v_pad[at : at + count, :] = low(dot(value, wv_pad) + v_ones)
    kt[:, at : at + count] = low(dot(wk_t, flipped))
    turned = low(dot(wv_t, flipped))
    for h in range(HEADS):
        vt[h * TALL : h * TALL + HEAD_DIM, at : at + count] = turned[h * HEAD_DIM : (h + 1) * HEAD_DIM]
        vt[h * TALL + HEAD_DIM : (h + 1) * TALL, at : at + count] = jnp.ones((16, count), BF)


def raw_attention(q_aug, k_aug, vt, part):
    for h in range(HEADS):
        lanes = slice(h * LANES, (h + 1) * LANES)
        tall = slice(h * TALL, (h + 1) * TALL)
        p = low(jnp.exp(dot_nt(k_aug[:, lanes], q_aug[:, lanes])))
        part[tall, :] = dot(vt[tall, :], p)


def exact_attention(q_aug, halves, self_rows, vt_own, scores, o_t, lse_out):
    for h in range(HEADS):
        lanes = slice(h * LANES, (h + 1) * LANES)
        q_h = q_aug[:, lanes]
        top = self_h = self_rows[h : h + 1]
        at = 0
        for k_half, _ in halves:
            count = k_half.shape[0]
            scores[at : at + count, :] = dot_nt(k_half[:, lanes], q_h)
            top = jnp.maximum(top, jnp.max(scores[at : at + count, :], axis=0, keepdims=True))
            at += count
        p_self = jnp.exp(self_h - top)
        total = p_self
        acc = high(low(p_self)) * high(vt_own[h * TALL : h * TALL + HEAD_DIM, :])
        at = 0
        for k_half, vt_half in halves:
            count = k_half.shape[0]
            p = jnp.exp(scores[at : at + count, :] - top)
            total = total + jnp.sum(p, axis=0, keepdims=True)
            acc = acc + dot(vt_half[h * TALL : h * TALL + HEAD_DIM, :], low(p))
            at += count
        o_t[h * LANES : h * LANES + HEAD_DIM, :] = acc / total
        lse_out[h : h + 1, :] = top + jnp.log(total)


def placed(rows16, first):
    upper = low(rows16)
    rest = rows16 - high(upper)
    middle = low(rest)
    parts = (upper, middle, low(rest - high(middle)))
    rows = lax.broadcasted_iota(jnp.int32, (16, WIDE), 0)
    lanes = lax.broadcasted_iota(jnp.int32, (16, WIDE), 1)
    total = 0.0
    for i, piece in enumerate(parts):
        picked = ((lanes >> 7) == rows) & ((lanes & (LANES - 1)) == first + i)
        total = total + dot_tn(piece, low(jnp.where(picked, 1.0, 0.0)))
    return low(total)


def lane_codes(rows_code):
    picked = lax.broadcasted_iota(jnp.int32, (16, LANES), 1) - HEAD_DIM
    picked = (picked == lax.broadcasted_iota(jnp.int32, (16, LANES), 0)) & (picked <= SEGS + 3)
    return low(dot_tn(low(rows_code), low(jnp.where(picked, 1.0, 0.0))))


def first_kernel(
    own_rows,
    spot, seg, core_rows, tokens, valid, gain_one, wq, wk, wv, wo,
    wq_pad, wk_pad, wv_pad, wo_pad, wk_t, wv_t, codes, real, counted,
    normed, normed_t, q_aug, k_aug, v_pad, kt, vt, part,
):
    me = jnp.max(spot[0:1, :])
    for step in range(4):
        at = pl.multiple_of((me ^ step) * own_rows, own_rows)
        spread, inside = segment_rows(seg, at, own_rows)
        ok = valid[:, pl.ds(at, own_rows)] > 0
        code = jnp.where(inside, HUGE, 0.0)
        code = jnp.where(spread == SEGS, jnp.where(ok, 0.0, HUGE), code)
        code = jnp.where(spread > SEGS, 1.0, code)
        codes[step * own_rows : (step + 1) * own_rows, :] = lane_codes(code)
        real[:, step * own_rows : (step + 1) * own_rows] = jnp.where(ok, 1.0, 0.0)
        counted[:, step * own_rows : (step + 1) * own_rows] = low(jnp.where(inside & ok, 1.0, 0.0))
    wq_pad[...] = low(widen(high(wq[...])))
    wk_pad[...] = low(widen(high(wk[...])))
    wv_pad[...] = low(widen(high(wv[...])))
    wo_pad[...] = low(widen_rows(high(wo[...])))
    wk_t[...] = wk[...].T
    wv_t[...] = wv[...].T
    gain = gain_one[...]
    for step, rows_in in enumerate((tokens, core_rows)):
        at = step * own_rows
        project(
            rows_in[...], gain, codes[at : at + own_rows, :], wk_pad[...], wv_pad[...], wk_t[...], wv_t[...], at,
            normed, normed_t, k_aug, v_pad, kt, vt,
        )
    spread, inside = segment_rows(seg, pl.multiple_of(me * own_rows, own_rows), own_rows)
    own_code = lane_codes(jnp.where(inside | (spread > SEGS), 0.0, 1.0))
    scaled = low(dot(normed[:own_rows, :], wq_pad[...]) * 0.125)
    q_aug[...] = scaled + jnp.concatenate([own_code] * HEADS, axis=1)
    raw_attention(q_aug, k_aug, vt, part)


def forward_kernel(
    own_rows,
    spot, y_rows, far_rows, codes, real, counted, tokens, cot,
    gain_one, wk_pad, wv_pad, wo_pad, wk_t, wv_t,
    w_cross, b_cross, w_mix, w_ens1, gain_two, w_up, b_up, w_ens2,
    normed_a, normed_ta, q_aug, k_a, v_a, kt_a, vt_a, part_a,
    out_rows, d_first_out, dn_own, payload, vectors,
    normed_b, normed_tb, k_b, v_b, kt_b,
    q_back, grad_att, pself_out, dself_out, seg_grad_out,
    vt_b, part_b, scores, o_t, lse_out,
):
    gain = gain_one[...]
    for step, rows_in in enumerate((y_rows[...], far_rows[:own_rows, :])):
        at = step * own_rows
        project(
            rows_in, gain, codes[at + 2 * own_rows : at + 3 * own_rows, :],
            wk_pad[...], wv_pad[...], wk_t[...], wv_t[...], at,
            normed_b, normed_tb, k_b, v_b, kt_b, vt_b,
        )
    normed_own = normed_a[:own_rows, :]
    heads16 = head_selector()
    lanes_own = lax.broadcasted_iota(jnp.int32, (own_rows, WIDE), 1) & (LANES - 1)
    v_own = v_a[:own_rows, :]
    self_product = jnp.where(
        lanes_own < HEAD_DIM, high(q_aug[...]) * high(k_a[:own_rows, :]), 0.0
    )
    self_scores = head_sums(heads16, self_product)
    own_real = real[:, :own_rows] > 0
    o_t[...] = jnp.zeros_like(o_t)
    lse_out[...] = jnp.zeros_like(lse_out)
    half_keys = 2 * own_rows
    raw_attention(q_aug, k_b, vt_b, part_b)
    vt_own = vt_a[:, :own_rows]
    smallest, largest = jnp.inf, -jnp.inf
    for h in range(HEADS):
        p_self = jnp.where(own_real, 0.0, jnp.exp(self_scores[h : h + 1]))
        both = part_a[h * TALL : (h + 1) * TALL, :] + part_b[h * TALL : (h + 1) * TALL, :]
        total = both[HEAD_DIM : HEAD_DIM + 1] + p_self
        acc = both[:HEAD_DIM] + high(low(p_self)) * high(vt_own[h * TALL : h * TALL + HEAD_DIM])
        o_t[h * LANES : h * LANES + HEAD_DIM, :] = acc / total
        lse_out[h : h + 1, :] = jnp.log(total)
        smallest = jnp.minimum(smallest, total)
        largest = jnp.maximum(largest, total)
    fits = (jnp.min(smallest) > 1e-25) & (jnp.max(largest) < 1e30)

    @pl.when(jnp.logical_not(fits))
    def _():
        self_rows = jnp.where(own_real, HUGE, self_scores)
        exact_attention(q_aug, ((k_a, vt_a), (k_b, vt_b)), self_rows, vt_own, scores, o_t, lse_out)

    q_back[...] = q_aug[...] + placed(-lse_out[...], HEAD_DIM + SEGS + 1)
    att = o_t[...].T
    att_low = low(att)

    modules = []
    for g in range(2):
        lanes = slice(g * 256, (g + 1) * 256)
        modules.append(low(dot(att_low[:, lanes], wo_pad[lanes, :])))
    crossed = dot(normed_own, w_cross[...]) + b_cross[...]
    modules.append(low(high(normed_own) * crossed))
    counts = jnp.sum(high(counted[...]), axis=1, keepdims=True)
    counts = jnp.maximum(counts, 1.0)
    seg_sums = dot(counted[:, :half_keys], normed_a[...]) + dot(counted[:, half_keys:], normed_b[...])
    seg_mean = low(seg_sums / counts)
    picked = lax.broadcasted_iota(jnp.int32, (LANES, 16), 0) - HEAD_DIM
    picked = (picked == lax.broadcasted_iota(jnp.int32, (LANES, 16), 1)) & (picked < SEGS)
    own_member = 1.0 - dot(q_aug[:, :LANES], low(jnp.where(picked, 1.0, 0.0)))
    own_lane = lax.broadcasted_iota(jnp.int32, (own_rows, 16), 1)
    own_member = low(jnp.where(own_lane < SEGS, own_member, 0.0))
    mixed = low(dot(own_member, seg_mean))
    modules.append(low(dot(mixed, w_mix[...])))
    first = high(tokens[...])
    for i in range(4):
        first = first + dot(modules[i], w_ens1[i * D : (i + 1) * D, :])
    unit_two, scale_two = unit_rows(first)
    normed_two = low(unit_two * gain_two[...])
    inner = dot(normed_two, w_up[...]) + b_up[...]
    cdf = 0.5 * (1.0 + lax.erf(inner * 0.7071067811865476))
    active = low(inner * cdf)
    slope = cdf + inner * jnp.exp(-0.5 * inner * inner) * 0.3989422804014327
    out_rows[...] = first + (dot(active, w_ens2[:FF, :]) + dot(normed_two, w_ens2[FF:, :]))

    core, y_bit, x_bit, z_bit = bits_of(spot)
    order = y_bit * 8 + x_bit * 4 + z_bit * 2
    block = payload.shape[0] // 32
    place = [0]

    def put(grad):
        middle = grad.shape[0] // 2
        for i in range(middle // block):
            n = place[0]
            place[0] = n + 1
            place_at = n ^ order
            for side in range(2):
                start = pl.multiple_of(((side ^ core) * 16 + place_at) * block, block)
                first = side * middle + i * block
                payload[pl.ds(start, block), :] = low(grad[first : first + block])

    e2 = cot[...]
    put(dot_tn(active, e2))
    put(dot_tn(normed_two, e2))
    d_inner = low(dot_nt(e2, w_ens2[:FF, :]) * slope)
    b_up_grad = jnp.sum(high(d_inner), axis=0, keepdims=True)
    grad_up = dot_tn(normed_two, d_inner)
    for i in range(FF // D):
        put(grad_up[:, i * D : (i + 1) * D])
    d_norm2 = dot_nt(e2, w_ens2[FF:, :]) + dot_nt(d_inner, w_up[...])
    d_first = high(e2) + norm_back(d_norm2, unit_two, scale_two, gain_two[...])
    d_first_out[...] = d_first
    e1 = low(d_first)
    d_modules = []
    for i in range(4):
        put(dot_tn(modules[i], e1))
        d_modules.append(low(dot_nt(e1, w_ens1[i * D : (i + 1) * D, :])))
    out_grads = []
    for g in range(2):
        lanes = slice(g * 256, (g + 1) * 256)
        out_grads.append(dot_tn(att_low[:, lanes], d_modules[g]))
        grad_att[:, lanes] = low(dot_nt(d_modules[g], wo_pad[lanes, :]))
    put(narrow_rows(jnp.concatenate(out_grads, axis=0)))
    d_cross = low(high(d_modules[2]) * high(normed_own))
    put(dot_tn(normed_own, d_cross))
    put(dot_tn(mixed, d_modules[3]))
    dn_own[...] = high(d_modules[2]) * crossed + dot_nt(d_cross, w_cross[...])
    d_mixed = dot_nt(d_modules[3], w_mix[...])
    mixed_up = low(d_mixed)
    mixed_down = low(d_mixed - high(mixed_up))
    seg_grad_out[...] = (dot_tn(own_member, mixed_up) + dot_tn(own_member, mixed_down)) / counts
    vectors[...] = jnp.zeros_like(vectors)
    for i in range(FF // D):
        vectors[i : i + 1, :] = b_up_grad[:, i * D : (i + 1) * D]
    vectors[4:5, :] = jnp.sum(high(d_cross), axis=0, keepdims=True)
    vectors[5:6, :] = jnp.sum(d_norm2 * unit_two, axis=0, keepdims=True)

    d_att = high(grad_att[...])
    delta = head_sums(heads16, d_att * att)
    grad_att[...] = grad_att[...] + placed(-delta, HEAD_DIM)
    p_self = jnp.where(own_real, 0.0, jnp.exp(self_scores - lse_out[...]))
    dp_self = head_sums(heads16, d_att * high(v_own))
    pself_out[...] = low(p_self)
    dself_out[...] = low(p_self * (dp_self - delta))


def head_kernel(
    own_rows, h,
    q_back, k_a, k_b, v_a, v_b, kt_a, kt_b, grad_att, pself, dself, after_one, after_two,
    dk_out, dv_out, dq_out,
):
    half_keys = 2 * own_rows
    row16 = lax.broadcasted_iota(jnp.int32, (16, LANES), 0)
    spread = low(jnp.where(row16 == h, 1.0, 0.0))
    lanes = slice(h * LANES, (h + 1) * LANES)
    rows_h = slice(h * HEAD_DIM, (h + 1) * HEAD_DIM)
    q_h = q_back[:, lanes]
    g_h = grad_att[:, lanes]
    acc = high(dself[h : h + 1, :]) * high(kt_a[rows_h, :own_rows])
    for c, (k_half, v_half, kt_half) in enumerate(((k_a, v_a, kt_a), (k_b, v_b, kt_b))):
        at = slice(c * half_keys, (c + 1) * half_keys)
        p = jnp.exp(dot_nt(k_half[:, lanes], q_h))
        ds = low(p * dot_nt(v_half[:, lanes], g_h))
        dv = dot(low(p), g_h)
        dk = dot(ds, q_h)
        if c == 0:
            dk_self = dot_tn(dself[...], spread) * high(q_h)
            dv_self = dot_tn(pself[...], spread) * high(g_h)
            dk_out[:own_rows, :] = low(dk[:own_rows] + dk_self)
            dv_out[:own_rows, :] = low(dv[:own_rows] + dv_self)
            dk_out[own_rows:half_keys, :] = low(dk[own_rows:])
            dv_out[own_rows:half_keys, :] = low(dv[own_rows:])
        else:
            dk_out[at, :] = low(dk)
            dv_out[at, :] = low(dv)
        acc = acc + dot(kt_half[rows_h, :], ds)
    dq_out[...] = low(acc * 0.125)


def rows_kernel(
    own_rows,
    dk0, dk1, dk2, dk3, dv0, dv1, dv2, dv3, dq0, dq1, dq2, dq3, after, normed_a, normed_b, counted, seg_grad, dn_own,
    gain_one, wq, wk_pad, wv_pad, vectors,
    out, dq_out,
    dn,
):
    half_keys = 2 * own_rows
    dq = jnp.concatenate([high(part[...]) for part in (dq0, dq1, dq2, dq3)], axis=0)
    dq_rows = low(dq.T)
    dq_out[...] = dq_rows
    dk_pairs = [jnp.concatenate([dk0[...], dk1[...]], axis=1), jnp.concatenate([dk2[...], dk3[...]], axis=1)]
    dv_pairs = [jnp.concatenate([dv0[...], dv1[...]], axis=1), jnp.concatenate([dv2[...], dv3[...]], axis=1)]
    up = low(seg_grad[...])
    down = low(seg_grad[...] - high(up))
    for c in range(2):
        at = slice(c * half_keys, (c + 1) * half_keys)
        mixing = dot_tn(counted[:, at], up) + dot_tn(counted[:, at], down)
        dn[at, :] = mixing + (
            dot_nt(dk_pairs[0][at, :], wk_pad[:, :256])
            + dot_nt(dk_pairs[1][at, :], wk_pad[:, 256:])
            + dot_nt(dv_pairs[0][at, :], wv_pad[:, :256])
            + dot_nt(dv_pairs[1][at, :], wv_pad[:, 256:])
        )
    dn[:own_rows, :] = dn[:own_rows, :] + (dot_nt(dq_rows, wq[...]) + dn_own[...])
    gain_grad = jnp.sum(dn[:half_keys, :] * high(normed_a[...]), axis=0, keepdims=True)
    gain_grad += jnp.sum(dn[half_keys:, :] * high(normed_b[...]), axis=0, keepdims=True)
    gain_grad = gain_grad / gain_one[...]
    count = out.shape[0] // 2
    for step in range(4):
        at = (step % 2) * count + (step // 2) * own_rows
        out[at : at + own_rows, :] = low(dn[step * own_rows : (step + 1) * own_rows, :])
    tail = lax.broadcasted_iota(jnp.int32, (16, D), 0)
    row = jnp.where(tail == 6, gain_grad, vectors[...])
    out[count - 16 : count, :] = low(row)
    out[2 * count - 16 :, :] = low(row)


def weights_kernel(
    own_rows,
    spot,
    dk0, dk1, dk2, dk3, dv0, dv1, dv2, dv3, dq_rows, normed_ta, normed_tb, after,
    out,
):
    half_keys = 2 * own_rows

    def key_grad(parts):
        pairs = [jnp.concatenate([parts[i][...], parts[i + 1][...]], axis=1) for i in (0, 2)]
        return narrow(
            jnp.concatenate(
                [
                    dot(normed_ta[...], pair[:half_keys]) + dot(normed_tb[...], pair[half_keys:])
                    for pair in pairs
                ],
                axis=1,
            )
        )

    core, y_bit, x_bit, _ = bits_of(spot)
    order = core * 4 + y_bit * 2 + x_bit
    part = D // 8
    for i, grad in enumerate(
        (
            dot(normed_ta[:, :own_rows], dq_rows[...]),
            key_grad((dk0, dk1, dk2, dk3)),
            key_grad((dv0, dv1, dv2, dv3)),
        )
    ):
        for n in range(8):
            at = ((n ^ order) * 3 + i) * part
            out[pl.ds(pl.multiple_of(at, part), part), :] = low(grad[n * part : (n + 1) * part])


def finish_kernel(mine, other, tokens, d_first, gain_one, after, grad_tokens, done):
    unit, scale = unit_rows(high(tokens[...]))
    total = high(mine[...]) + high(other[...])
    grad_tokens[...] = d_first[...] + norm_back(total, unit, scale, gain_one[...])
    done[...] = after[:16, :]


def unpack_kernel(spot, mine, other, attn_out, cross, mix, ens1, up, ens2, done):
    core, y_bit, x_bit, z_bit = bits_of(spot)
    order = y_bit * 8 + x_bit * 4 + z_bit * 2
    block = mine.shape[0] // 16
    every = slice(None)
    jobs = [(ens2, 0, FF, every), (ens2, FF, D, every)]
    jobs += [(up, 0, D, slice(i * D, (i + 1) * D)) for i in range(FF // D)]
    jobs += [(ens1, i * D, D, every) for i in range(4)]
    jobs += [(attn_out, 0, D, every), (cross, 0, D, every), (mix, 0, D, every)]
    n = 0
    for to, first, count, columns in jobs:
        for i in range(count // 2 // block):
            place_at = n ^ order
            n += 1
            for side, source in ((core, mine), (1 - core, other)):
                at = pl.multiple_of(first + side * (count // 2) + i * block, block)
                value = source[pl.ds(pl.multiple_of(place_at * block, block), block), :]
                to[pl.ds(at, block), columns] = high(value)
    done[...] = mine[:16, :]


def unpack_small_kernel(
    spot, mine, other, vec, after, gain_one, query, key, value, b_cross, gain_two, b_up
):
    core, y_bit, x_bit, _ = bits_of(spot)
    order = y_bit * 2 + x_bit
    part = D // 8
    for side, source in ((core, mine), (1 - core, other)):
        for n in range(4):
            for i, to in enumerate((query, key, value)):
                at = pl.multiple_of((n ^ order) * 3 * part + i * part, part)
                here = pl.ds(pl.multiple_of((side * 4 + n) * part, part), part)
                to[here, :] = high(source[pl.ds(at, part), :])
    wide = high(vec[...])
    for i in range(FF // D):
        b_up[:, i * D : (i + 1) * D] = wide[i : i + 1]
    b_cross[...] = wide[4:5]
    gain_two[...] = wide[5:6]
    gain_one[...] = wide[6:7]


def swap(value, axis, count, step):
    return lax.ppermute(value, axis, [(i, i ^ step) for i in range(count)])


def bits_of(spot):
    module, batch = jnp.max(spot[0:1, :]), jnp.max(spot[1:2, :])
    return module & 1, (module >> 1) & 1, batch & 1, (batch >> 1) & 1


def sum_kernel(counts, afters, *refs):
    inputs, outs = refs[: len(refs) - afters - len(counts)], refs[len(refs) - len(counts) :]
    at = 0
    for count, out in zip(counts, outs):
        total = high(inputs[0][at : at + count, :])
        for other in inputs[1:]:
            total = total + high(other[at : at + count, :])
        out[...] = low(total)
        at += count


def join_kernel(jobs, afters, *refs):
    out = refs[-1]
    at = 0
    for ref in refs[:jobs]:
        count = ref.shape[0]
        out[at : at + count, :] = ref[...]
        at += count


def added(one, two):
    return low(high(one) + high(two))


def shards(
    n_batch,
    n_module,
    tokens,
    seg_lengths,
    valid,
    cotangent,
    gain_one,
    w_query,
    w_key,
    w_value,
    w_attn_out,
    w_cross,
    b_cross,
    w_mix,
    w_ens1,
    gain_two,
    w_up,
    b_up,
    w_ens2,
):
    module = lax.axis_index("module")
    batch = lax.axis_index("batch")
    own = tokens.shape[0]
    rows = valid.shape[0]
    me = jnp.stack([module, batch]).astype(jnp.int32)

    def by_core(value):
        return swap(value, "module", n_module, 1)

    def by_y(value):
        return swap(value, "module", n_module, 2)

    def by_batch(value, step):
        return swap(value, "batch", n_batch, step)

    from_core = by_core(tokens)
    from_y = by_y(tokens)
    square = ((D, D), BF)
    keys = 2 * own
    row = ((1, D), F32)
    gain_row, valid_row = gain_one.reshape(1, D), valid.reshape(1, rows)
    (spot,) = call(start_kernel, [((8, LANES), jnp.int32)], [], "s", 4, 20)(me)
    (
        wq_pad, wk_pad, wv_pad, wo_pad, wk_t, wv_t, codes, real, counted,
        normed_a, normed_ta, q_aug, k_a, v_a, kt_a, vt_a, part_a,
    ) = call(
        functools.partial(first_kernel, own),
        [
            ((D, WIDE), BF), ((D, WIDE), BF), ((D, WIDE), BF), ((WIDE, D), BF), square, square,
            ((rows, LANES), BF), ((1, rows), F32), ((16, rows), BF),
            ((keys, D), BF), ((D, keys), BF), ((own, WIDE), BF), ((keys, WIDE), BF), ((keys, WIDE), BF),
            ((D, keys), BF), ((HEADS * TALL, keys), BF), ((HEADS * TALL, own), F32),
        ],
        [], "vs" + "v" * 8, 16, 5,
    )(
        spot, seg_lengths, from_core, tokens, valid_row, gain_row, w_query, w_key, w_value, w_attn_out
    )
    from_far = by_core(jnp.concatenate([from_y, normed_a[:16]], axis=0))
    (
        out_rows, d_first, dn_own, payload, vectors, normed_b, normed_tb, k_b, v_b, kt_b,
        q_back, grad_att, pself, dself, seg_grad,
    ) = call(
        functools.partial(forward_kernel, own),
        [
            ((own, D), F32), ((own, D), F32), ((own, D), F32), ((16 * D, D), BF), ((16, D), F32),
            ((keys, D), BF), ((D, keys), BF), ((keys, WIDE), BF), ((keys, WIDE), BF), ((D, keys), BF),
            ((own, WIDE), BF), ((own, WIDE), BF), ((16, own), BF), ((16, own), BF), ((16, D), F32),
        ],
        [
            pltpu.VMEM((HEADS * TALL, keys), BF), pltpu.VMEM((HEADS * TALL, own), F32), pltpu.VMEM((rows, own), F32),
            pltpu.VMEM((WIDE, own), F32), pltpu.VMEM((16, own), F32),
        ],
        "v" * 30, 32, 10,
    )(
        spot, from_y, from_far, codes, real, counted, tokens, cotangent, gain_row, wk_pad, wv_pad, wo_pad, wk_t, wv_t,
        w_cross, b_cross.reshape(1, D), w_mix, w_ens1, gain_two.reshape(1, D), w_up, b_up.reshape(1, FF), w_ens2,
        normed_a, normed_ta, q_aug, k_a, v_a, kt_a, vt_a, part_a,
    )

    def head(index, after_one, after_two):
        return call(
            functools.partial(head_kernel, own, index),
            [((rows, LANES), BF), ((rows, LANES), BF), ((HEAD_DIM, own), BF)],
            [], "v" * 12, 16, 2,
        )(
            q_back, k_a, k_b, v_a, v_b, kt_a, kt_b, grad_att, pself, dself, after_one[:16], after_two[:16]
        )

    def summed(counts, parts, *after, cost=0):
        outs = [((count, D), BF) for count in counts]
        args = list(parts) + list(after)
        body = functools.partial(sum_kernel, counts, len(after))
        return call(body, outs, [], "v" * len(args), 8, cost)(*args)

    def joined(parts, *after, cost=0):
        count = sum(part.shape[0] for part in parts)
        body = functools.partial(join_kernel, len(parts), len(after))
        args = list(parts) + list(after)
        return call(body, [((count, D), BF)], [], "v" * len(args), 8, cost)(*args)[0]

    def by_both(value):
        pairs = [(i, i ^ (n_module + 2)) for i in range(n_batch * n_module)]
        return lax.ppermute(value, ("batch", "module"), pairs)

    size = payload.shape[0] // 8
    big_got = by_core(payload[4 * size :])
    dk0, dv0, dq0 = head(0, pself, pself)
    mine, to_x, to_y, to_both = summed([size] * 4, [payload, big_got])
    got = (by_batch(to_x, 1), by_y(to_y), by_both(to_both))
    dk1, dv1, dq1 = head(1, mine, dq0)
    dk2, dv2, dq2 = head(2, to_x, dq1)
    dk3, dv3, dq3 = head(3, to_y, dq2)
    steps = [1 << place for place in range(1, n_batch.bit_length() - 1)]
    part = D // 8
    count = 2 * own + 16
    shared, dq_rows = call(
        functools.partial(rows_kernel, own),
        [((2 * count, D), BF), ((own, D), BF)],
        [pltpu.VMEM((rows, D), F32)],
        "v" * 23, 16, 3,
    )(
        dk0, dk1, dk2, dk3, dv0, dv1, dv2, dv3, dq0, dq1, dq2, dq3, mine, normed_a, normed_b, counted, seg_grad, dn_own,
        gain_row, w_query, wk_pad, wv_pad, vectors,
    )
    shared_got = by_core(shared[count:])
    half = size // 2
    ab, ab_send = summed([half] * 2, [mine, *got], shared)
    ab_got = by_batch(ab_send, steps[0])
    (q,) = call(functools.partial(weights_kernel, own), [((24 * part, D), BF)], [], "v" * 13, 16, 3)(
        spot, dk0, dk1, dk2, dk3, dv0, dv1, dv2, dv3, dq_rows, normed_ta, normed_tb, ab
    )
    q_got = by_core(q[12 * part :])
    (ab,) = summed([half], [ab, ab_got], q, cost=1)
    ab_got = by_batch(ab, steps[1]) if len(steps) > 1 else ab
    dn, dn_send, vec = summed([own, own, 16], [shared, shared_got], q)
    dn_got = by_y(dn_send)
    grad_tokens, done = call(
        finish_kernel, [((own, D), F32), ((16, D), BF)], [], "v" * 6, 16, 6
    )(dn, dn_got, tokens, d_first, gain_row, ab)
    blocks = summed([3 * part] * 4, [q, q_got], ab)
    q, *sends = [joined([block, vec]) for block in blocks]
    q_got = (by_batch(sends[0], 1), by_y(sends[1]), by_both(sends[2]))
    for i in range(1, len(steps)):
        (ab,) = summed([half], [ab, ab_got], sends[2], done, cost=4)
        if i + 1 < len(steps):
            ab_got = by_batch(ab, steps[i + 1])
    ab_got = by_batch(ab, steps[0])
    rows_q = 3 * part + 16
    (q,) = summed([rows_q], [q, *q_got], ab, cost=3)
    q_got = by_batch(q, steps[0])
    mine = joined([ab, ab_got], q, cost=2)
    got = (by_batch(mine, 1), by_y(mine), by_both(mine))
    (q,) = summed([rows_q], [q, q_got], mine, cost=3)
    for step in steps[1:]:
        q_got = by_batch(q, step)
        (q,) = summed([rows_q], [q, q_got], cost=4)
    q, vec = q[: 3 * part], q[3 * part :]
    q_got = (by_batch(q, 1), by_y(q), by_both(q))
    big = joined([mine, *got], cost=5)
    big_got = by_core(big)
    q = joined([q, *q_got], cost=8)
    q_got = by_core(q)
    wide = ((D, D), F32)
    attn_out, cross, mix, ens1, up, ens2, done = call(
        unpack_kernel,
        [wide, wide, wide, ((4 * D, D), F32), ((D, FF), F32), ((FF + D, D), F32), ((16, D), BF)],
        [], "vvv", 16, 3,
    )(spot, big, big_got)
    gain_one_g, query, key, value, b_cross_g, gain_two_g, b_up_g = call(
        unpack_small_kernel, [row, wide, wide, wide, row, row, ((1, FF), F32)], [], "vvvvv", 16, 2
    )(spot, q, q_got, vec, done)
    return (
        out_rows, grad_tokens, gain_one_g.reshape(D), query, key, value, attn_out, cross, b_cross_g.reshape(D), mix,
        ens1, gain_two_g.reshape(D), up, b_up_g.reshape(FF), ens2,
    )


def solution(mesh):
    rows = P(("batch", "module"), None)
    in_specs = (rows, P("batch", None), P("batch"), rows) + (P(),) * 13
    out_specs = (rows, rows) + (P(),) * 13
    body = functools.partial(shards, mesh.shape["batch"], mesh.shape["module"])
    return jax.shard_map(body, mesh=mesh, in_specs=in_specs, out_specs=out_specs, check_vma=False)
```

```python
import functools

import jax
import jax.numpy as jnp
from jax import lax
from jax.experimental import pallas as pl
from jax.experimental.pallas import tpu as pltpu
from jax.sharding import PartitionSpec as P

D = 256
HEADS = 4
HEAD_DIM = 64
FF = 1024
SEGS = 8
LANES = 128
WIDE = HEADS * LANES
HUGE = -1e30
TALL = HEAD_DIM + 16
BF = jnp.bfloat16
F32 = jnp.float32
MIB = 1024 * 1024


def low(v):
    return v.astype(BF)


def high(v):
    return v.astype(F32)


def dot(a, b):
    return jnp.dot(a, b, preferred_element_type=F32)


def dot_nt(a, b):
    return lax.dot_general(a, b, (((1,), (1,)), ((), ())), preferred_element_type=F32)


def dot_tn(a, b):
    return lax.dot_general(a, b, (((0,), (0,)), ((), ())), preferred_element_type=F32)


def head_sums(selector, product):
    upper = low(product)
    lower = low(product - high(upper))
    return dot_nt(selector, upper) + dot_nt(selector, lower)


def unit_rows(values):
    center = values - jnp.mean(values, axis=1, keepdims=True)
    scale = lax.rsqrt(jnp.mean(center * center, axis=1, keepdims=True) + 1e-05)
    return center * scale, scale


def norm_back(grad, unit, scale, gain):
    scaled = grad * gain
    first_mean = jnp.mean(scaled, axis=1, keepdims=True)
    second_mean = jnp.mean(scaled * unit, axis=1, keepdims=True)
    return scale * (scaled - first_mean - unit * second_mean)


def call(body, outs, scratch, places, limit, microseconds):
    spaces = {"s": pltpu.SMEM, "v": pltpu.VMEM, "h": pltpu.HBM}
    return pl.pallas_call(
        body,
        out_shape=[jax.ShapeDtypeStruct(shape, kind) for shape, kind in outs],
        in_specs=[pl.BlockSpec(memory_space=spaces[place]) for place in places],
        out_specs=[pl.BlockSpec(memory_space=pltpu.VMEM)] * len(outs),
        scratch_shapes=list(scratch),
        compiler_params=pltpu.CompilerParams(vmem_limit_bytes=limit * MIB),
        cost_estimate=pl.CostEstimate(
            flops=microseconds * 10**9, bytes_accessed=0, transcendentals=0
        ),
    )


def widen(weight):
    rows = weight.shape[0]
    gap = jnp.zeros((rows, LANES - HEAD_DIM), weight.dtype)
    pieces = []
    for head in range(HEADS):
        pieces += [weight[:, head * HEAD_DIM : (head + 1) * HEAD_DIM], gap]
    return jnp.concatenate(pieces, axis=1)


def widen_rows(weight):
    gap = jnp.zeros((LANES - HEAD_DIM, weight.shape[1]), weight.dtype)
    pieces = []
    for head in range(HEADS):
        pieces += [weight[head * HEAD_DIM : (head + 1) * HEAD_DIM], gap]
    return jnp.concatenate(pieces, axis=0)


def narrow(wide):
    return jnp.concatenate(
        [wide[:, h * LANES : h * LANES + HEAD_DIM] for h in range(HEADS)], axis=1
    )


def narrow_rows(wide):
    return jnp.concatenate([wide[h * LANES : h * LANES + HEAD_DIM] for h in range(HEADS)], axis=0)


def segment_rows(seg_ref, first_place, count):
    spread = lax.broadcasted_iota(jnp.int32, (16, count), 0)
    places = lax.broadcasted_iota(jnp.int32, (16, count), 1) + first_place
    begin = jnp.zeros((16, count), jnp.int32)
    end = jnp.zeros((16, count), jnp.int32)
    edge = jnp.int32(0)
    for j in range(SEGS):
        begin = jnp.where(spread == j, edge, begin)
        edge = edge + seg_ref[0, j]
        end = jnp.where(spread == j, edge, end)
    return spread, (places >= begin) & (places < end)


def head_selector():
    rows = lax.broadcasted_iota(jnp.int32, (16, WIDE), 0)
    lanes = lax.broadcasted_iota(jnp.int32, (16, WIDE), 1)
    return low(jnp.where((lanes >> 7) == rows, 1.0, 0.0))


def start_kernel(me_ref, spot):
    rows = lax.broadcasted_iota(jnp.int32, spot.shape, 0)
    spot[...] = jnp.where(rows == 0, me_ref[0], me_ref[1])


def project(rows_in, gain, code, wk_pad, wv_t, at, normed, normed_t, k_aug, vt):
    count = rows_in.shape[0]
    unit, _ = unit_rows(high(rows_in))
    value = low(unit * gain)
    flipped = value.T
    normed[at : at + count, :] = value
    normed_t[:, at : at + count] = flipped
    wide = low(dot(value, wk_pad))
    k_aug[at : at + count, :] = wide + jnp.concatenate([code] * HEADS, axis=1)
    turned = low(dot(wv_t, flipped))
    for h in range(HEADS):
        vt[h * TALL : h * TALL + HEAD_DIM, at : at + count] = turned[h * HEAD_DIM : (h + 1) * HEAD_DIM]
        vt[h * TALL + HEAD_DIM : (h + 1) * TALL, at : at + count] = jnp.ones((16, count), BF)


def raw_attention(q_aug, k_aug, vt, before, part):
    for h in range(HEADS):
        lanes = slice(h * LANES, (h + 1) * LANES)
        tall = slice(h * TALL, (h + 1) * TALL)
        p = low(jnp.exp(dot_nt(k_aug[:, lanes], q_aug[:, lanes])))
        got = dot(vt[tall, :], p)
        part[tall, :] = got if before is None else got + before[tall, :]


def exact_attention(q_aug, parts, self_rows, vt_own, scores, o_t, lse_out):
    step = 256

    def one_head(h, _):
        lanes = pl.ds(pl.multiple_of(h * LANES, LANES), LANES)
        tall = pl.ds(pl.multiple_of(h * TALL, 16), HEAD_DIM)
        q_h = q_aug[:, lanes]
        self_h = self_rows[pl.ds(h, 1), :]
        top = self_h
        first = 0
        for k_part, _ in parts:

            def score(c, top, k_part=k_part, first=first):
                at = pl.multiple_of(c * step, step)
                part = dot_nt(k_part[pl.ds(at, step), lanes], q_h)
                scores[pl.ds(first + at, step), :] = part
                return jnp.maximum(top, jnp.max(part, axis=0, keepdims=True))

            top = lax.fori_loop(0, k_part.shape[0] // step, score, top)
            first += k_part.shape[0]
        p_self = jnp.exp(self_h - top)
        total = p_self
        acc = high(low(p_self)) * high(vt_own[tall, :])
        first = 0
        for _, vt_part in parts:

            def weigh(c, carry, vt_part=vt_part, first=first):
                total, acc = carry
                at = pl.multiple_of(c * step, step)
                p = jnp.exp(scores[pl.ds(first + at, step), :] - top)
                total = total + jnp.sum(p, axis=0, keepdims=True)
                return total, acc + dot(vt_part[tall, pl.ds(at, step)], low(p))

            total, acc = lax.fori_loop(0, vt_part.shape[1] // step, weigh, (total, acc))
            first += vt_part.shape[1]
        o_t[pl.ds(pl.multiple_of(h * LANES, LANES), HEAD_DIM), :] = acc / total
        lse_out[pl.ds(h, 1), :] = top + jnp.log(total)
        return 0

    lax.fori_loop(0, HEADS, one_head, 0)


def placed(rows16, first):
    upper = low(rows16)
    rest = rows16 - high(upper)
    middle = low(rest)
    parts = (upper, middle, low(rest - high(middle)))
    rows = lax.broadcasted_iota(jnp.int32, (16, WIDE), 0)
    lanes = lax.broadcasted_iota(jnp.int32, (16, WIDE), 1)
    total = 0.0
    for i, piece in enumerate(parts):
        picked = ((lanes >> 7) == rows) & ((lanes & (LANES - 1)) == first + i)
        total = total + dot_tn(piece, low(jnp.where(picked, 1.0, 0.0)))
    return low(total)


def lane_codes(rows_code):
    picked = lax.broadcasted_iota(jnp.int32, (16, LANES), 1) - HEAD_DIM
    picked = (picked == lax.broadcasted_iota(jnp.int32, (16, LANES), 0)) & (picked <= SEGS + 3)
    return low(dot_tn(low(rows_code), low(jnp.where(picked, 1.0, 0.0))))


def first_kernel(
    own_rows,
    spot, seg, core_rows, tokens, valid, gain_one, wq, wk, wv, wo, w_cross, b_cross,
    wq_pad, wk_pad, wv_pad, wo_pad, wk_t, wv_t, codes, real, counted,
    normed, normed_t, q_aug, k_aug, vt, part, self_scores, crossed,
):
    me = jnp.max(spot[0:1, :])
    for step in range(4):
        at = pl.multiple_of((me ^ step) * own_rows, own_rows)
        spread, inside = segment_rows(seg, at, own_rows)
        ok = valid[:, pl.ds(at, own_rows)] > 0
        code = jnp.where(inside, HUGE, 0.0)
        code = jnp.where(spread == SEGS, jnp.where(ok, 0.0, HUGE), code)
        code = jnp.where(spread > SEGS, 1.0, code)
        codes[step * own_rows : (step + 1) * own_rows, :] = lane_codes(code)
        real[:, step * own_rows : (step + 1) * own_rows] = jnp.where(ok, 1.0, 0.0)
        counted[:, step * own_rows : (step + 1) * own_rows] = low(jnp.where(inside & ok, 1.0, 0.0))
    wq_pad[...] = low(widen(high(wq[...])))
    wk_pad[...] = low(widen(high(wk[...])))
    wv_pad[...] = low(widen(high(wv[...])))
    wo_pad[...] = low(widen_rows(high(wo[...])))
    wk_t[...] = wk[...].T
    wv_t[...] = wv[...].T
    gain = gain_one[...]
    for step, rows_in in enumerate((tokens, core_rows)):
        at = step * own_rows
        project(
            rows_in[...], gain, codes[at : at + own_rows, :], wk_pad[...], wv_t[...], at,
            normed, normed_t, k_aug, vt,
        )
    spread, inside = segment_rows(seg, pl.multiple_of(me * own_rows, own_rows), own_rows)
    own_code = lane_codes(jnp.where(inside | (spread > SEGS), 0.0, 1.0))
    scaled = low(dot(normed[:own_rows, :], wq_pad[...]) * 0.125)
    q_aug[...] = scaled + jnp.concatenate([own_code] * HEADS, axis=1)
    raw_attention(q_aug, k_aug, vt, None, part)
    lanes_own = lax.broadcasted_iota(jnp.int32, (own_rows, WIDE), 1) & (LANES - 1)
    product = high(q_aug[...]) * high(k_aug[:own_rows, :])
    self_scores[...] = head_sums(head_selector(), jnp.where(lanes_own < HEAD_DIM, product, 0.0))
    crossed[...] = dot(normed[:own_rows, :], w_cross[...]) + b_cross[...]


def middle_kernel(
    own_rows,
    y_rows, gain_one, codes, wk_pad, wv_t, q_aug, part_a,
    normed, normed_t, k_aug, vt, part,
):
    project(
        y_rows[...], gain_one[...], codes[2 * own_rows : 3 * own_rows, :], wk_pad[...], wv_t[...], 0,
        normed, normed_t, k_aug, vt,
    )
    raw_attention(q_aug, k_aug, vt, part_a, part)


def forward_kernel(
    own_rows,
    spot, far_rows, codes, real, counted, tokens, cot,
    gain_one, wk_pad, wo_pad, wv_t,
    w_mix, w_ens1, gain_two, w_up, b_up, w_ens2,
    normed_a, normed_y, q_aug, k_a, k_y, vt_a, vt_y, part_y, self_scores, crossed,
    payload, d_first_out, vectors, normed_f, normed_tf, k_f,
    first_out, active_out, normed_two_out, d_modules_out, att_out, lse_out, member_out, counts_out,
    vt_f, part_f, scores, o_t, self_rows,
):
    project(
        far_rows[:own_rows, :], gain_one[...], codes[3 * own_rows :, :], wk_pad[...], wv_t[...], 0,
        normed_f, normed_tf, k_f, vt_f,
    )
    normed_own = normed_a[:own_rows, :]
    own_real = real[:, :own_rows] > 0
    o_t[...] = jnp.zeros_like(o_t)
    lse_out[...] = jnp.zeros_like(lse_out)
    raw_attention(q_aug, k_f, vt_f, part_y, part_f)
    vt_own = vt_a[:, :own_rows]
    smallest, largest = jnp.inf, -jnp.inf
    for h in range(HEADS):
        p_self = jnp.where(own_real, 0.0, jnp.exp(self_scores[h : h + 1, :]))
        both = part_f[h * TALL : (h + 1) * TALL, :]
        total = both[HEAD_DIM : HEAD_DIM + 1] + p_self
        acc = both[:HEAD_DIM] + high(low(p_self)) * high(vt_own[h * TALL : h * TALL + HEAD_DIM])
        o_t[h * LANES : h * LANES + HEAD_DIM, :] = acc / total
        lse_out[h : h + 1, :] = jnp.log(total)
        smallest = jnp.minimum(smallest, total)
        largest = jnp.maximum(largest, total)
    fits = (jnp.min(smallest) > 1e-25) & (jnp.max(largest) < 1e30)

    @pl.when(jnp.logical_not(fits))
    def _():
        self_rows[...] = jnp.where(own_real, HUGE, self_scores[...])
        parts = ((k_a, vt_a), (k_y, vt_y), (k_f, vt_f))
        exact_attention(q_aug, parts, self_rows, vt_a.at[:, :own_rows], scores, o_t, lse_out)

    att = o_t[...].T
    att_out[...] = att
    att_low = low(att)

    modules = []
    for g in range(2):
        lanes = slice(g * 256, (g + 1) * 256)
        modules.append(low(dot(att_low[:, lanes], wo_pad[lanes, :])))
    modules.append(low(high(normed_own) * crossed[...]))
    counts = jnp.sum(high(counted[...]), axis=1, keepdims=True)
    counts = jnp.maximum(counts, 1.0)
    counts_out[...] = jnp.broadcast_to(counts, counts_out.shape)
    seg_sums = dot(counted[:, : 2 * own_rows], normed_a[...])
    seg_sums = seg_sums + dot(counted[:, 2 * own_rows : 3 * own_rows], normed_y[...])
    seg_sums = seg_sums + dot(counted[:, 3 * own_rows :], normed_f[...])
    seg_mean = low(seg_sums / counts)
    picked = lax.broadcasted_iota(jnp.int32, (LANES, 16), 0) - HEAD_DIM
    picked = (picked == lax.broadcasted_iota(jnp.int32, (LANES, 16), 1)) & (picked < SEGS)
    own_member = 1.0 - dot(q_aug[:, :LANES], low(jnp.where(picked, 1.0, 0.0)))
    own_lane = lax.broadcasted_iota(jnp.int32, (own_rows, 16), 1)
    own_member = low(jnp.where(own_lane < SEGS, own_member, 0.0))
    member_out[...] = own_member
    mixed = low(dot(own_member, seg_mean))
    modules.append(low(dot(mixed, w_mix[...])))
    first = high(tokens[...])
    for i in range(4):
        first = first + dot(modules[i], w_ens1[i * D : (i + 1) * D, :])
    first_out[...] = first
    unit_two, scale_two = unit_rows(first)
    normed_two = low(unit_two * gain_two[...])
    inner = dot(normed_two, w_up[...]) + b_up[...]
    cdf = 0.5 * (1.0 + lax.erf(inner * 0.7071067811865476))
    active = low(inner * cdf)
    slope = cdf + inner * jnp.exp(-0.5 * inner * inner) * 0.3989422804014327
    active_out[...] = active
    normed_two_out[...] = normed_two

    core, y_bit, x_bit, z_bit = bits_of(spot)
    order = y_bit * 8 + x_bit * 4 + z_bit * 2
    block = payload.shape[0] // 32
    place = [0]

    def put(grad):
        middle = grad.shape[0] // 2
        for i in range(middle // block):
            n = place[0]
            place[0] = n + 1
            place_at = n ^ order
            for side in range(2):
                start = pl.multiple_of(((side ^ core) * 16 + place_at) * block, block)
                first = side * middle + i * block
                payload[pl.ds(start, block), :] = low(grad[first : first + block])

    e2 = cot[...]
    put(dot_tn(active, e2))
    put(dot_tn(normed_two, e2))
    d_inner = low(dot_nt(e2, w_ens2[:FF, :]) * slope)
    b_up_grad = jnp.sum(high(d_inner), axis=0, keepdims=True)
    grad_up = dot_tn(normed_two, d_inner)
    for i in range(FF // D):
        put(grad_up[:, i * D : (i + 1) * D])
    d_norm2 = dot_nt(e2, w_ens2[FF:, :]) + dot_nt(d_inner, w_up[...])
    d_first = high(e2) + norm_back(d_norm2, unit_two, scale_two, gain_two[...])
    d_first_out[...] = d_first
    e1 = low(d_first)
    d_modules = []
    for i in range(4):
        put(dot_tn(modules[i], e1))
        d_modules.append(low(dot_nt(e1, w_ens1[i * D : (i + 1) * D, :])))
        d_modules_out[:, i * D : (i + 1) * D] = d_modules[i]
    out_grads = []
    for g in range(2):
        lanes = slice(g * 256, (g + 1) * 256)
        out_grads.append(dot_tn(att_low[:, lanes], d_modules[g]))
    put(narrow_rows(jnp.concatenate(out_grads, axis=0)))
    put(dot_tn(normed_own, low(high(d_modules[2]) * high(normed_own))))
    put(dot_tn(mixed, d_modules[3]))
    vectors[...] = jnp.zeros_like(vectors)
    for i in range(FF // D):
        vectors[i : i + 1, :] = b_up_grad[:, i * D : (i + 1) * D]
    vectors[5:6, :] = jnp.sum(d_norm2 * unit_two, axis=0, keepdims=True)


def side_kernel(
    own_rows,
    first, active, normed_two, w_ens2, d_modules, att, lse, own_member, counts, vectors_in,
    normed_a, normed_y, normed_f, normed_ta, normed_ty, normed_tf, q_aug, self_scores, crossed, real,
    wv_pad, wk_t, wo_pad, w_cross, w_mix,
    out_rows, dn_own, vectors, v_all, kt_all, q_back, grad_att, pself_out, dself_out, seg_grad_out,
):
    v_lane = lax.broadcasted_iota(jnp.int32, (1, WIDE), 1) & (LANES - 1)
    v_ones = jnp.where((v_lane >= HEAD_DIM) & (v_lane < HEAD_DIM + 3), 1.0, 0.0)
    at = 0
    for normed, flipped in ((normed_a, normed_ta), (normed_y, normed_ty), (normed_f, normed_tf)):
        count = normed.shape[0]
        v_all[at : at + count, :] = low(dot(normed[...], wv_pad[...]) + v_ones)
        kt_all[:, at : at + count] = low(dot(wk_t[...], flipped[...]))
        at += count
    out_rows[...] = first[...] + (dot(active[...], w_ens2[:FF, :]) + dot(normed_two[...], w_ens2[FF:, :]))
    d_att = []
    for g in range(2):
        lanes = slice(g * 256, (g + 1) * 256)
        d_att.append(low(dot_nt(d_modules[:, g * D : (g + 1) * D], wo_pad[lanes, :])))
    d_att = jnp.concatenate(d_att, axis=1)
    heads16 = head_selector()
    delta = head_sums(heads16, high(d_att) * att[...])
    grad_att[...] = d_att + placed(-delta, HEAD_DIM)
    q_back[...] = q_aug[...] + placed(-lse[...], HEAD_DIM + SEGS + 1)
    p_self = jnp.where(real[:, :own_rows] > 0, 0.0, jnp.exp(self_scores[...] - lse[...]))
    dp_self = head_sums(heads16, high(d_att) * high(v_all[:own_rows, :]))
    pself_out[...] = low(p_self)
    dself_out[...] = low(p_self * (dp_self - delta))
    d_two = high(d_modules[:, 2 * D : 3 * D])
    d_cross = low(d_two * high(normed_a[:own_rows, :]))
    dn_own[...] = d_two * crossed[...] + dot_nt(d_cross, w_cross[...])
    d_mixed = dot_nt(d_modules[:, 3 * D :], w_mix[...])
    mixed_up = low(d_mixed)
    mixed_down = low(d_mixed - high(mixed_up))
    seg_grad = dot_tn(own_member[...], mixed_up) + dot_tn(own_member[...], mixed_down)
    seg_grad_out[...] = seg_grad / counts[:, :1]
    tail = lax.broadcasted_iota(jnp.int32, (16, D), 0)
    b_cross_grad = jnp.sum(high(d_cross), axis=0, keepdims=True)
    vectors[...] = jnp.where(tail == 4, b_cross_grad, vectors_in[...])


def head_kernel(
    own_rows, h,
    q_back, k_a, k_y, k_f, v_all, kt_all, grad_att, pself, dself,
    *rest,
):
    dk_out, dv_out, dq_out = rest[-3:]
    row16 = lax.broadcasted_iota(jnp.int32, (16, LANES), 0)
    spread = low(jnp.where(row16 == h, 1.0, 0.0))
    lanes = slice(h * LANES, (h + 1) * LANES)
    rows_h = slice(h * HEAD_DIM, (h + 1) * HEAD_DIM)
    q_h = q_back[:, lanes]
    g_h = grad_att[:, lanes]
    acc = high(dself[h : h + 1, :]) * high(kt_all[rows_h, :own_rows])
    first = 0
    for k_part in (k_a, k_y, k_f):
        count = k_part.shape[0]
        at = slice(first, first + count)
        p = jnp.exp(dot_nt(k_part[:, lanes], q_h))
        ds = low(p * dot_nt(v_all[at, lanes], g_h))
        dv = dot(low(p), g_h)
        dk = dot(ds, q_h)
        if first == 0:
            dk_self = dot_tn(dself[...], spread) * high(q_h)
            dv_self = dot_tn(pself[...], spread) * high(g_h)
            dk_out[:own_rows, :] = low(dk[:own_rows] + dk_self)
            dv_out[:own_rows, :] = low(dv[:own_rows] + dv_self)
            dk_out[own_rows:count, :] = low(dk[own_rows:])
            dv_out[own_rows:count, :] = low(dv[own_rows:])
        else:
            dk_out[at, :] = low(dk)
            dv_out[at, :] = low(dv)
        acc = acc + dot(kt_all[rows_h, at], ds)
        first += count
    dq_out[...] = low(acc * 0.125)


def rows_kernel(
    own_rows,
    dk0, dk1, dk2, dk3, dv0, dv1, dv2, dv3, dq0, dq1, dq2, dq3, normed_a, normed_y, normed_f, counted, seg_grad, dn_own,
    gain_one, wq, wk_pad, wv_pad, vectors,
    *rest,
):
    out, dq_out, dn = rest[-3:]
    half_keys = 2 * own_rows
    dq = jnp.concatenate([high(part[...]) for part in (dq0, dq1, dq2, dq3)], axis=0)
    dq_rows = low(dq.T)
    dq_out[...] = dq_rows
    dk_pairs = [jnp.concatenate([dk0[...], dk1[...]], axis=1), jnp.concatenate([dk2[...], dk3[...]], axis=1)]
    dv_pairs = [jnp.concatenate([dv0[...], dv1[...]], axis=1), jnp.concatenate([dv2[...], dv3[...]], axis=1)]
    up = low(seg_grad[...])
    down = low(seg_grad[...] - high(up))
    for c in range(2):
        at = slice(c * half_keys, (c + 1) * half_keys)
        mixing = dot_tn(counted[:, at], up) + dot_tn(counted[:, at], down)
        dn[at, :] = mixing + (
            dot_nt(dk_pairs[0][at, :], wk_pad[:, :256])
            + dot_nt(dk_pairs[1][at, :], wk_pad[:, 256:])
            + dot_nt(dv_pairs[0][at, :], wv_pad[:, :256])
            + dot_nt(dv_pairs[1][at, :], wv_pad[:, 256:])
        )
    dn[:own_rows, :] = dn[:own_rows, :] + (dot_nt(dq_rows, wq[...]) + dn_own[...])
    gain_grad = jnp.sum(dn[:half_keys, :] * high(normed_a[...]), axis=0, keepdims=True)
    for i, normed in enumerate((normed_y, normed_f)):
        here = dn[(2 + i) * own_rows : (3 + i) * own_rows, :]
        gain_grad = gain_grad + jnp.sum(here * high(normed[...]), axis=0, keepdims=True)
    gain_grad = gain_grad / gain_one[...]
    count = out.shape[0] // 2
    for step in range(4):
        at = (step % 2) * count + (step // 2) * own_rows
        out[at : at + own_rows, :] = low(dn[step * own_rows : (step + 1) * own_rows, :])
    tail = lax.broadcasted_iota(jnp.int32, (16, D), 0)
    row = jnp.where(tail == 6, gain_grad, vectors[...])
    out[count - 16 : count, :] = low(row)
    out[2 * count - 16 :, :] = low(row)


def weights_kernel(
    own_rows,
    spot,
    dk0, dk1, dk2, dk3, dv0, dv1, dv2, dv3, dq_rows, normed_ta, normed_ty, normed_tf,
    *rest,
):
    out = rest[-1]
    flips = ((normed_ta, 0), (normed_ty, 2), (normed_tf, 3))

    def key_grad(parts):
        pairs = [jnp.concatenate([parts[i][...], parts[i + 1][...]], axis=1) for i in (0, 2)]
        return narrow(
            jnp.concatenate(
                [
                    sum(
                        dot(flip[...], pair[at * own_rows : at * own_rows + flip.shape[1]])
                        for flip, at in flips
                    )
                    for pair in pairs
                ],
                axis=1,
            )
        )

    core, y_bit, x_bit, _ = bits_of(spot)
    order = core * 4 + y_bit * 2 + x_bit
    part = D // 8
    for i, grad in enumerate(
        (
            dot(normed_ta[:, :own_rows], dq_rows[...]),
            key_grad((dk0, dk1, dk2, dk3)),
            key_grad((dv0, dv1, dv2, dv3)),
        )
    ):
        for n in range(8):
            at = ((n ^ order) * 3 + i) * part
            out[pl.ds(pl.multiple_of(at, part), part), :] = low(grad[n * part : (n + 1) * part])


def finish_kernel(mine, other, tokens, d_first, gain_one, *rest):
    grad_tokens, done = rest[-2:]
    unit, scale = unit_rows(high(tokens[...]))
    total = high(mine[...]) + high(other[...])
    grad_tokens[...] = d_first[...] + norm_back(total, unit, scale, gain_one[...])
    done[...] = mine[:16, :]


def unpack_kernel(spot, mine, other, *rest):
    attn_out, cross, mix, ens1, up, ens2, done = rest[-7:]
    core, y_bit, x_bit, z_bit = bits_of(spot)
    order = y_bit * 8 + x_bit * 4 + z_bit * 2
    block = mine.shape[0] // 16
    every = slice(None)
    jobs = [(ens2, 0, FF, every), (ens2, FF, D, every)]
    jobs += [(up, 0, D, slice(i * D, (i + 1) * D)) for i in range(FF // D)]
    jobs += [(ens1, i * D, D, every) for i in range(4)]
    jobs += [(attn_out, 0, D, every), (cross, 0, D, every), (mix, 0, D, every)]
    n = 0
    for to, first, count, columns in jobs:
        for i in range(count // 2 // block):
            place_at = n ^ order
            n += 1
            for side, source in ((core, mine), (1 - core, other)):
                at = pl.multiple_of(first + side * (count // 2) + i * block, block)
                value = source[pl.ds(pl.multiple_of(place_at * block, block), block), :]
                to[pl.ds(at, block), columns] = high(value)
    done[...] = mine[:16, :]


def unpack_small_kernel(spot, mine, other, vec, *rest):
    gain_one, query, key, value, b_cross, gain_two, b_up, done = rest[-8:]
    core, y_bit, x_bit, _ = bits_of(spot)
    order = y_bit * 2 + x_bit
    part = D // 8
    for side, source in ((core, mine), (1 - core, other)):
        for n in range(4):
            for i, to in enumerate((query, key, value)):
                at = pl.multiple_of((n ^ order) * 3 * part + i * part, part)
                here = pl.ds(pl.multiple_of((side * 4 + n) * part, part), part)
                to[here, :] = high(source[pl.ds(at, part), :])
    wide = high(vec[...])
    for i in range(FF // D):
        b_up[:, i * D : (i + 1) * D] = wide[i : i + 1]
    b_cross[...] = wide[4:5]
    gain_two[...] = wide[5:6]
    gain_one[...] = wide[6:7]
    done[...] = mine[:16, :]


def swap(value, axis, count, step):
    return lax.ppermute(value, axis, [(i, i ^ step) for i in range(count)])


def bits_of(spot):
    module, batch = jnp.max(spot[0:1, :]), jnp.max(spot[1:2, :])
    return module & 1, (module >> 1) & 1, batch & 1, (batch >> 1) & 1


def sum_kernel(counts, afters, *refs):
    inputs, outs = refs[: len(refs) - afters - len(counts)], refs[len(refs) - len(counts) :]
    at = 0
    for count, out in zip(counts, outs):
        total = high(inputs[0][at : at + count, :])
        for other in inputs[1:]:
            total = total + high(other[at : at + count, :])
        out[...] = low(total)
        at += count


def join_kernel(jobs, afters, *refs):
    out = refs[-1]
    at = 0
    for ref in refs[:jobs]:
        count = ref.shape[0]
        out[at : at + count, :] = ref[...]
        at += count


def added(one, two):
    return low(high(one) + high(two))


def shards(
    n_batch,
    n_module,
    tokens,
    seg_lengths,
    valid,
    cotangent,
    gain_one,
    w_query,
    w_key,
    w_value,
    w_attn_out,
    w_cross,
    b_cross,
    w_mix,
    w_ens1,
    gain_two,
    w_up,
    b_up,
    w_ens2,
):
    module = lax.axis_index("module")
    batch = lax.axis_index("batch")
    own = tokens.shape[0]
    rows = valid.shape[0]
    me = jnp.stack([module, batch]).astype(jnp.int32)

    def by_core(value):
        return swap(value, "module", n_module, 1)

    def by_y(value):
        return swap(value, "module", n_module, 2)

    def by_batch(value, step):
        return swap(value, "batch", n_batch, step)

    from_core = by_core(tokens)
    from_y = by_y(tokens)
    square = ((D, D), BF)
    keys = 2 * own
    row = ((1, D), F32)
    gain_row, valid_row = gain_one.reshape(1, D), valid.reshape(1, rows)
    (spot,) = call(start_kernel, [((8, LANES), jnp.int32)], [], "s", 4, 20)(me)
    (
        wq_pad, wk_pad, wv_pad, wo_pad, wk_t, wv_t, codes, real, counted,
        normed_a, normed_ta, q_aug, k_a, vt_a, part_a, self_scores, crossed,
    ) = call(
        functools.partial(first_kernel, own),
        [
            ((D, WIDE), BF), ((D, WIDE), BF), ((D, WIDE), BF), ((WIDE, D), BF), square, square,
            ((rows, LANES), BF), ((1, rows), F32), ((16, rows), BF),
            ((keys, D), BF), ((D, keys), BF), ((own, WIDE), BF), ((keys, WIDE), BF),
            ((HEADS * TALL, keys), BF), ((HEADS * TALL, own), F32), ((16, own), F32), ((own, D), F32),
        ],
        [], "vs" + "v" * 10, 16, 5,
    )(
        spot, seg_lengths, from_core, tokens, valid_row, gain_row, w_query, w_key, w_value, w_attn_out,
        w_cross, b_cross.reshape(1, D),
    )
    from_far = by_core(jnp.concatenate([from_y, normed_a[:16]], axis=0))
    normed_y, normed_ty, k_y, vt_y, part_y = call(
        functools.partial(middle_kernel, own),
        [((own, D), BF), ((D, own), BF), ((own, WIDE), BF), ((HEADS * TALL, own), BF), ((HEADS * TALL, own), F32)],
        [], "v" * 7, 16, 2,
    )(from_y, gain_row, codes, wk_pad, wv_t, q_aug, part_a)
    (
        payload, d_first, vectors, normed_f, normed_tf, k_f,
        first, active, normed_two, d_modules, att, lse, own_member, counts,
    ) = call(
        functools.partial(forward_kernel, own),
        [
            ((16 * D, D), BF), ((own, D), F32), ((16, D), F32), ((own, D), BF), ((D, own), BF), ((own, WIDE), BF),
            ((own, D), F32), ((own, FF), BF), ((own, D), BF), ((own, 4 * D), BF), ((own, WIDE), F32), ((16, own), F32),
            ((own, 16), BF), ((16, LANES), F32),
        ],
        [
            pltpu.VMEM((HEADS * TALL, own), BF), pltpu.VMEM((HEADS * TALL, own), F32), pltpu.VMEM((rows, own), F32),
            pltpu.VMEM((WIDE, own), F32), pltpu.VMEM((16, own), F32),
        ],
        "v" * 27, 32, 8,
    )(
        spot, from_far, codes, real, counted, tokens, cotangent, gain_row, wk_pad, wo_pad, wv_t,
        w_mix, w_ens1, gain_two.reshape(1, D), w_up, b_up.reshape(1, FF), w_ens2,
        normed_a, normed_y, q_aug, k_a, k_y, vt_a, vt_y, part_y, self_scores, crossed,
    )
    big_got = by_core(payload[payload.shape[0] // 2 :])
    out_rows, dn_own, vectors, v_all, kt_all, q_back, grad_att, pself, dself, seg_grad = call(
        functools.partial(side_kernel, own),
        [
            ((own, D), F32), ((own, D), F32), ((16, D), F32), ((rows, WIDE), BF), ((D, rows), BF),
            ((own, WIDE), BF), ((own, WIDE), BF), ((16, own), BF), ((16, own), BF), ((16, D), F32),
        ],
        [], "v" * 25, 16, 3,
    )(
        first, active, normed_two, w_ens2, d_modules, att, lse, own_member, counts, vectors,
        normed_a, normed_y, normed_f, normed_ta, normed_ty, normed_tf, q_aug, self_scores, crossed, real,
        wv_pad, wk_t, wo_pad, w_cross, w_mix,
    )

    def head(index, *after, cost=0):
        args = [q_back, k_a, k_y, k_f, v_all, kt_all, grad_att, pself, dself, *after]
        return call(
            functools.partial(head_kernel, own, index),
            [((rows, LANES), BF), ((rows, LANES), BF), ((HEAD_DIM, own), BF)],
            [], "v" * len(args), 16, cost,
        )(*args)

    def summed(counts, parts, *after, cost=0):
        outs = [((count, D), BF) for count in counts]
        args = list(parts) + list(after)
        body = functools.partial(sum_kernel, counts, len(after))
        return call(body, outs, [], "v" * len(args), 8, cost)(*args)

    def joined(parts, *after, cost=0):
        count = sum(part.shape[0] for part in parts)
        body = functools.partial(join_kernel, len(parts), len(after))
        args = list(parts) + list(after)
        return call(body, [((count, D), BF)], [], "v" * len(args), 8, cost)(*args)[0]

    def by_both(value):
        pairs = [(i, i ^ (n_module + 2)) for i in range(n_batch * n_module)]
        return lax.ppermute(value, ("batch", "module"), pairs)

    def around(values):
        return by_batch(values[0], 1), by_y(values[1]), by_both(values[2])

    steps = [1 << place for place in range(1, n_batch.bit_length() - 1)]

    def through(value, got, *after, cost=0):
        for step in steps[2:] + [0]:
            (value,) = summed([value.shape[0]], [value, got], *after, cost=cost)
            got = by_batch(value, step) if step else None
        return value

    size = payload.shape[0] // 8
    half = size // 2
    part = D // 8
    count = 2 * own + 16
    rows_q = 3 * part + 16
    wide = ((D, D), F32)
    mine, *outward = summed([size] * 4, [payload, big_got], pself, cost=0)
    xy_got = around(outward)
    dk0, dv0, dq0 = head(0, mine, cost=2)
    dk1, dv1, dq1 = head(1, dq0, cost=2)
    dk2, dv2, dq2 = head(2, dq1, cost=2)
    dk3, dv3, dq3 = head(3, dq2, cost=2)
    args = [
        dk0, dk1, dk2, dk3, dv0, dv1, dv2, dv3, dq0, dq1, dq2, dq3, normed_a, normed_y, normed_f, counted, seg_grad,
        dn_own, gain_row, w_query, wk_pad, wv_pad, vectors,
    ]
    shared, dq_rows = call(
        functools.partial(rows_kernel, own),
        [((2 * count, D), BF), ((own, D), BF)],
        [pltpu.VMEM((rows, D), F32)],
        "v" * len(args), 16, 3,
    )(*args)
    ab, ab_send = summed([half] * 2, [mine, *xy_got], dq_rows, cost=0)
    z1_got = by_batch(ab_send, steps[0])
    shared_got = by_core(shared[count:])
    args = [
        spot, dk0, dk1, dk2, dk3, dv0, dv1, dv2, dv3, dq_rows, normed_ta, normed_ty, normed_tf, ab,
    ]
    (q,) = call(
        functools.partial(weights_kernel, own), [((24 * part, D), BF)], [], "v" * len(args), 16, 3
    )(*args)
    (ab1,) = summed([half], [ab, z1_got], q, cost=0)
    z2_got = by_batch(ab1, steps[1])
    q_out = joined([q[12 * part :]], ab1, cost=0)
    q_core = by_core(q_out)
    dn, dn_send, vec = summed([own, own, 16], [shared, shared_got], q, cost=0)
    dn_got = by_y(dn_send)
    args = [dn, dn_got, tokens, d_first, gain_row, ab1]
    grad_tokens, done = call(
        finish_kernel, [((own, D), F32), ((16, D), BF)], [], "v" * len(args), 16, 6
    )(*args)
    blocks = summed([3 * part] * 4, [q, q_core], ab1, cost=0)
    q0, *sends = [joined([block, vec]) for block in blocks]
    q_xy = around(sends)
    ab2 = through(ab1, z2_got, sends[2], done, cost=4)
    back_got = by_batch(ab2, steps[0])
    (q1,) = summed([rows_q], [q0, *q_xy], ab2, cost=3)
    q_z1 = by_batch(q1, steps[0])
    mine2 = joined([ab2, back_got], q1, cost=2)
    xy_back = around([mine2] * 3)
    (q2,) = summed([rows_q], [q1, q_z1], mine2, cost=3)
    q_z2 = by_batch(q2, steps[1])
    q3 = through(q2, q_z2, cost=0)
    q4 = q3[: 3 * part]
    q_back_got = around([q4] * 3)
    big = joined([mine2, *xy_back], q3, cost=0)
    big_got = by_core(big)
    args = [spot, big, big_got]
    attn_out, cross, mix, ens1, up, ens2, done_big = call(
        unpack_kernel,
        [wide, wide, wide, ((4 * D, D), F32), ((D, FF), F32), ((FF + D, D), F32), ((16, D), BF)],
        [], "v" * len(args), 16, 3,
    )(*args)
    q5 = joined([q4, *q_back_got], done_big, cost=0)
    q_last = by_core(q5)
    args = [spot, q5, q_last, q3[3 * part :], done_big]
    gain_one_g, query, key, value, b_cross_g, gain_two_g, b_up_g, done_small = call(
        unpack_small_kernel, [row, wide, wide, wide, row, row, ((1, FF), F32), ((16, D), BF)],
        [], "v" * len(args), 16, 2,
    )(*args)
    return (
        out_rows, grad_tokens, gain_one_g.reshape(D), query, key, value, attn_out, cross, b_cross_g.reshape(D), mix,
        ens1, gain_two_g.reshape(D), up, b_up_g.reshape(FF), ens2,
    )


def solution(mesh):
    rows = P(("batch", "module"), None)
    in_specs = (rows, P("batch", None), P("batch"), rows) + (P(),) * 13
    out_specs = (rows, rows) + (P(),) * 13
    body = functools.partial(shards, mesh.shape["batch"], mesh.shape["module"])
    return jax.shard_map(body, mesh=mesh, in_specs=in_specs, out_specs=out_specs, check_vma=False)
```

```python
import functools

import jax
import jax.numpy as jnp
from jax import lax
from jax.experimental import pallas as pl
from jax.experimental.pallas import tpu as pltpu
from jax.sharding import PartitionSpec as P

D = 256
HEADS = 4
HEAD_DIM = 64
FF = 1024
SEGS = 8
LANES = 128
WIDE = HEADS * LANES
HUGE = -1e30
TALL = HEAD_DIM + 16
BF = jnp.bfloat16
F32 = jnp.float32
MIB = 1024 * 1024


def low(v):
    return v.astype(BF)


def high(v):
    return v.astype(F32)


def dot(a, b):
    return jnp.dot(a, b, preferred_element_type=F32)


def dot_nt(a, b):
    return lax.dot_general(a, b, (((1,), (1,)), ((), ())), preferred_element_type=F32)


def dot_tn(a, b):
    return lax.dot_general(a, b, (((0,), (0,)), ((), ())), preferred_element_type=F32)


def head_sums(selector, product):
    upper = low(product)
    lower = low(product - high(upper))
    return dot_nt(selector, upper) + dot_nt(selector, lower)


def unit_rows(values):
    center = values - jnp.mean(values, axis=1, keepdims=True)
    scale = lax.rsqrt(jnp.mean(center * center, axis=1, keepdims=True) + 1e-05)
    return center * scale, scale


def norm_back(grad, unit, scale, gain):
    scaled = grad * gain
    first_mean = jnp.mean(scaled, axis=1, keepdims=True)
    second_mean = jnp.mean(scaled * unit, axis=1, keepdims=True)
    return scale * (scaled - first_mean - unit * second_mean)


def call(body, outs, scratch, places, limit, microseconds):
    spaces = {"s": pltpu.SMEM, "v": pltpu.VMEM, "h": pltpu.HBM}
    return pl.pallas_call(
        body,
        out_shape=[jax.ShapeDtypeStruct(shape, kind) for shape, kind in outs],
        in_specs=[pl.BlockSpec(memory_space=spaces[place]) for place in places],
        out_specs=[pl.BlockSpec(memory_space=pltpu.VMEM)] * len(outs),
        scratch_shapes=list(scratch),
        compiler_params=pltpu.CompilerParams(vmem_limit_bytes=limit * MIB),
        cost_estimate=pl.CostEstimate(
            flops=microseconds * 10**9, bytes_accessed=0, transcendentals=0
        ),
    )


def widen(weight):
    rows = weight.shape[0]
    gap = jnp.zeros((rows, LANES - HEAD_DIM), weight.dtype)
    pieces = []
    for head in range(HEADS):
        pieces += [weight[:, head * HEAD_DIM : (head + 1) * HEAD_DIM], gap]
    return jnp.concatenate(pieces, axis=1)


def widen_rows(weight):
    gap = jnp.zeros((LANES - HEAD_DIM, weight.shape[1]), weight.dtype)
    pieces = []
    for head in range(HEADS):
        pieces += [weight[head * HEAD_DIM : (head + 1) * HEAD_DIM], gap]
    return jnp.concatenate(pieces, axis=0)


def narrow(wide):
    return jnp.concatenate(
        [wide[:, h * LANES : h * LANES + HEAD_DIM] for h in range(HEADS)], axis=1
    )


def narrow_rows(wide):
    return jnp.concatenate([wide[h * LANES : h * LANES + HEAD_DIM] for h in range(HEADS)], axis=0)


def segment_rows(seg_ref, first_place, count):
    spread = lax.broadcasted_iota(jnp.int32, (16, count), 0)
    places = lax.broadcasted_iota(jnp.int32, (16, count), 1) + first_place
    begin = jnp.zeros((16, count), jnp.int32)
    end = jnp.zeros((16, count), jnp.int32)
    edge = jnp.int32(0)
    for j in range(SEGS):
        begin = jnp.where(spread == j, edge, begin)
        edge = edge + seg_ref[0, j]
        end = jnp.where(spread == j, edge, end)
    return spread, (places >= begin) & (places < end)


def head_selector():
    rows = lax.broadcasted_iota(jnp.int32, (16, WIDE), 0)
    lanes = lax.broadcasted_iota(jnp.int32, (16, WIDE), 1)
    return low(jnp.where((lanes >> 7) == rows, 1.0, 0.0))


def start_kernel(me_ref, spot):
    rows = lax.broadcasted_iota(jnp.int32, spot.shape, 0)
    spot[...] = jnp.where(rows == 0, me_ref[0], me_ref[1])


def project(rows_in, gain, code, wk_pad, wv_t, at, normed, normed_t, k_aug, vt):
    count = rows_in.shape[0]
    unit, _ = unit_rows(high(rows_in))
    value = low(unit * gain)
    flipped = value.T
    normed[at : at + count, :] = value
    normed_t[:, at : at + count] = flipped
    wide = low(dot(value, wk_pad))
    k_aug[at : at + count, :] = wide + jnp.concatenate([code] * HEADS, axis=1)
    turned = low(dot(wv_t, flipped))
    for h in range(HEADS):
        vt[h * TALL : h * TALL + HEAD_DIM, at : at + count] = turned[h * HEAD_DIM : (h + 1) * HEAD_DIM]
        vt[h * TALL + HEAD_DIM : (h + 1) * TALL, at : at + count] = jnp.ones((16, count), BF)


def raw_attention(q_aug, k_aug, vt, before, part):
    for h in range(HEADS):
        lanes = slice(h * LANES, (h + 1) * LANES)
        tall = slice(h * TALL, (h + 1) * TALL)
        p = low(jnp.exp(dot_nt(k_aug[:, lanes], q_aug[:, lanes])))
        got = dot(vt[tall, :], p)
        part[tall, :] = got if before is None else got + before[tall, :]


def exact_attention(q_aug, parts, self_rows, vt_own, scores, o_t, lse_out):
    step = 256

    def one_head(h, _):
        lanes = pl.ds(pl.multiple_of(h * LANES, LANES), LANES)
        tall = pl.ds(pl.multiple_of(h * TALL, 16), HEAD_DIM)
        q_h = q_aug[:, lanes]
        self_h = self_rows[pl.ds(h, 1), :]
        top = self_h
        first = 0
        for k_part, _ in parts:

            def score(c, top, k_part=k_part, first=first):
                at = pl.multiple_of(c * step, step)
                part = dot_nt(k_part[pl.ds(at, step), lanes], q_h)
                scores[pl.ds(first + at, step), :] = part
                return jnp.maximum(top, jnp.max(part, axis=0, keepdims=True))

            top = lax.fori_loop(0, k_part.shape[0] // step, score, top)
            first += k_part.shape[0]
        p_self = jnp.exp(self_h - top)
        total = p_self
        acc = high(low(p_self)) * high(vt_own[tall, :])
        first = 0
        for _, vt_part in parts:

            def weigh(c, carry, vt_part=vt_part, first=first):
                total, acc = carry
                at = pl.multiple_of(c * step, step)
                p = jnp.exp(scores[pl.ds(first + at, step), :] - top)
                total = total + jnp.sum(p, axis=0, keepdims=True)
                return total, acc + dot(vt_part[tall, pl.ds(at, step)], low(p))

            total, acc = lax.fori_loop(0, vt_part.shape[1] // step, weigh, (total, acc))
            first += vt_part.shape[1]
        o_t[pl.ds(pl.multiple_of(h * LANES, LANES), HEAD_DIM), :] = acc / total
        lse_out[pl.ds(h, 1), :] = top + jnp.log(total)
        return 0

    lax.fori_loop(0, HEADS, one_head, 0)


def placed(rows16, first):
    upper = low(rows16)
    rest = rows16 - high(upper)
    middle = low(rest)
    parts = (upper, middle, low(rest - high(middle)))
    rows = lax.broadcasted_iota(jnp.int32, (16, WIDE), 0)
    lanes = lax.broadcasted_iota(jnp.int32, (16, WIDE), 1)
    total = 0.0
    for i, piece in enumerate(parts):
        picked = ((lanes >> 7) == rows) & ((lanes & (LANES - 1)) == first + i)
        total = total + dot_tn(piece, low(jnp.where(picked, 1.0, 0.0)))
    return low(total)


def lane_codes(rows_code):
    picked = lax.broadcasted_iota(jnp.int32, (16, LANES), 1) - HEAD_DIM
    picked = (picked == lax.broadcasted_iota(jnp.int32, (16, LANES), 0)) & (picked <= SEGS + 3)
    return low(dot_tn(low(rows_code), low(jnp.where(picked, 1.0, 0.0))))


def first_kernel(
    own_rows,
    spot, seg, core_rows, tokens, valid, gain_one, wq, wk, wv, wo, w_cross, b_cross, cot, w_ens2,
    wq_pad, wk_pad, wv_pad, wo_pad, wk_t, wv_t, codes, real, counted,
    normed, normed_t, q_aug, k_aug, vt, part, self_scores, crossed, d_joint,
):
    me = jnp.max(spot[0:1, :])
    for step in range(4):
        at = pl.multiple_of((me ^ step) * own_rows, own_rows)
        spread, inside = segment_rows(seg, at, own_rows)
        ok = valid[:, pl.ds(at, own_rows)] > 0
        code = jnp.where(inside, HUGE, 0.0)
        code = jnp.where(spread == SEGS, jnp.where(ok, 0.0, HUGE), code)
        code = jnp.where(spread > SEGS, 1.0, code)
        codes[step * own_rows : (step + 1) * own_rows, :] = lane_codes(code)
        real[:, step * own_rows : (step + 1) * own_rows] = jnp.where(ok, 1.0, 0.0)
        counted[:, step * own_rows : (step + 1) * own_rows] = low(jnp.where(inside & ok, 1.0, 0.0))
    wq_pad[...] = low(widen(high(wq[...])))
    wk_pad[...] = low(widen(high(wk[...])))
    wv_pad[...] = low(widen(high(wv[...])))
    wo_pad[...] = low(widen_rows(high(wo[...])))
    wk_t[...] = wk[...].T
    wv_t[...] = wv[...].T
    gain = gain_one[...]
    for step, rows_in in enumerate((tokens, core_rows)):
        at = step * own_rows
        project(
            rows_in[...], gain, codes[at : at + own_rows, :], wk_pad[...], wv_t[...], at,
            normed, normed_t, k_aug, vt,
        )
    spread, inside = segment_rows(seg, pl.multiple_of(me * own_rows, own_rows), own_rows)
    own_code = lane_codes(jnp.where(inside | (spread > SEGS), 0.0, 1.0))
    scaled = low(dot(normed[:own_rows, :], wq_pad[...]) * 0.125)
    q_aug[...] = scaled + jnp.concatenate([own_code] * HEADS, axis=1)
    raw_attention(q_aug, k_aug, vt, None, part)
    lanes_own = lax.broadcasted_iota(jnp.int32, (own_rows, WIDE), 1) & (LANES - 1)
    product = high(q_aug[...]) * high(k_aug[:own_rows, :])
    self_scores[...] = head_sums(head_selector(), jnp.where(lanes_own < HEAD_DIM, product, 0.0))
    crossed[...] = dot(normed[:own_rows, :], w_cross[...]) + b_cross[...]
    d_joint[...] = dot_nt(cot[...], w_ens2[...])


def middle_kernel(
    own_rows,
    y_rows, gain_one, codes, wk_pad, wv_t, q_aug, part_a,
    normed, normed_t, k_aug, vt, part,
):
    project(
        y_rows[...], gain_one[...], codes[2 * own_rows : 3 * own_rows, :], wk_pad[...], wv_t[...], 0,
        normed, normed_t, k_aug, vt,
    )
    raw_attention(q_aug, k_aug, vt, part_a, part)


def forward_kernel(
    own_rows,
    spot, far_rows, codes, real, counted, tokens, cot,
    gain_one, wk_pad, wo_pad, wv_t,
    w_mix, w_ens1, gain_two, w_up, b_up, d_joint,
    normed_a, normed_y, q_aug, k_a, k_y, vt_a, vt_y, part_y, self_scores, crossed,
    payload, d_first_out, vectors, normed_f, normed_tf, k_f,
    first_out, active_out, normed_two_out, d_modules_out, att_out, lse_out, member_out, counts_out,
    vt_f, part_f, scores, o_t, self_rows,
):
    project(
        far_rows[:own_rows, :], gain_one[...], codes[3 * own_rows :, :], wk_pad[...], wv_t[...], 0,
        normed_f, normed_tf, k_f, vt_f,
    )
    normed_own = normed_a[:own_rows, :]
    own_real = real[:, :own_rows] > 0
    o_t[...] = jnp.zeros_like(o_t)
    lse_out[...] = jnp.zeros_like(lse_out)
    raw_attention(q_aug, k_f, vt_f, part_y, part_f)
    vt_own = vt_a[:, :own_rows]
    smallest, largest = jnp.inf, -jnp.inf
    for h in range(HEADS):
        p_self = jnp.where(own_real, 0.0, jnp.exp(self_scores[h : h + 1, :]))
        both = part_f[h * TALL : (h + 1) * TALL, :]
        total = both[HEAD_DIM : HEAD_DIM + 1] + p_self
        acc = both[:HEAD_DIM] + high(low(p_self)) * high(vt_own[h * TALL : h * TALL + HEAD_DIM])
        o_t[h * LANES : h * LANES + HEAD_DIM, :] = acc / total
        lse_out[h : h + 1, :] = jnp.log(total)
        smallest = jnp.minimum(smallest, total)
        largest = jnp.maximum(largest, total)
    fits = (jnp.min(smallest) > 1e-25) & (jnp.max(largest) < 1e30)

    @pl.when(jnp.logical_not(fits))
    def _():
        self_rows[...] = jnp.where(own_real, HUGE, self_scores[...])
        parts = ((k_a, vt_a), (k_y, vt_y), (k_f, vt_f))
        exact_attention(q_aug, parts, self_rows, vt_a.at[:, :own_rows], scores, o_t, lse_out)

    att = o_t[...].T
    att_out[...] = att
    att_low = low(att)

    modules = []
    for g in range(2):
        lanes = slice(g * 256, (g + 1) * 256)
        modules.append(low(dot(att_low[:, lanes], wo_pad[lanes, :])))
    modules.append(low(high(normed_own) * crossed[...]))
    counts = jnp.sum(high(counted[...]), axis=1, keepdims=True)
    counts = jnp.maximum(counts, 1.0)
    counts_out[...] = jnp.broadcast_to(counts, counts_out.shape)
    seg_sums = dot(counted[:, : 2 * own_rows], normed_a[...])
    seg_sums = seg_sums + dot(counted[:, 2 * own_rows : 3 * own_rows], normed_y[...])
    seg_sums = seg_sums + dot(counted[:, 3 * own_rows :], normed_f[...])
    seg_mean = low(seg_sums / counts)
    picked = lax.broadcasted_iota(jnp.int32, (LANES, 16), 0) - HEAD_DIM
    picked = (picked == lax.broadcasted_iota(jnp.int32, (LANES, 16), 1)) & (picked < SEGS)
    own_member = 1.0 - dot(q_aug[:, :LANES], low(jnp.where(picked, 1.0, 0.0)))
    own_lane = lax.broadcasted_iota(jnp.int32, (own_rows, 16), 1)
    own_member = low(jnp.where(own_lane < SEGS, own_member, 0.0))
    member_out[...] = own_member
    mixed = low(dot(own_member, seg_mean))
    modules.append(low(dot(mixed, w_mix[...])))
    first = high(tokens[...])
    for i in range(4):
        first = first + dot(modules[i], w_ens1[i * D : (i + 1) * D, :])
    first_out[...] = first
    unit_two, scale_two = unit_rows(first)
    normed_two = low(unit_two * gain_two[...])
    inner = dot(normed_two, w_up[...]) + b_up[...]
    cdf = 0.5 * (1.0 + lax.erf(inner * 0.7071067811865476))
    active = low(inner * cdf)
    slope = cdf + inner * jnp.exp(-0.5 * inner * inner) * 0.3989422804014327
    active_out[...] = active
    normed_two_out[...] = normed_two

    core, y_bit, x_bit, z_bit = bits_of(spot)
    order = y_bit * 8 + x_bit * 4 + z_bit * 2
    block = payload.shape[0] // 32
    place = [0]

    def put(grad):
        middle = grad.shape[0] // 2
        for i in range(middle // block):
            n = place[0]
            place[0] = n + 1
            place_at = n ^ order
            for side in range(2):
                start = pl.multiple_of(((side ^ core) * 16 + place_at) * block, block)
                first = side * middle + i * block
                payload[pl.ds(start, block), :] = low(grad[first : first + block])

    e2 = cot[...]
    put(dot_tn(active, e2))
    put(dot_tn(normed_two, e2))
    d_inner = low(d_joint[:, :FF] * slope)
    b_up_grad = jnp.sum(high(d_inner), axis=0, keepdims=True)
    grad_up = dot_tn(normed_two, d_inner)
    for i in range(FF // D):
        put(grad_up[:, i * D : (i + 1) * D])
    d_norm2 = d_joint[:, FF:] + dot_nt(d_inner, w_up[...])
    d_first = high(e2) + norm_back(d_norm2, unit_two, scale_two, gain_two[...])
    d_first_out[...] = d_first
    e1 = low(d_first)
    d_modules = []
    for i in range(4):
        put(dot_tn(modules[i], e1))
        d_modules.append(low(dot_nt(e1, w_ens1[i * D : (i + 1) * D, :])))
        d_modules_out[:, i * D : (i + 1) * D] = d_modules[i]
    out_grads = []
    for g in range(2):
        lanes = slice(g * 256, (g + 1) * 256)
        out_grads.append(dot_tn(att_low[:, lanes], d_modules[g]))
    put(narrow_rows(jnp.concatenate(out_grads, axis=0)))
    put(dot_tn(normed_own, low(high(d_modules[2]) * high(normed_own))))
    put(dot_tn(mixed, d_modules[3]))
    vectors[...] = jnp.zeros_like(vectors)
    for i in range(FF // D):
        vectors[i : i + 1, :] = b_up_grad[:, i * D : (i + 1) * D]
    vectors[5:6, :] = jnp.sum(d_norm2 * unit_two, axis=0, keepdims=True)


def side_kernel(
    own_rows,
    d_modules, att, lse,
    normed_a, normed_y, normed_f, normed_ta, normed_ty, normed_tf, q_aug, self_scores, real,
    wv_pad, wk_t, wo_pad,
    v_all, kt_all, q_back, grad_att, pself_out, dself_out,
):
    v_lane = lax.broadcasted_iota(jnp.int32, (1, WIDE), 1) & (LANES - 1)
    v_ones = jnp.where((v_lane >= HEAD_DIM) & (v_lane < HEAD_DIM + 3), 1.0, 0.0)
    at = 0
    for normed, flipped in ((normed_a, normed_ta), (normed_y, normed_ty), (normed_f, normed_tf)):
        count = normed.shape[0]
        v_all[at : at + count, :] = low(dot(normed[...], wv_pad[...]) + v_ones)
        kt_all[:, at : at + count] = low(dot(wk_t[...], flipped[...]))
        at += count
    d_att = []
    for g in range(2):
        lanes = slice(g * 256, (g + 1) * 256)
        d_att.append(low(dot_nt(d_modules[:, g * D : (g + 1) * D], wo_pad[lanes, :])))
    d_att = jnp.concatenate(d_att, axis=1)
    heads16 = head_selector()
    delta = head_sums(heads16, high(d_att) * att[...])
    grad_att[...] = d_att + placed(-delta, HEAD_DIM)
    q_back[...] = q_aug[...] + placed(-lse[...], HEAD_DIM + SEGS + 1)
    p_self = jnp.where(real[:, :own_rows] > 0, 0.0, jnp.exp(self_scores[...] - lse[...]))
    dp_self = head_sums(heads16, high(d_att) * high(v_all[:own_rows, :]))
    pself_out[...] = low(p_self)
    dself_out[...] = low(p_self * (dp_self - delta))


def head_kernel(
    own_rows, h,
    q_back, k_a, k_y, k_f, v_all, kt_all, grad_att, pself, dself,
    *rest,
):
    dk_out, dv_out, dq_out = rest[-3:]
    row16 = lax.broadcasted_iota(jnp.int32, (16, LANES), 0)
    spread = low(jnp.where(row16 == h, 1.0, 0.0))
    lanes = slice(h * LANES, (h + 1) * LANES)
    rows_h = slice(h * HEAD_DIM, (h + 1) * HEAD_DIM)
    q_h = q_back[:, lanes]
    g_h = grad_att[:, lanes]
    acc = high(dself[h : h + 1, :]) * high(kt_all[rows_h, :own_rows])
    first = 0
    for k_part in (k_a, k_y, k_f):
        count = k_part.shape[0]
        at = slice(first, first + count)
        p = jnp.exp(dot_nt(k_part[:, lanes], q_h))
        ds = low(p * dot_nt(v_all[at, lanes], g_h))
        dv = dot(low(p), g_h)
        dk = dot(ds, q_h)
        if first == 0:
            dk_self = dot_tn(dself[...], spread) * high(q_h)
            dv_self = dot_tn(pself[...], spread) * high(g_h)
            dk_out[:own_rows, :] = low(dk[:own_rows] + dk_self)
            dv_out[:own_rows, :] = low(dv[:own_rows] + dv_self)
            dk_out[own_rows:count, :] = low(dk[own_rows:])
            dv_out[own_rows:count, :] = low(dv[own_rows:])
        else:
            dk_out[at, :] = low(dk)
            dv_out[at, :] = low(dv)
        acc = acc + dot(kt_all[rows_h, at], ds)
        first += count
    dq_out[...] = low(acc * 0.125)


def rows_kernel(
    own_rows,
    dk0, dk1, dk2, dk3, dv0, dv1, dv2, dv3, dq0, dq1, dq2, dq3, normed_a, normed_y, normed_f, counted, d_modules, crossed,
    w_cross, w_mix, own_member, counts, gain_one, wq, wk_pad, wv_pad, vectors,
    *rest,
):
    out, dq_out, dn = rest[-3:]
    d_two = high(d_modules[:, 2 * D : 3 * D])
    d_cross = low(d_two * high(normed_a[:own_rows, :]))
    dn_own = d_two * crossed[...] + dot_nt(d_cross, w_cross[...])
    b_cross_grad = jnp.sum(high(d_cross), axis=0, keepdims=True)
    d_mixed = dot_nt(d_modules[:, 3 * D :], w_mix[...])
    mixed_up = low(d_mixed)
    mixed_down = low(d_mixed - high(mixed_up))
    seg_grad = dot_tn(own_member[...], mixed_up) + dot_tn(own_member[...], mixed_down)
    seg_grad = seg_grad / counts[:, :1]
    half_keys = 2 * own_rows
    dq = jnp.concatenate([high(part[...]) for part in (dq0, dq1, dq2, dq3)], axis=0)
    dq_rows = low(dq.T)
    dq_out[...] = dq_rows
    dk_pairs = [jnp.concatenate([dk0[...], dk1[...]], axis=1), jnp.concatenate([dk2[...], dk3[...]], axis=1)]
    dv_pairs = [jnp.concatenate([dv0[...], dv1[...]], axis=1), jnp.concatenate([dv2[...], dv3[...]], axis=1)]
    up = low(seg_grad)
    down = low(seg_grad - high(up))
    for c in range(2):
        at = slice(c * half_keys, (c + 1) * half_keys)
        mixing = dot_tn(counted[:, at], up) + dot_tn(counted[:, at], down)
        dn[at, :] = mixing + (
            dot_nt(dk_pairs[0][at, :], wk_pad[:, :256])
            + dot_nt(dk_pairs[1][at, :], wk_pad[:, 256:])
            + dot_nt(dv_pairs[0][at, :], wv_pad[:, :256])
            + dot_nt(dv_pairs[1][at, :], wv_pad[:, 256:])
        )
    dn[:own_rows, :] = dn[:own_rows, :] + (dot_nt(dq_rows, wq[...]) + dn_own)
    gain_grad = jnp.sum(dn[:half_keys, :] * high(normed_a[...]), axis=0, keepdims=True)
    for i, normed in enumerate((normed_y, normed_f)):
        here = dn[(2 + i) * own_rows : (3 + i) * own_rows, :]
        gain_grad = gain_grad + jnp.sum(here * high(normed[...]), axis=0, keepdims=True)
    gain_grad = gain_grad / gain_one[...]
    count = out.shape[0] // 2
    for step in range(4):
        at = (step % 2) * count + (step // 2) * own_rows
        out[at : at + own_rows, :] = low(dn[step * own_rows : (step + 1) * own_rows, :])
    tail = lax.broadcasted_iota(jnp.int32, (16, D), 0)
    row = jnp.where(tail == 6, gain_grad, jnp.where(tail == 4, b_cross_grad, vectors[...]))
    out[count - 16 : count, :] = low(row)
    out[2 * count - 16 :, :] = low(row)


def weights_kernel(
    own_rows,
    spot,
    dk0, dk1, dk2, dk3, dv0, dv1, dv2, dv3, dq_rows, normed_ta, normed_ty, normed_tf,
    *rest,
):
    out = rest[-1]
    flips = ((normed_ta, 0), (normed_ty, 2), (normed_tf, 3))

    def key_grad(parts):
        pairs = [jnp.concatenate([parts[i][...], parts[i + 1][...]], axis=1) for i in (0, 2)]
        return narrow(
            jnp.concatenate(
                [
                    sum(
                        dot(flip[...], pair[at * own_rows : at * own_rows + flip.shape[1]])
                        for flip, at in flips
                    )
                    for pair in pairs
                ],
                axis=1,
            )
        )

    core, y_bit, x_bit, _ = bits_of(spot)
    order = core * 4 + y_bit * 2 + x_bit
    part = D // 8
    for i, grad in enumerate(
        (
            dot(normed_ta[:, :own_rows], dq_rows[...]),
            key_grad((dk0, dk1, dk2, dk3)),
            key_grad((dv0, dv1, dv2, dv3)),
        )
    ):
        for n in range(8):
            at = ((n ^ order) * 3 + i) * part
            out[pl.ds(pl.multiple_of(at, part), part), :] = low(grad[n * part : (n + 1) * part])


def finish_kernel(
    mine, other, tokens, d_first, gain_one, first, active, normed_two, w_ens2, *rest
):
    grad_tokens, out_rows, done = rest[-3:]
    out_rows[...] = first[...] + (dot(active[...], w_ens2[:FF, :]) + dot(normed_two[...], w_ens2[FF:, :]))
    unit, scale = unit_rows(high(tokens[...]))
    total = high(mine[...]) + high(other[...])
    grad_tokens[...] = d_first[...] + norm_back(total, unit, scale, gain_one[...])
    done[...] = mine[:16, :]


def unpack_kernel(spot, mine, other, *rest):
    attn_out, cross, mix, ens1, up, ens2, done = rest[-7:]
    core, y_bit, x_bit, z_bit = bits_of(spot)
    order = y_bit * 8 + x_bit * 4 + z_bit * 2
    block = mine.shape[0] // 16
    every = slice(None)
    jobs = [(ens2, 0, FF, every), (ens2, FF, D, every)]
    jobs += [(up, 0, D, slice(i * D, (i + 1) * D)) for i in range(FF // D)]
    jobs += [(ens1, i * D, D, every) for i in range(4)]
    jobs += [(attn_out, 0, D, every), (cross, 0, D, every), (mix, 0, D, every)]
    n = 0
    for to, first, count, columns in jobs:
        for i in range(count // 2 // block):
            place_at = n ^ order
            n += 1
            for side, source in ((core, mine), (1 - core, other)):
                at = pl.multiple_of(first + side * (count // 2) + i * block, block)
                value = source[pl.ds(pl.multiple_of(place_at * block, block), block), :]
                to[pl.ds(at, block), columns] = high(value)
    done[...] = mine[:16, :]


def unpack_small_kernel(spot, mine, other, vec, *rest):
    gain_one, query, key, value, b_cross, gain_two, b_up, done = rest[-8:]
    core, y_bit, x_bit, _ = bits_of(spot)
    order = y_bit * 2 + x_bit
    part = D // 8
    for side, source in ((core, mine), (1 - core, other)):
        for n in range(4):
            for i, to in enumerate((query, key, value)):
                at = pl.multiple_of((n ^ order) * 3 * part + i * part, part)
                here = pl.ds(pl.multiple_of((side * 4 + n) * part, part), part)
                to[here, :] = high(source[pl.ds(at, part), :])
    wide = high(vec[...])
    for i in range(FF // D):
        b_up[:, i * D : (i + 1) * D] = wide[i : i + 1]
    b_cross[...] = wide[4:5]
    gain_two[...] = wide[5:6]
    gain_one[...] = wide[6:7]
    done[...] = mine[:16, :]


def swap(value, axis, count, step):
    return lax.ppermute(value, axis, [(i, i ^ step) for i in range(count)])


def bits_of(spot):
    module, batch = jnp.max(spot[0:1, :]), jnp.max(spot[1:2, :])
    return module & 1, (module >> 1) & 1, batch & 1, (batch >> 1) & 1


def sum_kernel(counts, afters, *refs):
    inputs, outs = refs[: len(refs) - afters - len(counts)], refs[len(refs) - len(counts) :]
    at = 0
    for count, out in zip(counts, outs):
        total = high(inputs[0][at : at + count, :])
        for other in inputs[1:]:
            total = total + high(other[at : at + count, :])
        out[...] = low(total)
        at += count


def join_kernel(jobs, afters, *refs):
    out = refs[-1]
    at = 0
    for ref in refs[:jobs]:
        count = ref.shape[0]
        out[at : at + count, :] = ref[...]
        at += count


def added(one, two):
    return low(high(one) + high(two))


def shards(
    n_batch,
    n_module,
    tokens,
    seg_lengths,
    valid,
    cotangent,
    gain_one,
    w_query,
    w_key,
    w_value,
    w_attn_out,
    w_cross,
    b_cross,
    w_mix,
    w_ens1,
    gain_two,
    w_up,
    b_up,
    w_ens2,
):
    module = lax.axis_index("module")
    batch = lax.axis_index("batch")
    own = tokens.shape[0]
    rows = valid.shape[0]
    me = jnp.stack([module, batch]).astype(jnp.int32)

    def by_core(value):
        return swap(value, "module", n_module, 1)

    def by_y(value):
        return swap(value, "module", n_module, 2)

    def by_batch(value, step):
        return swap(value, "batch", n_batch, step)

    from_core = by_core(tokens)
    from_y = by_y(tokens)
    square = ((D, D), BF)
    keys = 2 * own
    row = ((1, D), F32)
    gain_row, valid_row = gain_one.reshape(1, D), valid.reshape(1, rows)
    (spot,) = call(start_kernel, [((8, LANES), jnp.int32)], [], "s", 4, 20)(me)
    (
        wq_pad, wk_pad, wv_pad, wo_pad, wk_t, wv_t, codes, real, counted,
        normed_a, normed_ta, q_aug, k_a, vt_a, part_a, self_scores, crossed, d_joint,
    ) = call(
        functools.partial(first_kernel, own),
        [
            ((D, WIDE), BF), ((D, WIDE), BF), ((D, WIDE), BF), ((WIDE, D), BF), square, square,
            ((rows, LANES), BF), ((1, rows), F32), ((16, rows), BF),
            ((keys, D), BF), ((D, keys), BF), ((own, WIDE), BF), ((keys, WIDE), BF),
            ((HEADS * TALL, keys), BF), ((HEADS * TALL, own), F32), ((16, own), F32), ((own, D), F32),
            ((own, FF + D), F32),
        ],
        [], "vs" + "v" * 12, 16, 5,
    )(
        spot, seg_lengths, from_core, tokens, valid_row, gain_row, w_query, w_key, w_value, w_attn_out,
        w_cross, b_cross.reshape(1, D), cotangent, w_ens2,
    )
    from_far = by_core(jnp.concatenate([from_y, normed_a[:16]], axis=0))
    normed_y, normed_ty, k_y, vt_y, part_y = call(
        functools.partial(middle_kernel, own),
        [((own, D), BF), ((D, own), BF), ((own, WIDE), BF), ((HEADS * TALL, own), BF), ((HEADS * TALL, own), F32)],
        [], "v" * 7, 16, 2,
    )(from_y, gain_row, codes, wk_pad, wv_t, q_aug, part_a)
    (
        payload, d_first, vectors, normed_f, normed_tf, k_f,
        first, active, normed_two, d_modules, att, lse, own_member, counts,
    ) = call(
        functools.partial(forward_kernel, own),
        [
            ((16 * D, D), BF), ((own, D), F32), ((16, D), F32), ((own, D), BF), ((D, own), BF), ((own, WIDE), BF),
            ((own, D), F32), ((own, FF), BF), ((own, D), BF), ((own, 4 * D), BF), ((own, WIDE), F32), ((16, own), F32),
            ((own, 16), BF), ((16, LANES), F32),
        ],
        [
            pltpu.VMEM((HEADS * TALL, own), BF), pltpu.VMEM((HEADS * TALL, own), F32), pltpu.VMEM((rows, own), F32),
            pltpu.VMEM((WIDE, own), F32), pltpu.VMEM((16, own), F32),
        ],
        "v" * 27, 32, 8,
    )(
        spot, from_far, codes, real, counted, tokens, cotangent, gain_row, wk_pad, wo_pad, wv_t,
        w_mix, w_ens1, gain_two.reshape(1, D), w_up, b_up.reshape(1, FF), d_joint,
        normed_a, normed_y, q_aug, k_a, k_y, vt_a, vt_y, part_y, self_scores, crossed,
    )
    big_got = by_core(payload[payload.shape[0] // 2 :])
    v_all, kt_all, q_back, grad_att, pself, dself = call(
        functools.partial(side_kernel, own),
        [
            ((rows, WIDE), BF), ((D, rows), BF), ((own, WIDE), BF), ((own, WIDE), BF), ((16, own), BF), ((16, own), BF),
        ],
        [], "v" * 15, 16, 3,
    )(
        d_modules, att, lse, normed_a, normed_y, normed_f, normed_ta, normed_ty, normed_tf, q_aug, self_scores, real,
        wv_pad, wk_t, wo_pad,
    )

    def head(index, *after, cost=0):
        args = [q_back, k_a, k_y, k_f, v_all, kt_all, grad_att, pself, dself, *after]
        return call(
            functools.partial(head_kernel, own, index),
            [((rows, LANES), BF), ((rows, LANES), BF), ((HEAD_DIM, own), BF)],
            [], "v" * len(args), 16, cost,
        )(*args)

    def summed(counts, parts, *after, cost=0):
        outs = [((count, D), BF) for count in counts]
        args = list(parts) + list(after)
        body = functools.partial(sum_kernel, counts, len(after))
        return call(body, outs, [], "v" * len(args), 8, cost)(*args)

    def joined(parts, *after, cost=0):
        count = sum(part.shape[0] for part in parts)
        body = functools.partial(join_kernel, len(parts), len(after))
        args = list(parts) + list(after)
        return call(body, [((count, D), BF)], [], "v" * len(args), 8, cost)(*args)[0]

    def by_both(value):
        pairs = [(i, i ^ (n_module + 2)) for i in range(n_batch * n_module)]
        return lax.ppermute(value, ("batch", "module"), pairs)

    def around(values):
        return by_batch(values[0], 1), by_y(values[1]), by_both(values[2])

    steps = [1 << place for place in range(1, n_batch.bit_length() - 1)]

    def through(value, got, *after, cost=0):
        for step in steps[2:] + [0]:
            (value,) = summed([value.shape[0]], [value, got], *after, cost=cost)
            got = by_batch(value, step) if step else None
        return value

    size = payload.shape[0] // 8
    half = size // 2
    part = D // 8
    count = 2 * own + 16
    rows_q = 3 * part + 16
    wide = ((D, D), F32)
    mine, *outward = summed([size] * 4, [payload, big_got], pself, cost=0)
    xy_got = around(outward)
    dk0, dv0, dq0 = head(0, mine, cost=2)
    dk1, dv1, dq1 = head(1, dq0, cost=2)
    dk2, dv2, dq2 = head(2, dq1, cost=2)
    dk3, dv3, dq3 = head(3, dq2, cost=2)
    args = [
        dk0, dk1, dk2, dk3, dv0, dv1, dv2, dv3, dq0, dq1, dq2, dq3, normed_a, normed_y, normed_f, counted,
        d_modules, crossed, w_cross, w_mix, own_member, counts, gain_row, w_query, wk_pad, wv_pad, vectors,
    ]
    shared, dq_rows = call(
        functools.partial(rows_kernel, own),
        [((2 * count, D), BF), ((own, D), BF)],
        [pltpu.VMEM((rows, D), F32)],
        "v" * len(args), 16, 3,
    )(*args)
    ab, ab_send = summed([half] * 2, [mine, *xy_got], dq_rows, cost=0)
    z1_got = by_batch(ab_send, steps[0])
    shared_got = by_core(shared[count:])
    args = [
        spot, dk0, dk1, dk2, dk3, dv0, dv1, dv2, dv3, dq_rows, normed_ta, normed_ty, normed_tf, ab,
    ]
    (q,) = call(
        functools.partial(weights_kernel, own), [((24 * part, D), BF)], [], "v" * len(args), 16, 3
    )(*args)
    (ab1,) = summed([half], [ab, z1_got], q, cost=0)
    z2_got = by_batch(ab1, steps[1])
    q_out = joined([q[12 * part :]], ab1, cost=0)
    q_core = by_core(q_out)
    dn, dn_send, vec = summed([own, own, 16], [shared, shared_got], q, cost=0)
    dn_got = by_y(dn_send)
    args = [dn, dn_got, tokens, d_first, gain_row, first, active, normed_two, w_ens2, ab1]
    grad_tokens, out_rows, done = call(
        finish_kernel, [((own, D), F32), ((own, D), F32), ((16, D), BF)], [], "v" * len(args), 16, 6
    )(*args)
    blocks = summed([3 * part] * 4, [q, q_core], ab1, cost=0)
    q0, *sends = [joined([block, vec]) for block in blocks]
    q_xy = around(sends)
    ab2 = through(ab1, z2_got, sends[2], done, cost=4)
    back_got = by_batch(ab2, steps[0])
    (q1,) = summed([rows_q], [q0, *q_xy], ab2, cost=3)
    q_z1 = by_batch(q1, steps[0])
    mine2 = joined([ab2, back_got], q1, cost=2)
    xy_back = around([mine2] * 3)
    (q2,) = summed([rows_q], [q1, q_z1], mine2, cost=3)
    q_z2 = by_batch(q2, steps[1])
    q3 = through(q2, q_z2, cost=0)
    q4 = q3[: 3 * part]
    q_back_got = around([q4] * 3)
    big = joined([mine2, *xy_back], q3, cost=0)
    big_got = by_core(big)
    args = [spot, big, big_got]
    attn_out, cross, mix, ens1, up, ens2, done_big = call(
        unpack_kernel,
        [wide, wide, wide, ((4 * D, D), F32), ((D, FF), F32), ((FF + D, D), F32), ((16, D), BF)],
        [], "v" * len(args), 16, 3,
    )(*args)
    q5 = joined([q4, *q_back_got], done_big, cost=0)
    q_last = by_core(q5)
    args = [spot, q5, q_last, q3[3 * part :], done_big]
    gain_one_g, query, key, value, b_cross_g, gain_two_g, b_up_g, done_small = call(
        unpack_small_kernel, [row, wide, wide, wide, row, row, ((1, FF), F32), ((16, D), BF)],
        [], "v" * len(args), 16, 2,
    )(*args)
    return (
        out_rows, grad_tokens, gain_one_g.reshape(D), query, key, value, attn_out, cross, b_cross_g.reshape(D), mix,
        ens1, gain_two_g.reshape(D), up, b_up_g.reshape(FF), ens2,
    )


def solution(mesh):
    rows = P(("batch", "module"), None)
    in_specs = (rows, P("batch", None), P("batch"), rows) + (P(),) * 13
    out_specs = (rows, rows) + (P(),) * 13
    body = functools.partial(shards, mesh.shape["batch"], mesh.shape["module"])
    return jax.shard_map(body, mesh=mesh, in_specs=in_specs, out_specs=out_specs, check_vma=False)
```

```python
import functools

import jax
import jax.numpy as jnp
from jax import lax
from jax.experimental import pallas as pl
from jax.experimental.pallas import tpu as pltpu
from jax.sharding import PartitionSpec as P

D = 256
HEADS = 4
HEAD_DIM = 64
FF = 1024
SEGS = 8
LANES = 128
WIDE = HEADS * LANES
HUGE = -1e30
TALL = HEAD_DIM + 16
BF = jnp.bfloat16
F32 = jnp.float32
MIB = 1024 * 1024


def low(v):
    return v.astype(BF)


def high(v):
    return v.astype(F32)


def dot(a, b):
    return jnp.dot(a, b, preferred_element_type=F32)


def dot_nt(a, b):
    return lax.dot_general(a, b, (((1,), (1,)), ((), ())), preferred_element_type=F32)


def dot_tn(a, b):
    return lax.dot_general(a, b, (((0,), (0,)), ((), ())), preferred_element_type=F32)


def head_sums(selector, product):
    upper = low(product)
    lower = low(product - high(upper))
    return dot_nt(selector, upper) + dot_nt(selector, lower)


def unit_rows(values):
    center = values - jnp.mean(values, axis=1, keepdims=True)
    scale = lax.rsqrt(jnp.mean(center * center, axis=1, keepdims=True) + 1e-05)
    return center * scale, scale


def norm_back(grad, unit, scale, gain):
    scaled = grad * gain
    first_mean = jnp.mean(scaled, axis=1, keepdims=True)
    second_mean = jnp.mean(scaled * unit, axis=1, keepdims=True)
    return scale * (scaled - first_mean - unit * second_mean)


def call(body, outs, scratch, places, limit, microseconds):
    spaces = {"s": pltpu.SMEM, "v": pltpu.VMEM, "h": pltpu.HBM}
    return pl.pallas_call(
        body,
        out_shape=[jax.ShapeDtypeStruct(shape, kind) for shape, kind in outs],
        in_specs=[pl.BlockSpec(memory_space=spaces[place]) for place in places],
        out_specs=[pl.BlockSpec(memory_space=pltpu.VMEM)] * len(outs),
        scratch_shapes=list(scratch),
        compiler_params=pltpu.CompilerParams(vmem_limit_bytes=limit * MIB),
        cost_estimate=pl.CostEstimate(
            flops=microseconds * 10**9, bytes_accessed=0, transcendentals=0
        ),
    )


def widen(weight):
    rows = weight.shape[0]
    gap = jnp.zeros((rows, LANES - HEAD_DIM), weight.dtype)
    pieces = []
    for head in range(HEADS):
        pieces += [weight[:, head * HEAD_DIM : (head + 1) * HEAD_DIM], gap]
    return jnp.concatenate(pieces, axis=1)


def widen_rows(weight):
    gap = jnp.zeros((LANES - HEAD_DIM, weight.shape[1]), weight.dtype)
    pieces = []
    for head in range(HEADS):
        pieces += [weight[head * HEAD_DIM : (head + 1) * HEAD_DIM], gap]
    return jnp.concatenate(pieces, axis=0)


def narrow_rows(wide):
    return jnp.concatenate([wide[h * LANES : h * LANES + HEAD_DIM] for h in range(HEADS)], axis=0)


def segment_rows(seg_ref, first_place, count):
    spread = lax.broadcasted_iota(jnp.int32, (16, count), 0)
    places = lax.broadcasted_iota(jnp.int32, (16, count), 1) + first_place
    begin = jnp.zeros((16, count), jnp.int32)
    end = jnp.zeros((16, count), jnp.int32)
    edge = jnp.int32(0)
    for j in range(SEGS):
        begin = jnp.where(spread == j, edge, begin)
        edge = edge + seg_ref[0, j]
        end = jnp.where(spread == j, edge, end)
    return spread, (places >= begin) & (places < end)


def head_selector():
    rows = lax.broadcasted_iota(jnp.int32, (16, WIDE), 0)
    lanes = lax.broadcasted_iota(jnp.int32, (16, WIDE), 1)
    return low(jnp.where((lanes >> 7) == rows, 1.0, 0.0))


def start_kernel(me_ref, spot):
    rows = lax.broadcasted_iota(jnp.int32, spot.shape, 0)
    spot[...] = jnp.where(rows == 0, me_ref[0], me_ref[1])


def project(rows_in, gain, code, wk_pad, wv_t, at, normed, normed_t, k_aug, vt):
    count = rows_in.shape[0]
    unit, _ = unit_rows(high(rows_in))
    value = low(unit * gain)
    flipped = value.T
    normed[at : at + count, :] = value
    normed_t[:, at : at + count] = flipped
    wide = low(dot(value, wk_pad))
    k_aug[at : at + count, :] = wide + jnp.concatenate([code] * HEADS, axis=1)
    turned = low(dot(wv_t, flipped))
    for h in range(HEADS):
        vt[h * TALL : h * TALL + HEAD_DIM, at : at + count] = turned[h * HEAD_DIM : (h + 1) * HEAD_DIM]
        vt[h * TALL + HEAD_DIM : (h + 1) * TALL, at : at + count] = jnp.ones((16, count), BF)


def raw_attention(q_aug, k_aug, vt, before, part):
    for h in range(HEADS):
        lanes = slice(h * LANES, (h + 1) * LANES)
        tall = slice(h * TALL, (h + 1) * TALL)
        p = low(jnp.exp(dot_nt(k_aug[:, lanes], q_aug[:, lanes])))
        got = dot(vt[tall, :], p)
        part[tall, :] = got if before is None else got + before[tall, :]


def exact_attention(q_aug, parts, self_rows, vt_own, scores, o_t, lse_out):
    step = 256

    def one_head(h, _):
        lanes = pl.ds(pl.multiple_of(h * LANES, LANES), LANES)
        tall = pl.ds(pl.multiple_of(h * TALL, 16), HEAD_DIM)
        q_h = q_aug[:, lanes]
        self_h = self_rows[pl.ds(h, 1), :]
        top = self_h
        first = 0
        for k_part, _ in parts:

            def score(c, top, k_part=k_part, first=first):
                at = pl.multiple_of(c * step, step)
                part = dot_nt(k_part[pl.ds(at, step), lanes], q_h)
                scores[pl.ds(first + at, step), :] = part
                return jnp.maximum(top, jnp.max(part, axis=0, keepdims=True))

            top = lax.fori_loop(0, k_part.shape[0] // step, score, top)
            first += k_part.shape[0]
        p_self = jnp.exp(self_h - top)
        total = p_self
        acc = high(low(p_self)) * high(vt_own[tall, :])
        first = 0
        for _, vt_part in parts:

            def weigh(c, carry, vt_part=vt_part, first=first):
                total, acc = carry
                at = pl.multiple_of(c * step, step)
                p = jnp.exp(scores[pl.ds(first + at, step), :] - top)
                total = total + jnp.sum(p, axis=0, keepdims=True)
                return total, acc + dot(vt_part[tall, pl.ds(at, step)], low(p))

            total, acc = lax.fori_loop(0, vt_part.shape[1] // step, weigh, (total, acc))
            first += vt_part.shape[1]
        o_t[pl.ds(pl.multiple_of(h * LANES, LANES), HEAD_DIM), :] = acc / total
        lse_out[pl.ds(h, 1), :] = top + jnp.log(total)
        return 0

    lax.fori_loop(0, HEADS, one_head, 0)


def placed(rows16, first):
    upper = low(rows16)
    rest = rows16 - high(upper)
    middle = low(rest)
    parts = (upper, middle, low(rest - high(middle)))
    rows = lax.broadcasted_iota(jnp.int32, (16, WIDE), 0)
    lanes = lax.broadcasted_iota(jnp.int32, (16, WIDE), 1)
    total = 0.0
    for i, piece in enumerate(parts):
        picked = ((lanes >> 7) == rows) & ((lanes & (LANES - 1)) == first + i)
        total = total + dot_tn(piece, low(jnp.where(picked, 1.0, 0.0)))
    return low(total)


def lane_codes(rows_code):
    picked = lax.broadcasted_iota(jnp.int32, (16, LANES), 1) - HEAD_DIM
    picked = (picked == lax.broadcasted_iota(jnp.int32, (16, LANES), 0)) & (picked <= SEGS + 3)
    return low(dot_tn(low(rows_code), low(jnp.where(picked, 1.0, 0.0))))


def first_kernel(
    own_rows,
    spot, seg, core_rows, tokens, valid, gain_one, wq, wk, wv, wo, w_cross, b_cross, cot, w_ens2,
    wq_pad, wk_pad, wv_pad, wo_pad, wk_t, wv_t, codes, real, counted,
    normed, normed_t, q_aug, k_aug, vt, part, self_scores, crossed, d_joint,
):
    me = jnp.max(spot[0:1, :])
    for step in range(4):
        at = pl.multiple_of((me ^ step) * own_rows, own_rows)
        spread, inside = segment_rows(seg, at, own_rows)
        ok = valid[:, pl.ds(at, own_rows)] > 0
        code = jnp.where(inside, HUGE, 0.0)
        code = jnp.where(spread == SEGS, jnp.where(ok, 0.0, HUGE), code)
        code = jnp.where(spread > SEGS, 1.0, code)
        codes[step * own_rows : (step + 1) * own_rows, :] = lane_codes(code)
        real[:, step * own_rows : (step + 1) * own_rows] = jnp.where(ok, 1.0, 0.0)
        counted[:, step * own_rows : (step + 1) * own_rows] = low(jnp.where(inside & ok, 1.0, 0.0))
    wq_pad[...] = low(widen(high(wq[...])))
    wk_pad[...] = low(widen(high(wk[...])))
    wv_pad[...] = low(widen(high(wv[...])))
    wo_pad[...] = low(widen_rows(high(wo[...])))
    wk_t[...] = wk[...].T
    wv_t[...] = wv[...].T
    gain = gain_one[...]
    for step, rows_in in enumerate((tokens, core_rows)):
        at = step * own_rows
        project(
            rows_in[...], gain, codes[at : at + own_rows, :], wk_pad[...], wv_t[...], at,
            normed, normed_t, k_aug, vt,
        )
    spread, inside = segment_rows(seg, pl.multiple_of(me * own_rows, own_rows), own_rows)
    own_code = lane_codes(jnp.where(inside | (spread > SEGS), 0.0, 1.0))
    scaled = low(dot(normed[:own_rows, :], wq_pad[...]) * 0.125)
    q_aug[...] = scaled + jnp.concatenate([own_code] * HEADS, axis=1)
    raw_attention(q_aug, k_aug, vt, None, part)
    lanes_own = lax.broadcasted_iota(jnp.int32, (own_rows, WIDE), 1) & (LANES - 1)
    product = high(q_aug[...]) * high(k_aug[:own_rows, :])
    self_scores[...] = head_sums(head_selector(), jnp.where(lanes_own < HEAD_DIM, product, 0.0))
    crossed[...] = dot(normed[:own_rows, :], w_cross[...]) + b_cross[...]
    d_joint[...] = dot_nt(cot[...], w_ens2[...])


def middle_kernel(
    own_rows,
    y_rows, gain_one, codes, wk_pad, wv_t, q_aug, part_a,
    normed, normed_t, k_aug, vt, part,
):
    project(
        y_rows[...], gain_one[...], codes[2 * own_rows : 3 * own_rows, :], wk_pad[...], wv_t[...], 0,
        normed, normed_t, k_aug, vt,
    )
    raw_attention(q_aug, k_aug, vt, part_a, part)


def forward_kernel(
    own_rows,
    spot, far_rows, codes, real, counted, tokens, cot,
    gain_one, wk_pad, wo_pad, wv_t,
    w_mix, w_ens1, gain_two, w_up, b_up, d_joint,
    normed_a, normed_y, q_aug, k_a, k_y, vt_a, vt_y, part_y, self_scores, crossed,
    payload, d_first_out, vectors, normed_f, normed_tf, k_f,
    first_out, active_out, normed_two_out, d_modules_out, att_out, lse_out, member_out, counts_out,
    vt_f, part_f, scores, o_t, self_rows,
):
    project(
        far_rows[:own_rows, :], gain_one[...], codes[3 * own_rows :, :], wk_pad[...], wv_t[...], 0,
        normed_f, normed_tf, k_f, vt_f,
    )
    normed_own = normed_a[:own_rows, :]
    own_real = real[:, :own_rows] > 0
    o_t[...] = jnp.zeros_like(o_t)
    lse_out[...] = jnp.zeros_like(lse_out)
    raw_attention(q_aug, k_f, vt_f, part_y, part_f)
    vt_own = vt_a[:, :own_rows]
    smallest, largest = jnp.inf, -jnp.inf
    for h in range(HEADS):
        p_self = jnp.where(own_real, 0.0, jnp.exp(self_scores[h : h + 1, :]))
        both = part_f[h * TALL : (h + 1) * TALL, :]
        total = both[HEAD_DIM : HEAD_DIM + 1] + p_self
        acc = both[:HEAD_DIM] + high(low(p_self)) * high(vt_own[h * TALL : h * TALL + HEAD_DIM])
        o_t[h * LANES : h * LANES + HEAD_DIM, :] = acc / total
        lse_out[h : h + 1, :] = jnp.log(total)
        smallest = jnp.minimum(smallest, total)
        largest = jnp.maximum(largest, total)
    fits = (jnp.min(smallest) > 1e-25) & (jnp.max(largest) < 1e30)

    @pl.when(jnp.logical_not(fits))
    def _():
        self_rows[...] = jnp.where(own_real, HUGE, self_scores[...])
        parts = ((k_a, vt_a), (k_y, vt_y), (k_f, vt_f))
        exact_attention(q_aug, parts, self_rows, vt_a.at[:, :own_rows], scores, o_t, lse_out)

    att = o_t[...].T
    att_out[...] = att
    att_low = low(att)

    modules = []
    for g in range(2):
        lanes = slice(g * 256, (g + 1) * 256)
        modules.append(low(dot(att_low[:, lanes], wo_pad[lanes, :])))
    modules.append(low(high(normed_own) * crossed[...]))
    counts = jnp.sum(high(counted[...]), axis=1, keepdims=True)
    counts = jnp.maximum(counts, 1.0)
    counts_out[...] = jnp.broadcast_to(counts, counts_out.shape)
    seg_sums = dot(counted[:, : 2 * own_rows], normed_a[...])
    seg_sums = seg_sums + dot(counted[:, 2 * own_rows : 3 * own_rows], normed_y[...])
    seg_sums = seg_sums + dot(counted[:, 3 * own_rows :], normed_f[...])
    seg_mean = low(seg_sums / counts)
    picked = lax.broadcasted_iota(jnp.int32, (LANES, 16), 0) - HEAD_DIM
    picked = (picked == lax.broadcasted_iota(jnp.int32, (LANES, 16), 1)) & (picked < SEGS)
    own_member = 1.0 - dot(q_aug[:, :LANES], low(jnp.where(picked, 1.0, 0.0)))
    own_lane = lax.broadcasted_iota(jnp.int32, (own_rows, 16), 1)
    own_member = low(jnp.where(own_lane < SEGS, own_member, 0.0))
    member_out[...] = own_member
    mixed = low(dot(own_member, seg_mean))
    modules.append(low(dot(mixed, w_mix[...])))
    first = high(tokens[...])
    for i in range(4):
        first = first + dot(modules[i], w_ens1[i * D : (i + 1) * D, :])
    first_out[...] = first
    unit_two, scale_two = unit_rows(first)
    normed_two = low(unit_two * gain_two[...])
    inner = dot(normed_two, w_up[...]) + b_up[...]
    cdf = 0.5 * (1.0 + lax.erf(inner * 0.7071067811865476))
    active = low(inner * cdf)
    slope = cdf + inner * jnp.exp(-0.5 * inner * inner) * 0.3989422804014327
    active_out[...] = active
    normed_two_out[...] = normed_two

    core, y_bit, x_bit, z_bit = bits_of(spot)
    order = y_bit * 8 + x_bit * 4 + z_bit * 2
    block = payload.shape[0] // 32
    place = [0]

    def put(grad):
        middle = grad.shape[0] // 2
        for i in range(middle // block):
            n = place[0]
            place[0] = n + 1
            place_at = n ^ order
            for side in range(2):
                start = pl.multiple_of(((side ^ core) * 16 + place_at) * block, block)
                first = side * middle + i * block
                payload[pl.ds(start, block), :] = low(grad[first : first + block])

    e2 = cot[...]
    put(dot_tn(active, e2))
    put(dot_tn(normed_two, e2))
    d_inner = low(d_joint[:, :FF] * slope)
    b_up_grad = jnp.sum(high(d_inner), axis=0, keepdims=True)
    grad_up = dot_tn(normed_two, d_inner)
    for i in range(FF // D):
        put(grad_up[:, i * D : (i + 1) * D])
    d_norm2 = d_joint[:, FF:] + dot_nt(d_inner, w_up[...])
    d_first = high(e2) + norm_back(d_norm2, unit_two, scale_two, gain_two[...])
    d_first_out[...] = d_first
    e1 = low(d_first)
    d_modules = []
    for i in range(4):
        put(dot_tn(modules[i], e1))
        d_modules.append(low(dot_nt(e1, w_ens1[i * D : (i + 1) * D, :])))
        d_modules_out[:, i * D : (i + 1) * D] = d_modules[i]
    out_grads = []
    for g in range(2):
        lanes = slice(g * 256, (g + 1) * 256)
        out_grads.append(dot_tn(att_low[:, lanes], d_modules[g]))
    put(narrow_rows(jnp.concatenate(out_grads, axis=0)))
    put(dot_tn(normed_own, low(high(d_modules[2]) * high(normed_own))))
    put(dot_tn(mixed, d_modules[3]))
    vectors[...] = jnp.zeros_like(vectors)
    for i in range(FF // D):
        vectors[i : i + 1, :] = b_up_grad[:, i * D : (i + 1) * D]
    vectors[5:6, :] = jnp.sum(d_norm2 * unit_two, axis=0, keepdims=True)


def side_kernel(
    own_rows,
    d_modules, att, lse,
    normed_a, normed_y, normed_f, normed_ta, normed_ty, normed_tf, q_aug, self_scores, real,
    wv_pad, wk_t, wo_pad,
    v_all, kt_all, q_back, grad_att, pself_out, dself_out,
):
    v_lane = lax.broadcasted_iota(jnp.int32, (1, WIDE), 1) & (LANES - 1)
    v_ones = jnp.where((v_lane >= HEAD_DIM) & (v_lane < HEAD_DIM + 3), 1.0, 0.0)
    at = 0
    for normed, flipped in ((normed_a, normed_ta), (normed_y, normed_ty), (normed_f, normed_tf)):
        count = normed.shape[0]
        v_all[at : at + count, :] = low(dot(normed[...], wv_pad[...]) + v_ones)
        kt_all[:, at : at + count] = low(dot(wk_t[...], flipped[...]))
        at += count
    d_att = []
    for g in range(2):
        lanes = slice(g * 256, (g + 1) * 256)
        d_att.append(low(dot_nt(d_modules[:, g * D : (g + 1) * D], wo_pad[lanes, :])))
    d_att = jnp.concatenate(d_att, axis=1)
    heads16 = head_selector()
    delta = head_sums(heads16, high(d_att) * att[...])
    grad_att[...] = d_att + placed(-delta, HEAD_DIM)
    q_back[...] = q_aug[...] + placed(-lse[...], HEAD_DIM + SEGS + 1)
    p_self = jnp.where(real[:, :own_rows] > 0, 0.0, jnp.exp(self_scores[...] - lse[...]))
    dp_self = head_sums(heads16, high(d_att) * high(v_all[:own_rows, :]))
    pself_out[...] = low(p_self)
    dself_out[...] = low(p_self * (dp_self - delta))


def head_kernel(
    own_rows, h,
    q_back, k_a, k_y, k_f, v_all, kt_all, grad_att, pself, dself,
    *rest,
):
    dk_out, dv_out, dq_out = rest[-3:]
    row16 = lax.broadcasted_iota(jnp.int32, (16, LANES), 0)
    spread = low(jnp.where(row16 == h, 1.0, 0.0))
    lanes = slice(h * LANES, (h + 1) * LANES)
    rows_h = slice(h * HEAD_DIM, (h + 1) * HEAD_DIM)
    q_h = q_back[:, lanes]
    g_h = grad_att[:, lanes]
    lane = lax.broadcasted_iota(jnp.int32, (1, LANES), 1)
    q_half = jnp.where(lane < HEAD_DIM, high(q_h), 0.0)
    g_half = jnp.where(lane < HEAD_DIM, high(g_h), 0.0)
    if h % 2:
        q_half, g_half = pltpu.roll(q_half, HEAD_DIM, 1), pltpu.roll(g_half, HEAD_DIM, 1)
    q_low, g_low = low(q_half), low(g_half)
    acc = high(dself[h : h + 1, :]) * high(kt_all[rows_h, :own_rows])
    first = 0
    for k_part in (k_a, k_y, k_f):
        count = k_part.shape[0]
        at = slice(first, first + count)
        p = jnp.exp(dot_nt(k_part[:, lanes], q_h))
        ds = low(p * dot_nt(v_all[at, lanes], g_h))
        dv = dot(low(p), g_low)
        dk = dot(ds, q_low)
        if first == 0:
            dk_self = dot_tn(dself[...], spread) * q_half
            dv_self = dot_tn(pself[...], spread) * g_half
            dk_out[:own_rows, :] = low(dk[:own_rows] + dk_self)
            dv_out[:own_rows, :] = low(dv[:own_rows] + dv_self)
            dk_out[own_rows:count, :] = low(dk[own_rows:])
            dv_out[own_rows:count, :] = low(dv[own_rows:])
        else:
            dk_out[at, :] = low(dk)
            dv_out[at, :] = low(dv)
        acc = acc + dot(kt_all[rows_h, at], ds)
        first += count
    dq_out[...] = low(acc * 0.125)


def rows_kernel(
    own_rows,
    dk0, dk1, dk2, dk3, dv0, dv1, dv2, dv3, dq0, dq1, dq2, dq3, normed_a, normed_y, normed_f, counted, d_modules, crossed,
    w_cross, w_mix, own_member, counts, gain_one, wq, wk, wv, vectors,
    *rest,
):
    out, dq_out, dn = rest[-3:]
    d_two = high(d_modules[:, 2 * D : 3 * D])
    d_cross = low(d_two * high(normed_a[:own_rows, :]))
    dn_own = d_two * crossed[...] + dot_nt(d_cross, w_cross[...])
    b_cross_grad = jnp.sum(high(d_cross), axis=0, keepdims=True)
    d_mixed = dot_nt(d_modules[:, 3 * D :], w_mix[...])
    mixed_up = low(d_mixed)
    mixed_down = low(d_mixed - high(mixed_up))
    seg_grad = dot_tn(own_member[...], mixed_up) + dot_tn(own_member[...], mixed_down)
    seg_grad = seg_grad / counts[:, :1]
    half_keys = 2 * own_rows
    dq = jnp.concatenate([high(part[...]) for part in (dq0, dq1, dq2, dq3)], axis=0)
    dq_rows = low(dq.T)
    dq_out[...] = dq_rows
    dk = jnp.concatenate([dk0[...] + dk1[...], dk2[...] + dk3[...]], axis=1)
    dv = jnp.concatenate([dv0[...] + dv1[...], dv2[...] + dv3[...]], axis=1)
    up = low(seg_grad)
    down = low(seg_grad - high(up))
    for c in range(2):
        at = slice(c * half_keys, (c + 1) * half_keys)
        mixing = dot_tn(counted[:, at], up) + dot_tn(counted[:, at], down)
        dn[at, :] = mixing + (dot_nt(dk[at, :], wk[...]) + dot_nt(dv[at, :], wv[...]))
    dn[:own_rows, :] = dn[:own_rows, :] + (dot_nt(dq_rows, wq[...]) + dn_own)
    gain_grad = jnp.sum(dn[:half_keys, :] * high(normed_a[...]), axis=0, keepdims=True)
    for i, normed in enumerate((normed_y, normed_f)):
        here = dn[(2 + i) * own_rows : (3 + i) * own_rows, :]
        gain_grad = gain_grad + jnp.sum(here * high(normed[...]), axis=0, keepdims=True)
    gain_grad = gain_grad / gain_one[...]
    count = out.shape[0] // 2
    for step in range(4):
        at = (step % 2) * count + (step // 2) * own_rows
        out[at : at + own_rows, :] = low(dn[step * own_rows : (step + 1) * own_rows, :])
    tail = lax.broadcasted_iota(jnp.int32, (16, D), 0)
    row = jnp.where(tail == 6, gain_grad, jnp.where(tail == 4, b_cross_grad, vectors[...]))
    out[count - 16 : count, :] = low(row)
    out[2 * count - 16 :, :] = low(row)


def weights_kernel(
    own_rows,
    spot,
    dk0, dk1, dk2, dk3, dv0, dv1, dv2, dv3, dq_rows, normed_ta, normed_ty, normed_tf,
    *rest,
):
    out = rest[-1]
    flips = ((normed_ta, 0), (normed_ty, 2), (normed_tf, 3))

    def key_grad(parts):
        whole = [parts[i][...] + parts[i + 1][...] for i in (0, 2)]
        whole = jnp.concatenate(whole, axis=1)
        return sum(
            dot(flip[...], whole[at * own_rows : at * own_rows + flip.shape[1]]) for flip, at in flips
        )

    core, y_bit, x_bit, _ = bits_of(spot)
    order = core * 4 + y_bit * 2 + x_bit
    part = D // 8
    for i, grad in enumerate(
        (
            dot(normed_ta[:, :own_rows], dq_rows[...]),
            key_grad((dk0, dk1, dk2, dk3)),
            key_grad((dv0, dv1, dv2, dv3)),
        )
    ):
        for n in range(8):
            at = ((n ^ order) * 3 + i) * part
            out[pl.ds(pl.multiple_of(at, part), part), :] = low(grad[n * part : (n + 1) * part])


def finish_kernel(
    mine, other, tokens, d_first, gain_one, first, active, normed_two, w_ens2, *rest
):
    grad_tokens, out_rows, done = rest[-3:]
    out_rows[...] = first[...] + (dot(active[...], w_ens2[:FF, :]) + dot(normed_two[...], w_ens2[FF:, :]))
    unit, scale = unit_rows(high(tokens[...]))
    total = high(mine[...]) + high(other[...])
    grad_tokens[...] = d_first[...] + norm_back(total, unit, scale, gain_one[...])
    done[...] = mine[:16, :]


def unpack_kernel(spot, mine, other, *rest):
    attn_out, cross, mix, ens1, up, ens2, done = rest[-7:]
    core, y_bit, x_bit, z_bit = bits_of(spot)
    order = y_bit * 8 + x_bit * 4 + z_bit * 2
    block = mine.shape[0] // 16
    every = slice(None)
    jobs = [(ens2, 0, FF, every), (ens2, FF, D, every)]
    jobs += [(up, 0, D, slice(i * D, (i + 1) * D)) for i in range(FF // D)]
    jobs += [(ens1, i * D, D, every) for i in range(4)]
    jobs += [(attn_out, 0, D, every), (cross, 0, D, every), (mix, 0, D, every)]
    n = 0
    for to, first, count, columns in jobs:
        for i in range(count // 2 // block):
            place_at = n ^ order
            n += 1
            for side, source in ((core, mine), (1 - core, other)):
                at = pl.multiple_of(first + side * (count // 2) + i * block, block)
                value = source[pl.ds(pl.multiple_of(place_at * block, block), block), :]
                to[pl.ds(at, block), columns] = high(value)
    done[...] = mine[:16, :]


def unpack_small_kernel(spot, mine, other, vec, *rest):
    gain_one, query, key, value, b_cross, gain_two, b_up, done = rest[-8:]
    core, y_bit, x_bit, _ = bits_of(spot)
    order = y_bit * 2 + x_bit
    part = D // 8
    for side, source in ((core, mine), (1 - core, other)):
        for n in range(4):
            for i, to in enumerate((query, key, value)):
                at = pl.multiple_of((n ^ order) * 3 * part + i * part, part)
                here = pl.ds(pl.multiple_of((side * 4 + n) * part, part), part)
                to[here, :] = high(source[pl.ds(at, part), :])
    wide = high(vec[...])
    for i in range(FF // D):
        b_up[:, i * D : (i + 1) * D] = wide[i : i + 1]
    b_cross[...] = wide[4:5]
    gain_two[...] = wide[5:6]
    gain_one[...] = wide[6:7]
    done[...] = mine[:16, :]


def swap(value, axis, count, step):
    return lax.ppermute(value, axis, [(i, i ^ step) for i in range(count)])


def bits_of(spot):
    module, batch = jnp.max(spot[0:1, :]), jnp.max(spot[1:2, :])
    return module & 1, (module >> 1) & 1, batch & 1, (batch >> 1) & 1


def sum_kernel(counts, afters, *refs):
    inputs, outs = refs[: len(refs) - afters - len(counts)], refs[len(refs) - len(counts) :]
    at = 0
    for count, out in zip(counts, outs):
        total = high(inputs[0][at : at + count, :])
        for other in inputs[1:]:
            total = total + high(other[at : at + count, :])
        out[...] = low(total)
        at += count


def join_kernel(jobs, afters, *refs):
    out = refs[-1]
    at = 0
    for ref in refs[:jobs]:
        count = ref.shape[0]
        out[at : at + count, :] = ref[...]
        at += count


def added(one, two):
    return low(high(one) + high(two))


def shards(
    n_batch,
    n_module,
    tokens,
    seg_lengths,
    valid,
    cotangent,
    gain_one,
    w_query,
    w_key,
    w_value,
    w_attn_out,
    w_cross,
    b_cross,
    w_mix,
    w_ens1,
    gain_two,
    w_up,
    b_up,
    w_ens2,
):
    module = lax.axis_index("module")
    batch = lax.axis_index("batch")
    own = tokens.shape[0]
    rows = valid.shape[0]
    me = jnp.stack([module, batch]).astype(jnp.int32)

    def by_core(value):
        return swap(value, "module", n_module, 1)

    def by_y(value):
        return swap(value, "module", n_module, 2)

    def by_batch(value, step):
        return swap(value, "batch", n_batch, step)

    from_core = by_core(tokens)
    from_y = by_y(tokens)
    square = ((D, D), BF)
    keys = 2 * own
    row = ((1, D), F32)
    gain_row, valid_row = gain_one.reshape(1, D), valid.reshape(1, rows)
    (spot,) = call(start_kernel, [((8, LANES), jnp.int32)], [], "s", 4, 20)(me)
    (
        wq_pad, wk_pad, wv_pad, wo_pad, wk_t, wv_t, codes, real, counted,
        normed_a, normed_ta, q_aug, k_a, vt_a, part_a, self_scores, crossed, d_joint,
    ) = call(
        functools.partial(first_kernel, own),
        [
            ((D, WIDE), BF), ((D, WIDE), BF), ((D, WIDE), BF), ((WIDE, D), BF), square, square,
            ((rows, LANES), BF), ((1, rows), F32), ((16, rows), BF),
            ((keys, D), BF), ((D, keys), BF), ((own, WIDE), BF), ((keys, WIDE), BF),
            ((HEADS * TALL, keys), BF), ((HEADS * TALL, own), F32), ((16, own), F32), ((own, D), F32),
            ((own, FF + D), F32),
        ],
        [], "vs" + "v" * 12, 16, 5,
    )(
        spot, seg_lengths, from_core, tokens, valid_row, gain_row, w_query, w_key, w_value, w_attn_out,
        w_cross, b_cross.reshape(1, D), cotangent, w_ens2,
    )
    from_far = by_core(jnp.concatenate([from_y, normed_a[:16]], axis=0))
    normed_y, normed_ty, k_y, vt_y, part_y = call(
        functools.partial(middle_kernel, own),
        [((own, D), BF), ((D, own), BF), ((own, WIDE), BF), ((HEADS * TALL, own), BF), ((HEADS * TALL, own), F32)],
        [], "v" * 7, 16, 2,
    )(from_y, gain_row, codes, wk_pad, wv_t, q_aug, part_a)
    (
        payload, d_first, vectors, normed_f, normed_tf, k_f,
        first, active, normed_two, d_modules, att, lse, own_member, counts,
    ) = call(
        functools.partial(forward_kernel, own),
        [
            ((16 * D, D), BF), ((own, D), F32), ((16, D), F32), ((own, D), BF), ((D, own), BF), ((own, WIDE), BF),
            ((own, D), F32), ((own, FF), BF), ((own, D), BF), ((own, 4 * D), BF), ((own, WIDE), F32), ((16, own), F32),
            ((own, 16), BF), ((16, LANES), F32),
        ],
        [
            pltpu.VMEM((HEADS * TALL, own), BF), pltpu.VMEM((HEADS * TALL, own), F32), pltpu.VMEM((rows, own), F32),
            pltpu.VMEM((WIDE, own), F32), pltpu.VMEM((16, own), F32),
        ],
        "v" * 27, 32, 8,
    )(
        spot, from_far, codes, real, counted, tokens, cotangent, gain_row, wk_pad, wo_pad, wv_t,
        w_mix, w_ens1, gain_two.reshape(1, D), w_up, b_up.reshape(1, FF), d_joint,
        normed_a, normed_y, q_aug, k_a, k_y, vt_a, vt_y, part_y, self_scores, crossed,
    )
    big_got = by_core(payload[payload.shape[0] // 2 :])
    v_all, kt_all, q_back, grad_att, pself, dself = call(
        functools.partial(side_kernel, own),
        [
            ((rows, WIDE), BF), ((D, rows), BF), ((own, WIDE), BF), ((own, WIDE), BF), ((16, own), BF), ((16, own), BF),
        ],
        [], "v" * 15, 16, 3,
    )(
        d_modules, att, lse, normed_a, normed_y, normed_f, normed_ta, normed_ty, normed_tf, q_aug, self_scores, real,
        wv_pad, wk_t, wo_pad,
    )

    def head(index, *after, cost=0):
        args = [q_back, k_a, k_y, k_f, v_all, kt_all, grad_att, pself, dself, *after]
        return call(
            functools.partial(head_kernel, own, index),
            [((rows, LANES), BF), ((rows, LANES), BF), ((HEAD_DIM, own), BF)],
            [], "v" * len(args), 16, cost,
        )(*args)

    def summed(counts, parts, *after, cost=0):
        outs = [((count, D), BF) for count in counts]
        args = list(parts) + list(after)
        body = functools.partial(sum_kernel, counts, len(after))
        return call(body, outs, [], "v" * len(args), 8, cost)(*args)

    def joined(parts, *after, cost=0):
        count = sum(part.shape[0] for part in parts)
        body = functools.partial(join_kernel, len(parts), len(after))
        args = list(parts) + list(after)
        return call(body, [((count, D), BF)], [], "v" * len(args), 8, cost)(*args)[0]

    def by_both(value):
        pairs = [(i, i ^ (n_module + 2)) for i in range(n_batch * n_module)]
        return lax.ppermute(value, ("batch", "module"), pairs)

    def around(values):
        return by_batch(values[0], 1), by_y(values[1]), by_both(values[2])

    steps = [1 << place for place in range(1, n_batch.bit_length() - 1)]

    def through(value, got, *after, cost=0):
        for step in steps[2:] + [0]:
            (value,) = summed([value.shape[0]], [value, got], *after, cost=cost)
            got = by_batch(value, step) if step else None
        return value

    size = payload.shape[0] // 8
    half = size // 2
    part = D // 8
    count = 2 * own + 16
    rows_q = 3 * part + 16
    wide = ((D, D), F32)
    mine, *outward = summed([size] * 4, [payload, big_got], pself, cost=0)
    xy_got = around(outward)
    dk0, dv0, dq0 = head(0, mine, cost=2)
    dk1, dv1, dq1 = head(1, dq0, cost=2)
    dk2, dv2, dq2 = head(2, dq1, cost=2)
    dk3, dv3, dq3 = head(3, dq2, cost=2)
    args = [
        dk0, dk1, dk2, dk3, dv0, dv1, dv2, dv3, dq0, dq1, dq2, dq3, normed_a, normed_y, normed_f, counted,
        d_modules, crossed, w_cross, w_mix, own_member, counts, gain_row, w_query, w_key, w_value, vectors,
    ]
    shared, dq_rows = call(
        functools.partial(rows_kernel, own),
        [((2 * count, D), BF), ((own, D), BF)],
        [pltpu.VMEM((rows, D), F32)],
        "v" * len(args), 16, 3,
    )(*args)
    ab, ab_send = summed([half] * 2, [mine, *xy_got], dq_rows, cost=0)
    z1_got = by_batch(ab_send, steps[0])
    shared_got = by_core(shared[count:])
    args = [
        spot, dk0, dk1, dk2, dk3, dv0, dv1, dv2, dv3, dq_rows, normed_ta, normed_ty, normed_tf, ab,
    ]
    (q,) = call(
        functools.partial(weights_kernel, own), [((24 * part, D), BF)], [], "v" * len(args), 16, 3
    )(*args)
    (ab1,) = summed([half], [ab, z1_got], q, cost=0)
    z2_got = by_batch(ab1, steps[1])
    q_out = joined([q[12 * part :]], ab1, cost=0)
    q_core = by_core(q_out)
    dn, dn_send, vec = summed([own, own, 16], [shared, shared_got], q, cost=0)
    dn_got = by_y(dn_send)
    args = [dn, dn_got, tokens, d_first, gain_row, first, active, normed_two, w_ens2, ab1]
    grad_tokens, out_rows, done = call(
        finish_kernel, [((own, D), F32), ((own, D), F32), ((16, D), BF)], [], "v" * len(args), 16, 6
    )(*args)
    blocks = summed([3 * part] * 4, [q, q_core], ab1, cost=0)
    q0, *sends = [joined([block, vec]) for block in blocks]
    q_xy = around(sends)
    ab2 = through(ab1, z2_got, sends[2], done, cost=4)
    back_got = by_batch(ab2, steps[0])
    (q1,) = summed([rows_q], [q0, *q_xy], ab2, cost=3)
    q_z1 = by_batch(q1, steps[0])
    mine2 = joined([ab2, back_got], q1, cost=2)
    xy_back = around([mine2] * 3)
    (q2,) = summed([rows_q], [q1, q_z1], mine2, cost=3)
    q_z2 = by_batch(q2, steps[1])
    q3 = through(q2, q_z2, cost=0)
    q4 = q3[: 3 * part]
    q_back_got = around([q4] * 3)
    big = joined([mine2, *xy_back], q3, cost=0)
    big_got = by_core(big)
    args = [spot, big, big_got]
    attn_out, cross, mix, ens1, up, ens2, done_big = call(
        unpack_kernel,
        [wide, wide, wide, ((4 * D, D), F32), ((D, FF), F32), ((FF + D, D), F32), ((16, D), BF)],
        [], "v" * len(args), 16, 3,
    )(*args)
    q5 = joined([q4, *q_back_got], done_big, cost=0)
    q_last = by_core(q5)
    args = [spot, q5, q_last, q3[3 * part :], done_big]
    gain_one_g, query, key, value, b_cross_g, gain_two_g, b_up_g, done_small = call(
        unpack_small_kernel, [row, wide, wide, wide, row, row, ((1, FF), F32), ((16, D), BF)],
        [], "v" * len(args), 16, 2,
    )(*args)
    return (
        out_rows, grad_tokens, gain_one_g.reshape(D), query, key, value, attn_out, cross, b_cross_g.reshape(D), mix,
        ens1, gain_two_g.reshape(D), up, b_up_g.reshape(FF), ens2,
    )


def solution(mesh):
    rows = P(("batch", "module"), None)
    in_specs = (rows, P("batch", None), P("batch"), rows) + (P(),) * 13
    out_specs = (rows, rows) + (P(),) * 13
    body = functools.partial(shards, mesh.shape["batch"], mesh.shape["module"])
    return jax.shard_map(body, mesh=mesh, in_specs=in_specs, out_specs=out_specs, check_vma=False)
```

```python
import functools

import jax
import jax.numpy as jnp
from jax import lax
from jax.experimental import pallas as pl
from jax.experimental.pallas import tpu as pltpu
from jax.sharding import PartitionSpec as P

D = 256
HEADS = 4
HEAD_DIM = 64
FF = 1024
SEGS = 8
LANES = 128
WIDE = HEADS * LANES
HUGE = -1e30
TALL = HEAD_DIM + 16
BF = jnp.bfloat16
F32 = jnp.float32
MIB = 1024 * 1024


def low(v):
    return v.astype(BF)


def high(v):
    return v.astype(F32)


def dot(a, b):
    return jnp.dot(a, b, preferred_element_type=F32)


def dot_nt(a, b):
    return lax.dot_general(a, b, (((1,), (1,)), ((), ())), preferred_element_type=F32)


def dot_tn(a, b):
    return lax.dot_general(a, b, (((0,), (0,)), ((), ())), preferred_element_type=F32)


def head_sums(selector, product):
    upper = low(product)
    lower = low(product - high(upper))
    return dot_nt(selector, upper) + dot_nt(selector, lower)


def unit_rows(values):
    center = values - jnp.mean(values, axis=1, keepdims=True)
    scale = lax.rsqrt(jnp.mean(center * center, axis=1, keepdims=True) + 1e-05)
    return center * scale, scale


def norm_back(grad, unit, scale, gain):
    scaled = grad * gain
    first_mean = jnp.mean(scaled, axis=1, keepdims=True)
    second_mean = jnp.mean(scaled * unit, axis=1, keepdims=True)
    return scale * (scaled - first_mean - unit * second_mean)


def call(body, outs, scratch, places, limit, microseconds):
    spaces = {"s": pltpu.SMEM, "v": pltpu.VMEM, "h": pltpu.HBM}
    return pl.pallas_call(
        body,
        out_shape=[jax.ShapeDtypeStruct(shape, kind) for shape, kind in outs],
        in_specs=[pl.BlockSpec(memory_space=spaces[place]) for place in places],
        out_specs=[pl.BlockSpec(memory_space=pltpu.VMEM)] * len(outs),
        scratch_shapes=list(scratch),
        compiler_params=pltpu.CompilerParams(vmem_limit_bytes=limit * MIB),
        cost_estimate=pl.CostEstimate(
            flops=microseconds * 10**9, bytes_accessed=0, transcendentals=0
        ),
    )


def widen(weight):
    rows = weight.shape[0]
    gap = jnp.zeros((rows, LANES - HEAD_DIM), weight.dtype)
    pieces = []
    for head in range(HEADS):
        pieces += [weight[:, head * HEAD_DIM : (head + 1) * HEAD_DIM], gap]
    return jnp.concatenate(pieces, axis=1)


def widen_rows(weight):
    gap = jnp.zeros((LANES - HEAD_DIM, weight.shape[1]), weight.dtype)
    pieces = []
    for head in range(HEADS):
        pieces += [weight[head * HEAD_DIM : (head + 1) * HEAD_DIM], gap]
    return jnp.concatenate(pieces, axis=0)


def narrow_rows(wide):
    return jnp.concatenate([wide[h * LANES : h * LANES + HEAD_DIM] for h in range(HEADS)], axis=0)


def segment_rows(seg_ref, first_place, count):
    spread = lax.broadcasted_iota(jnp.int32, (16, count), 0)
    places = lax.broadcasted_iota(jnp.int32, (16, count), 1) + first_place
    begin = jnp.zeros((16, count), jnp.int32)
    end = jnp.zeros((16, count), jnp.int32)
    edge = jnp.int32(0)
    for j in range(SEGS):
        begin = jnp.where(spread == j, edge, begin)
        edge = edge + seg_ref[0, j]
        end = jnp.where(spread == j, edge, end)
    return spread, (places >= begin) & (places < end)


def head_selector():
    rows = lax.broadcasted_iota(jnp.int32, (16, WIDE), 0)
    lanes = lax.broadcasted_iota(jnp.int32, (16, WIDE), 1)
    return low(jnp.where((lanes >> 7) == rows, 1.0, 0.0))


def start_kernel(me_ref, spot):
    rows = lax.broadcasted_iota(jnp.int32, spot.shape, 0)
    spot[...] = jnp.where(rows == 0, me_ref[0], me_ref[1])


def project(rows_in, gain, code, wk_pad, wv_t, at, normed, normed_t, k_aug, vt):
    count = rows_in.shape[0]
    unit, _ = unit_rows(high(rows_in))
    value = low(unit * gain)
    flipped = value.T
    normed[at : at + count, :] = value
    normed_t[:, at : at + count] = flipped
    wide = low(dot(value, wk_pad))
    k_aug[at : at + count, :] = wide + jnp.concatenate([code] * HEADS, axis=1)
    turned = low(dot(wv_t, flipped))
    for h in range(HEADS):
        vt[h * TALL : h * TALL + HEAD_DIM, at : at + count] = turned[h * HEAD_DIM : (h + 1) * HEAD_DIM]
        vt[h * TALL + HEAD_DIM : (h + 1) * TALL, at : at + count] = jnp.ones((16, count), BF)


def raw_attention(q_aug, k_aug, vt, before, part):
    for h in range(HEADS):
        lanes = slice(h * LANES, (h + 1) * LANES)
        tall = slice(h * TALL, (h + 1) * TALL)
        p = low(jnp.exp(dot_nt(k_aug[:, lanes], q_aug[:, lanes])))
        got = dot(vt[tall, :], p)
        part[tall, :] = got if before is None else got + before[tall, :]


def exact_attention(q_aug, parts, self_rows, vt_own, scores, o_t, lse_out):
    step = 256

    def one_head(h, _):
        lanes = pl.ds(pl.multiple_of(h * LANES, LANES), LANES)
        tall = pl.ds(pl.multiple_of(h * TALL, 16), HEAD_DIM)
        q_h = q_aug[:, lanes]
        self_h = self_rows[pl.ds(h, 1), :]
        top = self_h
        first = 0
        for k_part, _ in parts:

            def score(c, top, k_part=k_part, first=first):
                at = pl.multiple_of(c * step, step)
                part = dot_nt(k_part[pl.ds(at, step), lanes], q_h)
                scores[pl.ds(first + at, step), :] = part
                return jnp.maximum(top, jnp.max(part, axis=0, keepdims=True))

            top = lax.fori_loop(0, k_part.shape[0] // step, score, top)
            first += k_part.shape[0]
        p_self = jnp.exp(self_h - top)
        total = p_self
        acc = high(low(p_self)) * high(vt_own[tall, :])
        first = 0
        for _, vt_part in parts:

            def weigh(c, carry, vt_part=vt_part, first=first):
                total, acc = carry
                at = pl.multiple_of(c * step, step)
                p = jnp.exp(scores[pl.ds(first + at, step), :] - top)
                total = total + jnp.sum(p, axis=0, keepdims=True)
                return total, acc + dot(vt_part[tall, pl.ds(at, step)], low(p))

            total, acc = lax.fori_loop(0, vt_part.shape[1] // step, weigh, (total, acc))
            first += vt_part.shape[1]
        o_t[pl.ds(pl.multiple_of(h * LANES, LANES), HEAD_DIM), :] = acc / total
        lse_out[pl.ds(h, 1), :] = top + jnp.log(total)
        return 0

    lax.fori_loop(0, HEADS, one_head, 0)


def placed(rows16, first):
    upper = low(rows16)
    rest = rows16 - high(upper)
    middle = low(rest)
    parts = jnp.concatenate([upper, middle, low(rest - high(middle))], axis=0)
    rows = lax.broadcasted_iota(jnp.int32, (48, WIDE), 0)
    lanes = lax.broadcasted_iota(jnp.int32, (48, WIDE), 1)
    picked = ((lanes >> 7) == (rows & 15)) & ((lanes & (LANES - 1)) == first + (rows >> 4))
    return low(dot_tn(parts, low(jnp.where(picked, 1.0, 0.0))))


def lane_codes(rows_code):
    picked = lax.broadcasted_iota(jnp.int32, (16, LANES), 1) - HEAD_DIM
    picked = (picked == lax.broadcasted_iota(jnp.int32, (16, LANES), 0)) & (picked <= SEGS + 3)
    return low(dot_tn(low(rows_code), low(jnp.where(picked, 1.0, 0.0))))


def first_kernel(
    own_rows,
    spot, seg, core_rows, tokens, valid, gain_one, wq, wk, wv, wo, w_cross, b_cross, cot, w_ens2,
    wq_pad, wk_pad, wv_pad, wo_pad, wk_t, wv_t, codes, real, counted,
    normed, normed_t, q_aug, k_aug, vt, part, self_scores, crossed, d_joint,
):
    me = jnp.max(spot[0:1, :])
    for step in range(4):
        at = pl.multiple_of((me ^ step) * own_rows, own_rows)
        spread, inside = segment_rows(seg, at, own_rows)
        ok = valid[:, pl.ds(at, own_rows)] > 0
        code = jnp.where(inside, HUGE, 0.0)
        code = jnp.where(spread == SEGS, jnp.where(ok, 0.0, HUGE), code)
        code = jnp.where(spread > SEGS, 1.0, code)
        codes[step * own_rows : (step + 1) * own_rows, :] = lane_codes(code)
        real[:, step * own_rows : (step + 1) * own_rows] = jnp.where(ok, 1.0, 0.0)
        counted[:, step * own_rows : (step + 1) * own_rows] = low(jnp.where(inside & ok, 1.0, 0.0))
    wq_pad[...] = low(widen(high(wq[...])))
    wk_pad[...] = low(widen(high(wk[...])))
    wv_pad[...] = low(widen(high(wv[...])))
    wo_pad[...] = low(widen_rows(high(wo[...])))
    wk_t[...] = wk[...].T
    wv_t[...] = wv[...].T
    gain = gain_one[...]
    for step, rows_in in enumerate((tokens, core_rows)):
        at = step * own_rows
        project(
            rows_in[...], gain, codes[at : at + own_rows, :], wk_pad[...], wv_t[...], at,
            normed, normed_t, k_aug, vt,
        )
    spread, inside = segment_rows(seg, pl.multiple_of(me * own_rows, own_rows), own_rows)
    own_code = lane_codes(jnp.where(inside | (spread > SEGS), 0.0, 1.0))
    scaled = low(dot(normed[:own_rows, :], wq_pad[...]) * 0.125)
    q_aug[...] = scaled + jnp.concatenate([own_code] * HEADS, axis=1)
    raw_attention(q_aug, k_aug, vt, None, part)
    lanes_own = lax.broadcasted_iota(jnp.int32, (own_rows, WIDE), 1) & (LANES - 1)
    product = high(q_aug[...]) * high(k_aug[:own_rows, :])
    self_scores[...] = head_sums(head_selector(), jnp.where(lanes_own < HEAD_DIM, product, 0.0))
    crossed[...] = dot(normed[:own_rows, :], w_cross[...]) + b_cross[...]
    d_joint[...] = dot_nt(cot[...], w_ens2[...])


def middle_kernel(
    own_rows,
    y_rows, gain_one, codes, wk_pad, wv_t, q_aug, part_a,
    normed, normed_t, k_aug, vt, part,
):
    project(
        y_rows[...], gain_one[...], codes[2 * own_rows : 3 * own_rows, :], wk_pad[...], wv_t[...], 0,
        normed, normed_t, k_aug, vt,
    )
    raw_attention(q_aug, k_aug, vt, part_a, part)


def forward_kernel(
    own_rows,
    spot, far_rows, codes, real, counted, tokens, cot,
    gain_one, wk_pad, wo_pad, wv_t,
    w_mix, w_ens1, gain_two, w_up, b_up, d_joint,
    normed_a, normed_y, q_aug, k_a, k_y, vt_a, vt_y, part_y, self_scores, crossed,
    payload, d_first_out, vectors, normed_f, normed_tf, k_f,
    first_out, active_out, normed_two_out, d_modules_out, att_out, lse_out, member_out, counts_out,
    vt_f, part_f, scores, o_t, self_rows,
):
    project(
        far_rows[:own_rows, :], gain_one[...], codes[3 * own_rows :, :], wk_pad[...], wv_t[...], 0,
        normed_f, normed_tf, k_f, vt_f,
    )
    normed_own = normed_a[:own_rows, :]
    own_real = real[:, :own_rows] > 0
    o_t[...] = jnp.zeros_like(o_t)
    lse_out[...] = jnp.zeros_like(lse_out)
    raw_attention(q_aug, k_f, vt_f, part_y, part_f)
    vt_own = vt_a[:, :own_rows]
    smallest, largest = jnp.inf, -jnp.inf
    for h in range(HEADS):
        p_self = jnp.where(own_real, 0.0, jnp.exp(self_scores[h : h + 1, :]))
        both = part_f[h * TALL : (h + 1) * TALL, :]
        total = both[HEAD_DIM : HEAD_DIM + 1] + p_self
        acc = both[:HEAD_DIM] + high(low(p_self)) * high(vt_own[h * TALL : h * TALL + HEAD_DIM])
        o_t[h * LANES : h * LANES + HEAD_DIM, :] = acc / total
        lse_out[h : h + 1, :] = jnp.log(total)
        smallest = jnp.minimum(smallest, total)
        largest = jnp.maximum(largest, total)
    fits = (jnp.min(smallest) > 1e-25) & (jnp.max(largest) < 1e30)

    @pl.when(jnp.logical_not(fits))
    def _():
        self_rows[...] = jnp.where(own_real, HUGE, self_scores[...])
        parts = ((k_a, vt_a), (k_y, vt_y), (k_f, vt_f))
        exact_attention(q_aug, parts, self_rows, vt_a.at[:, :own_rows], scores, o_t, lse_out)

    att = o_t[...].T
    att_out[...] = att
    att_low = low(att)

    modules = []
    for g in range(2):
        lanes = slice(g * 256, (g + 1) * 256)
        modules.append(low(dot(att_low[:, lanes], wo_pad[lanes, :])))
    modules.append(low(high(normed_own) * crossed[...]))
    counts = jnp.sum(high(counted[...]), axis=1, keepdims=True)
    counts = jnp.maximum(counts, 1.0)
    counts_out[...] = jnp.broadcast_to(counts, counts_out.shape)
    seg_sums = dot(counted[:, : 2 * own_rows], normed_a[...])
    seg_sums = seg_sums + dot(counted[:, 2 * own_rows : 3 * own_rows], normed_y[...])
    seg_sums = seg_sums + dot(counted[:, 3 * own_rows :], normed_f[...])
    seg_mean = low(seg_sums / counts)
    picked = lax.broadcasted_iota(jnp.int32, (LANES, 16), 0) - HEAD_DIM
    picked = (picked == lax.broadcasted_iota(jnp.int32, (LANES, 16), 1)) & (picked < SEGS)
    own_member = 1.0 - dot(q_aug[:, :LANES], low(jnp.where(picked, 1.0, 0.0)))
    own_lane = lax.broadcasted_iota(jnp.int32, (own_rows, 16), 1)
    own_member = low(jnp.where(own_lane < SEGS, own_member, 0.0))
    member_out[...] = own_member
    mixed = low(dot(own_member, seg_mean))
    modules.append(low(dot(mixed, w_mix[...])))
    first = high(tokens[...])
    for i in range(4):
        first = first + dot(modules[i], w_ens1[i * D : (i + 1) * D, :])
    first_out[...] = first
    unit_two, scale_two = unit_rows(first)
    normed_two = low(unit_two * gain_two[...])
    inner = dot(normed_two, w_up[...]) + b_up[...]
    cdf = 0.5 * (1.0 + lax.erf(inner * 0.7071067811865476))
    active = low(inner * cdf)
    slope = cdf + inner * jnp.exp(-0.5 * inner * inner) * 0.3989422804014327
    active_out[...] = active
    normed_two_out[...] = normed_two

    core, y_bit, x_bit, z_bit = bits_of(spot)
    order = y_bit * 8 + x_bit * 4 + z_bit * 2
    block = payload.shape[0] // 32
    place = [0]

    def put(grad):
        middle = grad.shape[0] // 2
        for i in range(middle // block):
            n = place[0]
            place[0] = n + 1
            place_at = n ^ order
            for side in range(2):
                start = pl.multiple_of(((side ^ core) * 16 + place_at) * block, block)
                first = side * middle + i * block
                payload[pl.ds(start, block), :] = low(grad[first : first + block])

    e2 = cot[...]
    put(dot_tn(active, e2))
    put(dot_tn(normed_two, e2))
    d_inner = low(d_joint[:, :FF] * slope)
    b_up_grad = jnp.sum(high(d_inner), axis=0, keepdims=True)
    grad_up = dot_tn(normed_two, d_inner)
    for i in range(FF // D):
        put(grad_up[:, i * D : (i + 1) * D])
    d_norm2 = d_joint[:, FF:] + dot_nt(d_inner, w_up[...])
    d_first = high(e2) + norm_back(d_norm2, unit_two, scale_two, gain_two[...])
    d_first_out[...] = d_first
    e1 = low(d_first)
    d_modules = []
    for i in range(4):
        put(dot_tn(modules[i], e1))
        d_modules.append(low(dot_nt(e1, w_ens1[i * D : (i + 1) * D, :])))
        d_modules_out[:, i * D : (i + 1) * D] = d_modules[i]
    out_grads = []
    for g in range(2):
        lanes = slice(g * 256, (g + 1) * 256)
        out_grads.append(dot_tn(att_low[:, lanes], d_modules[g]))
    put(narrow_rows(jnp.concatenate(out_grads, axis=0)))
    put(dot_tn(normed_own, low(high(d_modules[2]) * high(normed_own))))
    put(dot_tn(mixed, d_modules[3]))
    vectors[...] = jnp.zeros_like(vectors)
    for i in range(FF // D):
        vectors[i : i + 1, :] = b_up_grad[:, i * D : (i + 1) * D]
    vectors[5:6, :] = jnp.sum(d_norm2 * unit_two, axis=0, keepdims=True)


def side_kernel(
    own_rows,
    d_modules, att, lse,
    normed_a, normed_y, normed_f, normed_ta, normed_ty, normed_tf, q_aug, self_scores, real,
    wv_pad, wk_t, wo_pad,
    v_all, kt_all, q_back, grad_att, pself_out, dself_out,
):
    v_lane = lax.broadcasted_iota(jnp.int32, (1, WIDE), 1) & (LANES - 1)
    v_ones = jnp.where((v_lane >= HEAD_DIM) & (v_lane < HEAD_DIM + 3), 1.0, 0.0)
    at = 0
    for normed, flipped in ((normed_a, normed_ta), (normed_y, normed_ty), (normed_f, normed_tf)):
        count = normed.shape[0]
        v_all[at : at + count, :] = low(dot(normed[...], wv_pad[...]) + v_ones)
        kt_all[:, at : at + count] = low(dot(wk_t[...], flipped[...]))
        at += count
    d_att = []
    for g in range(2):
        lanes = slice(g * 256, (g + 1) * 256)
        d_att.append(low(dot_nt(d_modules[:, g * D : (g + 1) * D], wo_pad[lanes, :])))
    d_att = jnp.concatenate(d_att, axis=1)
    heads16 = head_selector()
    delta = head_sums(heads16, high(d_att) * att[...])
    grad_att[...] = d_att + placed(-delta, HEAD_DIM)
    q_back[...] = q_aug[...] + placed(-lse[...], HEAD_DIM + SEGS + 1)
    p_self = jnp.where(real[:, :own_rows] > 0, 0.0, jnp.exp(self_scores[...] - lse[...]))
    dp_self = head_sums(heads16, high(d_att) * high(v_all[:own_rows, :]))
    pself_out[...] = low(p_self)
    dself_out[...] = low(p_self * (dp_self - delta))


def head_kernel(
    own_rows, h,
    q_back, k_a, k_y, k_f, v_all, kt_all, grad_att, pself, dself,
    *rest,
):
    dk_out, dv_out, dq_out = rest[-3:]
    row16 = lax.broadcasted_iota(jnp.int32, (16, LANES), 0)
    spread = low(jnp.where(row16 == h, 1.0, 0.0))
    lanes = slice(h * LANES, (h + 1) * LANES)
    rows_h = slice(h * HEAD_DIM, (h + 1) * HEAD_DIM)
    q_h = q_back[:, lanes]
    g_h = grad_att[:, lanes]
    lane = lax.broadcasted_iota(jnp.int32, (1, LANES), 1)
    q_half = jnp.where(lane < HEAD_DIM, high(q_h), 0.0)
    g_half = jnp.where(lane < HEAD_DIM, high(g_h), 0.0)
    if h % 2:
        q_half, g_half = pltpu.roll(q_half, HEAD_DIM, 1), pltpu.roll(g_half, HEAD_DIM, 1)
    q_low, g_low = low(q_half), low(g_half)
    acc = high(dself[h : h + 1, :]) * high(kt_all[rows_h, :own_rows])
    first = 0
    for k_part in (k_a, k_y, k_f):
        count = k_part.shape[0]
        at = slice(first, first + count)
        p = jnp.exp(dot_nt(k_part[:, lanes], q_h))
        ds = low(p * dot_nt(v_all[at, lanes], g_h))
        dv = dot(low(p), g_low)
        dk = dot(ds, q_low)
        if first == 0:
            dk_self = dot_tn(dself[...], spread) * q_half
            dv_self = dot_tn(pself[...], spread) * g_half
            dk_out[:own_rows, :] = low(dk[:own_rows] + dk_self)
            dv_out[:own_rows, :] = low(dv[:own_rows] + dv_self)
            dk_out[own_rows:count, :] = low(dk[own_rows:])
            dv_out[own_rows:count, :] = low(dv[own_rows:])
        else:
            dk_out[at, :] = low(dk)
            dv_out[at, :] = low(dv)
        acc = acc + dot(kt_all[rows_h, at], ds)
        first += count
    dq_out[...] = low(acc * 0.125)


def rows_kernel(
    own_rows,
    dk0, dk1, dk2, dk3, dv0, dv1, dv2, dv3, dq0, dq1, dq2, dq3, normed_a, normed_y, normed_f, counted, d_modules, crossed,
    w_cross, w_mix, own_member, counts, gain_one, wq, wk, wv, vectors,
    *rest,
):
    out, dq_out, dn = rest[-3:]
    d_two = high(d_modules[:, 2 * D : 3 * D])
    d_cross = low(d_two * high(normed_a[:own_rows, :]))
    dn_own = d_two * crossed[...] + dot_nt(d_cross, w_cross[...])
    b_cross_grad = jnp.sum(high(d_cross), axis=0, keepdims=True)
    d_mixed = dot_nt(d_modules[:, 3 * D :], w_mix[...])
    mixed_up = low(d_mixed)
    mixed_down = low(d_mixed - high(mixed_up))
    seg_grad = dot_tn(own_member[...], mixed_up) + dot_tn(own_member[...], mixed_down)
    seg_grad = seg_grad / counts[:, :1]
    half_keys = 2 * own_rows
    dq = jnp.concatenate([high(part[...]) for part in (dq0, dq1, dq2, dq3)], axis=0)
    dq_rows = low(dq.T)
    dq_out[...] = dq_rows
    dk = jnp.concatenate([dk0[...] + dk1[...], dk2[...] + dk3[...]], axis=1)
    dv = jnp.concatenate([dv0[...] + dv1[...], dv2[...] + dv3[...]], axis=1)
    up = low(seg_grad)
    both = jnp.concatenate([up, low(seg_grad - high(up))], axis=0)
    for c in range(2):
        at = slice(c * half_keys, (c + 1) * half_keys)
        mixing = dot_tn(jnp.concatenate([counted[:, at], counted[:, at]], axis=0), both)
        dn[at, :] = mixing + (dot_nt(dk[at, :], wk[...]) + dot_nt(dv[at, :], wv[...]))
    dn[:own_rows, :] = dn[:own_rows, :] + (dot_nt(dq_rows, wq[...]) + dn_own)
    gain_grad = jnp.sum(dn[:half_keys, :] * high(normed_a[...]), axis=0, keepdims=True)
    for i, normed in enumerate((normed_y, normed_f)):
        here = dn[(2 + i) * own_rows : (3 + i) * own_rows, :]
        gain_grad = gain_grad + jnp.sum(here * high(normed[...]), axis=0, keepdims=True)
    gain_grad = gain_grad / gain_one[...]
    count = out.shape[0] // 2
    for step in range(4):
        at = (step % 2) * count + (step // 2) * own_rows
        out[at : at + own_rows, :] = low(dn[step * own_rows : (step + 1) * own_rows, :])
    tail = lax.broadcasted_iota(jnp.int32, (16, D), 0)
    row = jnp.where(tail == 6, gain_grad, jnp.where(tail == 4, b_cross_grad, vectors[...]))
    out[count - 16 : count, :] = low(row)
    out[2 * count - 16 :, :] = low(row)


def weights_kernel(
    own_rows,
    spot,
    dk0, dk1, dk2, dk3, dv0, dv1, dv2, dv3, dq_rows, normed_ta, normed_ty, normed_tf,
    *rest,
):
    out = rest[-1]
    flips = ((normed_ta, 0), (normed_ty, 2), (normed_tf, 3))

    def key_grad(parts):
        whole = [parts[i][...] + parts[i + 1][...] for i in (0, 2)]
        whole = jnp.concatenate(whole, axis=1)
        return sum(
            dot(flip[...], whole[at * own_rows : at * own_rows + flip.shape[1]]) for flip, at in flips
        )

    core, y_bit, x_bit, _ = bits_of(spot)
    order = core * 4 + y_bit * 2 + x_bit
    part = D // 8
    for i, grad in enumerate(
        (
            dot(normed_ta[:, :own_rows], dq_rows[...]),
            key_grad((dk0, dk1, dk2, dk3)),
            key_grad((dv0, dv1, dv2, dv3)),
        )
    ):
        for n in range(8):
            at = ((n ^ order) * 3 + i) * part
            out[pl.ds(pl.multiple_of(at, part), part), :] = low(grad[n * part : (n + 1) * part])


def finish_kernel(
    mine, other, tokens, d_first, gain_one, first, active, normed_two, w_ens2, *rest
):
    grad_tokens, out_rows, done = rest[-3:]
    out_rows[...] = first[...] + (dot(active[...], w_ens2[:FF, :]) + dot(normed_two[...], w_ens2[FF:, :]))
    unit, scale = unit_rows(high(tokens[...]))
    total = high(mine[...]) + high(other[...])
    grad_tokens[...] = d_first[...] + norm_back(total, unit, scale, gain_one[...])
    done[...] = mine[:16, :]


def unpack_kernel(spot, mine, other, *rest):
    attn_out, cross, mix, ens1, up, ens2, done = rest[-7:]
    core, y_bit, x_bit, z_bit = bits_of(spot)
    order = y_bit * 8 + x_bit * 4 + z_bit * 2
    block = mine.shape[0] // 16
    every = slice(None)
    jobs = [(ens2, 0, FF, every), (ens2, FF, D, every)]
    jobs += [(up, 0, D, slice(i * D, (i + 1) * D)) for i in range(FF // D)]
    jobs += [(ens1, i * D, D, every) for i in range(4)]
    jobs += [(attn_out, 0, D, every), (cross, 0, D, every), (mix, 0, D, every)]
    n = 0
    for to, first, count, columns in jobs:
        for i in range(count // 2 // block):
            place_at = n ^ order
            n += 1
            for side, source in ((core, mine), (1 - core, other)):
                at = pl.multiple_of(first + side * (count // 2) + i * block, block)
                value = source[pl.ds(pl.multiple_of(place_at * block, block), block), :]
                to[pl.ds(at, block), columns] = high(value)
    done[...] = mine[:16, :]


def unpack_small_kernel(spot, mine, other, vec, *rest):
    gain_one, query, key, value, b_cross, gain_two, b_up, done = rest[-8:]
    core, y_bit, x_bit, _ = bits_of(spot)
    order = y_bit * 2 + x_bit
    part = D // 8
    for side, source in ((core, mine), (1 - core, other)):
        for n in range(4):
            for i, to in enumerate((query, key, value)):
                at = pl.multiple_of((n ^ order) * 3 * part + i * part, part)
                here = pl.ds(pl.multiple_of((side * 4 + n) * part, part), part)
                to[here, :] = high(source[pl.ds(at, part), :])
    wide = high(vec[...])
    for i in range(FF // D):
        b_up[:, i * D : (i + 1) * D] = wide[i : i + 1]
    b_cross[...] = wide[4:5]
    gain_two[...] = wide[5:6]
    gain_one[...] = wide[6:7]
    done[...] = mine[:16, :]


def swap(value, axis, count, step):
    return lax.ppermute(value, axis, [(i, i ^ step) for i in range(count)])


def bits_of(spot):
    module, batch = jnp.max(spot[0:1, :]), jnp.max(spot[1:2, :])
    return module & 1, (module >> 1) & 1, batch & 1, (batch >> 1) & 1


def sum_kernel(counts, afters, *refs):
    inputs, outs = refs[: len(refs) - afters - len(counts)], refs[len(refs) - len(counts) :]
    at = 0
    for count, out in zip(counts, outs):
        total = high(inputs[0][at : at + count, :])
        for other in inputs[1:]:
            total = total + high(other[at : at + count, :])
        out[...] = low(total)
        at += count


def join_kernel(jobs, afters, *refs):
    out = refs[-1]
    at = 0
    for ref in refs[:jobs]:
        count = ref.shape[0]
        out[at : at + count, :] = ref[...]
        at += count


def added(one, two):
    return low(high(one) + high(two))


def shards(
    n_batch,
    n_module,
    tokens,
    seg_lengths,
    valid,
    cotangent,
    gain_one,
    w_query,
    w_key,
    w_value,
    w_attn_out,
    w_cross,
    b_cross,
    w_mix,
    w_ens1,
    gain_two,
    w_up,
    b_up,
    w_ens2,
):
    module = lax.axis_index("module")
    batch = lax.axis_index("batch")
    own = tokens.shape[0]
    rows = valid.shape[0]
    me = jnp.stack([module, batch]).astype(jnp.int32)

    def by_core(value):
        return swap(value, "module", n_module, 1)

    def by_y(value):
        return swap(value, "module", n_module, 2)

    def by_batch(value, step):
        return swap(value, "batch", n_batch, step)

    from_core = by_core(tokens)
    from_y = by_y(tokens)
    square = ((D, D), BF)
    keys = 2 * own
    row = ((1, D), F32)
    gain_row, valid_row = gain_one.reshape(1, D), valid.reshape(1, rows)
    (spot,) = call(start_kernel, [((8, LANES), jnp.int32)], [], "s", 4, 20)(me)
    (
        wq_pad, wk_pad, wv_pad, wo_pad, wk_t, wv_t, codes, real, counted,
        normed_a, normed_ta, q_aug, k_a, vt_a, part_a, self_scores, crossed, d_joint,
    ) = call(
        functools.partial(first_kernel, own),
        [
            ((D, WIDE), BF), ((D, WIDE), BF), ((D, WIDE), BF), ((WIDE, D), BF), square, square,
            ((rows, LANES), BF), ((1, rows), F32), ((16, rows), BF),
            ((keys, D), BF), ((D, keys), BF), ((own, WIDE), BF), ((keys, WIDE), BF),
            ((HEADS * TALL, keys), BF), ((HEADS * TALL, own), F32), ((16, own), F32), ((own, D), F32),
            ((own, FF + D), F32),
        ],
        [], "vs" + "v" * 12, 16, 5,
    )(
        spot, seg_lengths, from_core, tokens, valid_row, gain_row, w_query, w_key, w_value, w_attn_out,
        w_cross, b_cross.reshape(1, D), cotangent, w_ens2,
    )
    from_far = by_core(jnp.concatenate([from_y, normed_a[:16]], axis=0))
    normed_y, normed_ty, k_y, vt_y, part_y = call(
        functools.partial(middle_kernel, own),
        [((own, D), BF), ((D, own), BF), ((own, WIDE), BF), ((HEADS * TALL, own), BF), ((HEADS * TALL, own), F32)],
        [], "v" * 7, 16, 2,
    )(from_y, gain_row, codes, wk_pad, wv_t, q_aug, part_a)
    (
        payload, d_first, vectors, normed_f, normed_tf, k_f,
        first, active, normed_two, d_modules, att, lse, own_member, counts,
    ) = call(
        functools.partial(forward_kernel, own),
        [
            ((16 * D, D), BF), ((own, D), F32), ((16, D), F32), ((own, D), BF), ((D, own), BF), ((own, WIDE), BF),
            ((own, D), F32), ((own, FF), BF), ((own, D), BF), ((own, 4 * D), BF), ((own, WIDE), F32), ((16, own), F32),
            ((own, 16), BF), ((16, LANES), F32),
        ],
        [
            pltpu.VMEM((HEADS * TALL, own), BF), pltpu.VMEM((HEADS * TALL, own), F32), pltpu.VMEM((rows, own), F32),
            pltpu.VMEM((WIDE, own), F32), pltpu.VMEM((16, own), F32),
        ],
        "v" * 27, 32, 8,
    )(
        spot, from_far, codes, real, counted, tokens, cotangent, gain_row, wk_pad, wo_pad, wv_t,
        w_mix, w_ens1, gain_two.reshape(1, D), w_up, b_up.reshape(1, FF), d_joint,
        normed_a, normed_y, q_aug, k_a, k_y, vt_a, vt_y, part_y, self_scores, crossed,
    )
    big_got = by_core(payload[payload.shape[0] // 2 :])
    v_all, kt_all, q_back, grad_att, pself, dself = call(
        functools.partial(side_kernel, own),
        [
            ((rows, WIDE), BF), ((D, rows), BF), ((own, WIDE), BF), ((own, WIDE), BF), ((16, own), BF), ((16, own), BF),
        ],
        [], "v" * 15, 16, 3,
    )(
        d_modules, att, lse, normed_a, normed_y, normed_f, normed_ta, normed_ty, normed_tf, q_aug, self_scores, real,
        wv_pad, wk_t, wo_pad,
    )

    def head(index, *after, cost=0):
        args = [q_back, k_a, k_y, k_f, v_all, kt_all, grad_att, pself, dself, *after]
        return call(
            functools.partial(head_kernel, own, index),
            [((rows, LANES), BF), ((rows, LANES), BF), ((HEAD_DIM, own), BF)],
            [], "v" * len(args), 16, cost,
        )(*args)

    def summed(counts, parts, *after, cost=0):
        outs = [((count, D), BF) for count in counts]
        args = list(parts) + list(after)
        body = functools.partial(sum_kernel, counts, len(after))
        return call(body, outs, [], "v" * len(args), 8, cost)(*args)

    def joined(parts, *after, cost=0):
        count = sum(part.shape[0] for part in parts)
        body = functools.partial(join_kernel, len(parts), len(after))
        args = list(parts) + list(after)
        return call(body, [((count, D), BF)], [], "v" * len(args), 8, cost)(*args)[0]

    def by_both(value):
        pairs = [(i, i ^ (n_module + 2)) for i in range(n_batch * n_module)]
        return lax.ppermute(value, ("batch", "module"), pairs)

    def around(values):
        return by_batch(values[0], 1), by_y(values[1]), by_both(values[2])

    steps = [1 << place for place in range(1, n_batch.bit_length() - 1)]

    def through(value, got, *after, cost=0):
        for step in steps[2:] + [0]:
            (value,) = summed([value.shape[0]], [value, got], *after, cost=cost)
            got = by_batch(value, step) if step else None
        return value

    size = payload.shape[0] // 8
    half = size // 2
    part = D // 8
    count = 2 * own + 16
    rows_q = 3 * part + 16
    wide = ((D, D), F32)
    mine, *outward = summed([size] * 4, [payload, big_got], pself, cost=0)
    xy_got = around(outward)
    dk0, dv0, dq0 = head(0, mine, cost=2)
    dk1, dv1, dq1 = head(1, dq0, cost=2)
    dk2, dv2, dq2 = head(2, dq1, cost=2)
    dk3, dv3, dq3 = head(3, dq2, cost=2)
    args = [
        dk0, dk1, dk2, dk3, dv0, dv1, dv2, dv3, dq0, dq1, dq2, dq3, normed_a, normed_y, normed_f, counted,
        d_modules, crossed, w_cross, w_mix, own_member, counts, gain_row, w_query, w_key, w_value, vectors,
    ]
    shared, dq_rows = call(
        functools.partial(rows_kernel, own),
        [((2 * count, D), BF), ((own, D), BF)],
        [pltpu.VMEM((rows, D), F32)],
        "v" * len(args), 16, 3,
    )(*args)
    ab, ab_send = summed([half] * 2, [mine, *xy_got], dq_rows, cost=0)
    z1_got = by_batch(ab_send, steps[0])
    shared_got = by_core(shared[count:])
    args = [
        spot, dk0, dk1, dk2, dk3, dv0, dv1, dv2, dv3, dq_rows, normed_ta, normed_ty, normed_tf, ab,
    ]
    (q,) = call(
        functools.partial(weights_kernel, own), [((24 * part, D), BF)], [], "v" * len(args), 16, 3
    )(*args)
    (ab1,) = summed([half], [ab, z1_got], q, cost=0)
    z2_got = by_batch(ab1, steps[1])
    q_out = joined([q[12 * part :]], ab1, cost=0)
    q_core = by_core(q_out)
    dn, dn_send, vec = summed([own, own, 16], [shared, shared_got], q, cost=0)
    dn_got = by_y(dn_send)
    args = [dn, dn_got, tokens, d_first, gain_row, first, active, normed_two, w_ens2, ab1]
    grad_tokens, out_rows, done = call(
        finish_kernel, [((own, D), F32), ((own, D), F32), ((16, D), BF)], [], "v" * len(args), 16, 6
    )(*args)
    blocks = summed([3 * part] * 4, [q, q_core], ab1, cost=0)
    q0, *sends = [joined([block, vec]) for block in blocks]
    q_xy = around(sends)
    ab2 = through(ab1, z2_got, sends[2], done, cost=4)
    back_got = by_batch(ab2, steps[0])
    (q1,) = summed([rows_q], [q0, *q_xy], ab2, cost=3)
    q_z1 = by_batch(q1, steps[0])
    mine2 = joined([ab2, back_got], q1, cost=2)
    xy_back = around([mine2] * 3)
    (q2,) = summed([rows_q], [q1, q_z1], mine2, cost=3)
    q_z2 = by_batch(q2, steps[1])
    q3 = through(q2, q_z2, cost=0)
    q4 = q3[: 3 * part]
    q_back_got = around([q4] * 3)
    big = joined([mine2, *xy_back], q3, cost=0)
    big_got = by_core(big)
    args = [spot, big, big_got]
    attn_out, cross, mix, ens1, up, ens2, done_big = call(
        unpack_kernel,
        [wide, wide, wide, ((4 * D, D), F32), ((D, FF), F32), ((FF + D, D), F32), ((16, D), BF)],
        [], "v" * len(args), 16, 3,
    )(*args)
    q5 = joined([q4, *q_back_got], done_big, cost=0)
    q_last = by_core(q5)
    args = [spot, q5, q_last, q3[3 * part :], done_big]
    gain_one_g, query, key, value, b_cross_g, gain_two_g, b_up_g, done_small = call(
        unpack_small_kernel, [row, wide, wide, wide, row, row, ((1, FF), F32), ((16, D), BF)],
        [], "v" * len(args), 16, 2,
    )(*args)
    return (
        out_rows, grad_tokens, gain_one_g.reshape(D), query, key, value, attn_out, cross, b_cross_g.reshape(D), mix,
        ens1, gain_two_g.reshape(D), up, b_up_g.reshape(FF), ens2,
    )


def solution(mesh):
    rows = P(("batch", "module"), None)
    in_specs = (rows, P("batch", None), P("batch"), rows) + (P(),) * 13
    out_specs = (rows, rows) + (P(),) * 13
    body = functools.partial(shards, mesh.shape["batch"], mesh.shape["module"])
    return jax.shard_map(body, mesh=mesh, in_specs=in_specs, out_specs=out_specs, check_vma=False)
```
